32 devices in a mesh: dp: 16 (over z, x, core), tp: 2 (over y).
Axes of the slice: x: 2, y: 2, z: 4, core: 2. Of those that a mesh axis runs over, the one named last changes fastest.
Arguments:
- tokens: bfloat16 [6144, 768], P('dp'), may hold values from -6 to 6
- lengths: int32 [16, 6], P('dp'), may hold values from 1 to 256, 384 in all within a row
- pad_mask: int32 [6144], P('dp'), may hold values 0 or 1
- w_qkv: bfloat16 [3, 768, 768], P(None, None, 'tp'), may hold values from -0.21875 to 0.21875
- b_qv: bfloat16 [2, 768], P(None, 'tp'), may hold values from -3 to 3
- w_out: bfloat16 [768, 768], P('tp'), may hold values from -0.875 to 0.875
- b_out: bfloat16 [768], replicated, may hold values from -2 to 2
- ln1_gain: bfloat16 [768], replicated, may hold values from 0.5 to 1.5
- ln1_bias: bfloat16 [768], replicated, may hold values from -2 to 2
- w_up: bfloat16 [768, 3072], P(None, 'tp'), may hold values from -0.21875 to 0.21875
- b_up: bfloat16 [3072], P('tp'), may hold values from -3 to 3
- w_down: bfloat16 [3072, 768], P('tp'), may hold values from -0.109375 to 0.109375
- b_down: bfloat16 [768], replicated, may hold values from -2 to 2
- ln2_gain: bfloat16 [768], replicated, may hold values from 0.5 to 1.5
- ln2_bias: bfloat16 [768], replicated, may hold values from -2 to 2
- cotangent: bfloat16 [6144, 768], P('dp'), may hold values from -6 to 6
Outputs:
- layer_out: bfloat16 [6144, 768], P('dp')
- d_tokens: float32 [6144, 768], P('dp')
- d_w_qkv: float32 [3, 768, 768], P(None, 'dp', 'tp')
- d_b_qv: float32 [2, 768], P(None, 'tp')
- d_w_out: float32 [768, 768], P('tp', 'dp')
- d_b_out: float32 [768], replicated
- d_ln1_gain: float32 [768], replicated
- d_ln1_bias: float32 [768], replicated
- d_w_up: float32 [768, 3072], P('dp', 'tp')
- d_b_up: float32 [3072], P('tp')
- d_w_down: float32 [3072, 768], P('tp', 'dp')
- d_b_down: float32 [768], replicated
- d_ln2_gain: float32 [768], replicated
- d_ln2_bias: float32 [768], replicated
The draws below stay inside these ranges and needn't reach their ends.
Inputs may be any that keep to these rules, and one draw needn't show every extreme that they name: Each row holds the lengths of the 6 sequences packed in order on one index of dp; a row sums to 384, and its largest length is exactly 256.
All inputs are finite; a program needn't handle non-finite values. No bound on the sum of `pad_mask` on one device may be relied on, other than what follows from the above.
Results may differ from the reference program's by a relative error of at most 0.013.
The reference program's roundings to bfloat16 on the way count: a program that leaves them out, or rounds other values in their place, can miss the bound.
Values sent between devices are 32-bit elements; how exact they have to be, the bound alone decides.
No kernel may reach another device: no remote copies, remote signals or barrier semaphores. Data moves between devices by JAX's collectives and lax.ppermute only.
A program may use at most 128 MiB of HBM per device.

```python
import math
import jax
import jax.numpy as jnp
import numpy as np
from jax import lax

D = 768
HEADS = 12
HEAD = 64
FF = 3072
TOK_DEV = 384
SEQ_DEV = 6
MAXLEN = 256
SLABS = 16
TOKENS = 6144


def touch_ends(drawn, own_key, low, top_value):
    longest = drawn.shape.index(max(drawn.shape))
    spots = []
    for shift in (0, 1):
        where = [jax.random.randint(jax.random.fold_in(own_key, axis), (), 0, length) for axis, length in enumerate(drawn.shape)]
        where[longest] = (where[longest] + shift) % drawn.shape[longest]
        spots.append(tuple(where))
    return drawn.at[spots[0]].set(low).at[spots[1]].set(top_value)


def level_of(own_key, dims, split, least, top_value):
    loudness, own = 1.0, jax.random.fold_in(own_key, 6)
    for dim, shards_of in split:
        heights = jnp.exp(jax.random.uniform(jax.random.fold_in(own, dim), (shards_of,), jnp.float32, least / len(split), top_value / len(split)))
        loudness = loudness * jnp.repeat(heights, dims[dim] // shards_of).reshape([-1 if axis == dim else 1 for axis in range(len(dims))])
    return loudness


def split_up(amount, total, reach, lean):
    weights = [(1 << 20) // math.isqrt(grade ** lean) + 1 for grade in range(2, amount + 1)]
    spare, counts = total - reach - (amount - 1), [1] * (amount - 1)
    while spare > 0:
        candidates = [i for i in range(amount - 1) if counts[i] < reach]
        whole, left = sum([weights[i] for i in candidates]), spare
        for i in candidates:
            more = min(reach - counts[i], max(1, left * weights[i] // whole), spare)
            counts[i] = counts[i] + more
            spare = spare - more
    return np.array([reach] + counts)


def uneven(stream_key, amount, total, reach, slope):
    if amount == 2:
        one = jax.random.randint(stream_key, (), max(1, total - reach), min(reach, total - 1) + 1)
        return jnp.stack([one, total - one])
    tallies = jnp.asarray(split_up(amount, total, reach, slope), jnp.int32)
    pairs = (amount - 1) // 2
    donor, taker = tallies[1:1 + 2 * pairs:2], tallies[2:2 + 2 * pairs:2]
    margin = jnp.minimum(donor - 1, reach - taker)
    shifted = jax.random.randint(jax.random.fold_in(stream_key, 1), (pairs,), 0, 1 << 20) % (margin + 1)
    tallies = tallies.at[1:1 + 2 * pairs:2].set(donor - shifted).at[2:2 + 2 * pairs:2].set(taker + shifted)
    return tallies[jax.random.permutation(jax.random.fold_in(stream_key, 2), amount)]


def noise(key, dims, deviation, reach, cuts=(), kind=jnp.bfloat16):
    loudness = level_of(key, dims, cuts, -0.22, 0.18) if cuts else 1.0
    values = jax.random.normal(key, dims, jnp.float32) * deviation * loudness
    return jnp.minimum(jnp.maximum(values, -reach), reach).astype(kind)


def setup_inputs(seed: int = 0) -> dict:
    arg_keys = jax.random.split(jax.random.key(seed), 17)
    return {
        "tokens": noise(arg_keys[0], (TOKENS, D), 1.0, 6.0, ((0, 16),)),
        "lengths": jax.vmap(lambda own: uneven(own, SEQ_DEV, TOK_DEV, MAXLEN, 2))(jax.random.split(arg_keys[1], SLABS)).reshape((SLABS, SEQ_DEV)).astype(jnp.int32),
        "pad_mask": touch_ends((jax.random.randint(arg_keys[2], (TOKENS,), 0, 8) < 7).astype(jnp.int32), jax.random.fold_in(arg_keys[2], 1), 0, 1),
        "w_qkv": noise(arg_keys[3], (3, D, D), D ** -0.5, 0.21875, ((2, 2),)),
        "b_qv": noise(arg_keys[4], (2, D), 0.5, 3.0, ((1, 2),)),
        "w_out": noise(arg_keys[5], (D, D), (D // 16) ** -0.5, 0.875, ((0, 2),)),
        "b_out": noise(arg_keys[6], (D,), 0.3, 2.0),
        "ln1_gain": jnp.clip(1.0 + 0.1 * jax.random.normal(arg_keys[7], (D,), jnp.float32), 0.5, 1.5).astype(jnp.bfloat16),
        "ln1_bias": noise(arg_keys[8], (D,), 0.3, 2.0),
        "w_up": noise(arg_keys[9], (D, FF), D ** -0.5, 0.21875, ((1, 2),)),
        "b_up": noise(arg_keys[10], (FF,), 0.5, 3.0, ((0, 2),)),
        "w_down": noise(arg_keys[11], (FF, D), FF ** -0.5, 0.109375, ((0, 2),)),
        "b_down": noise(arg_keys[12], (D,), 0.3, 2.0),
        "ln2_gain": jnp.clip(1.0 + 0.1 * jax.random.normal(arg_keys[13], (D,), jnp.float32), 0.5, 1.5).astype(jnp.bfloat16),
        "ln2_bias": noise(arg_keys[14], (D,), 0.3, 2.0),
        "cotangent": noise(arg_keys[15], (TOKENS, D), 1.0, 6.0, ((0, 16),)),
    }


@jax.custom_vjp
def low(v):
    return lax.optimization_barrier(v.astype(jnp.bfloat16)).astype(jnp.float32)

@jax.custom_vjp
def low_back(v):
    return v

def low_keep(v):
    return (low(v), None)

def low_pass(kept, grad):
    return (grad,)

def back_keep(v):
    return (v, None)

def back_low(kept, grad):
    return (low(grad),)
low.defvjp(low_keep, low_pass)
low_back.defvjp(back_keep, back_low)
NEG_FILL = -1e+30
EPS_NORM = 1e-12

def layer_norm(value, gain, bias):
    centered = value - lax.optimization_barrier(jnp.mean(value, -1, keepdims=True))
    variance = lax.optimization_barrier(jnp.mean(centered * centered, -1, keepdims=True))
    return centered * lax.rsqrt(variance + EPS_NORM) * gain + bias

def forward(params, inputs, allowed):
    w_qkv, b_qv, w_out, b_out, ln1_gain, ln1_bias, w_up, b_up, w_down, b_down, ln2_gain, ln2_bias = params
    highest = lax.Precision.HIGHEST
    count = inputs.shape[0]
    scale = float(HEAD) ** (-0.5)
    query = low_back(low((jnp.dot(inputs, w_qkv[0], precision=highest) + b_qv[0]) * scale))
    keys = low_back(low(jnp.dot(inputs, w_qkv[1], precision=highest)))
    values = low_back(low(jnp.dot(inputs, w_qkv[2], precision=highest) + b_qv[1]))
    query = query.reshape(count, HEADS, HEAD)
    keys = keys.reshape(count, HEADS, HEAD)
    values = values.reshape(count, HEADS, HEAD)
    scores = low_back(jnp.einsum('qhd,khd->hqk', query, keys, precision=highest))
    scores = jnp.where(allowed[None], scores, NEG_FILL)
    top = lax.optimization_barrier(jnp.max(scores, -1, keepdims=True))
    expo = jnp.exp(scores - top)
    probs = low(expo / lax.optimization_barrier(jnp.sum(expo, -1, keepdims=True)))
    context = jnp.einsum('hqk,khd->qhd', probs, values, precision=highest).reshape(count, D)
    context = low_back(low(context))
    attn = low_back(jnp.dot(context, w_out, precision=highest))
    hidden = layer_norm(inputs + attn + b_out, ln1_gain, ln1_bias)
    pre = low_back(jnp.dot(low(hidden), w_up, precision=highest) + b_up)
    act = low(jax.nn.gelu(pre, approximate=False))
    ffn = low_back(jnp.dot(act, w_down, precision=highest))
    return layer_norm(hidden + ffn + b_down, ln2_gain, ln2_bias)

def reference(tokens, lengths, pad_mask, w_qkv, b_qv, w_out, b_out, ln1_gain, ln1_bias, w_up, b_up, w_down, b_down, ln2_gain, ln2_bias, cotangent):
    params = tuple((a.astype(jnp.float32) for a in (w_qkv, b_qv, w_out, b_out, ln1_gain, ln1_bias, w_up, b_up, w_down, b_down, ln2_gain, ln2_bias)))
    slab_inputs = tokens.astype(jnp.float32).reshape(SLABS, TOK_DEV, D)
    slab_grads = cotangent.astype(jnp.float32).reshape(SLABS, TOK_DEV, D)
    slab_pads = pad_mask.reshape(SLABS, TOK_DEV)
    places = jnp.arange(TOK_DEV, dtype=jnp.int32)

    def slab(total, pieces):
        inputs, lens, pads, upstream = pieces
        ends = jnp.cumsum(lens).astype(jnp.int32)
        segment = lax.optimization_barrier(jnp.sum((ends[None, :] <= places[:, None]).astype(jnp.int32), 1)).astype(jnp.int32)
        allowed = (segment[:, None] == segment[None, :]) & ((pads[None, :] == 1) | (places[:, None] == places[None, :]))
        output, pull = jax.vjp(lambda p, v: forward(p, v, allowed), params, inputs)
        grads, grad_inputs = pull(upstream)
        return (jax.tree.map(jnp.add, total, grads), (output, grad_inputs))
    zeros = jax.tree.map(jnp.zeros_like, params)
    total, (outputs, grad_inputs) = lax.scan(slab, zeros, (slab_inputs, lengths, slab_pads, slab_grads))
    layer_out = outputs.reshape(TOKENS, D).astype(jnp.bfloat16)
    d_tokens = grad_inputs.reshape(TOKENS, D)
    return (layer_out, d_tokens, total[0], total[1], total[2], total[3], total[4], total[5], total[6], total[7], total[8], total[9], total[10], total[11])
```

```python
import functools

import jax
import jax.numpy as jnp
from jax import lax
from jax.experimental import pallas as pl
from jax.experimental.pallas import tpu as pltpu
from jax.sharding import PartitionSpec as P

HEAD = 64
NEG_FILL = -1e30
EPS_NORM = 1e-12
LANES = 128
F32 = jnp.float32
LOW = jnp.bfloat16
MIB = 1 << 20


def dot(a, b):
    return lax.dot_general(a, b, (((1,), (0,)), ((), ())), preferred_element_type=F32)


def dot_nt(a, b):
    return lax.dot_general(a, b, (((1,), (1,)), ((), ())), preferred_element_type=F32)


def whole(shape):
    return pl.BlockSpec(shape, lambda *_: (0,) * len(shape))


def params(limit=48):
    return pltpu.CompilerParams(vmem_limit_bytes=limit * MIB)


def cost(flops, moved, special=0):
    return pl.CostEstimate(flops=int(flops), bytes_accessed=int(moved), transcendentals=int(special))


def key_mask(lengths_ref, pad_ref, rows):
    seqs = lengths_ref.shape[1]
    key_at = lax.broadcasted_iota(jnp.int32, (rows, LANES), 0)
    query_at = lax.broadcasted_iota(jnp.int32, (8, rows), 1)
    key_seg = jnp.zeros((rows, LANES), jnp.int32)
    query_seg = jnp.zeros((8, rows), jnp.int32)
    end = jnp.int32(0)
    for i in range(seqs):
        end = end + lengths_ref[0, i]
        key_seg = key_seg + (key_at >= end).astype(jnp.int32)
        query_seg = query_seg + (query_at >= end).astype(jnp.int32)
    pad = jnp.broadcast_to(pad_ref[...].astype(F32), (LANES, rows)).T
    pieces = []
    for j in range(rows // LANES):
        span = slice(j * LANES, (j + 1) * LANES)
        same = key_seg == query_seg[0:1, span]
        usable = (pad == 1.0) | (key_at == query_at[0:1, span])
        pieces.append(jnp.where(same & usable, 0.0, NEG_FILL))
    return jnp.concatenate(pieces, 1)


def halves():
    lane = lax.broadcasted_iota(jnp.int32, (1, LANES), 1)
    left = (lane < HEAD).astype(F32)
    return left.astype(LOW), (1.0 - left).astype(LOW)


def attend(x_ref, w_ref, b_ref, lengths_ref, pad_ref, q_ref, k_ref, v_ref, ctx_ref, wide_ref, lse_ref):
    rows = x_ref.shape[0]
    local = w_ref.shape[2]
    scale = float(HEAD) ** (-0.5)
    x = x_ref[...]
    q_ref[...] = ((dot(x, w_ref[0]) + b_ref[0:1, :].astype(F32)) * scale).astype(LOW)
    k_ref[...] = dot(x, w_ref[1]).astype(LOW)
    v_ref[...] = (dot(x, w_ref[2]) + b_ref[1:2, :].astype(F32)).astype(LOW)
    bias = key_mask(lengths_ref, pad_ref, rows)
    sides = halves()
    for pair in range(local // LANES):
        span = slice(pair * LANES, (pair + 1) * LANES)
        query = q_ref[:, span]
        keys = k_ref[:, span]
        flipped = v_ref[:, span].T
        parts = []
        for side in range(2):
            scores = dot_nt(keys * sides[side], query) + bias
            top = jnp.max(scores, 0, keepdims=True)
            expo = jnp.exp(scores - top)
            total = jnp.sum(expo, 0, keepdims=True)
            probs = (expo * (1.0 / total)).astype(LOW)
            parts.append(dot(flipped[side * HEAD : (side + 1) * HEAD], probs))
            head = 2 * pair + side
            lse_ref[head : head + 1, :] = top + jnp.log(total)
        context = jnp.concatenate(parts, 0).T.astype(LOW)
        ctx_ref[:, span] = context
        wide_ref[:, span] = context.astype(F32)


def norm_rows(value):
    centered = value - jnp.mean(value, -1, keepdims=True)
    inverse = lax.rsqrt(jnp.mean(centered * centered, -1, keepdims=True) + EPS_NORM)
    return centered * inverse, inverse


def norm_back(grad, normed, inverse, gain):
    scaled = grad * gain
    return inverse * (
        scaled
        - jnp.mean(scaled, -1, keepdims=True)
        - normed * jnp.mean(scaled * normed, -1, keepdims=True)
    )


def row(ref):
    return ref[...].astype(F32)


def feed(
    core_ref, x_ref, own_ref, far_ref, w_own_ref, w_near_ref, w_far_ref, b_out_ref, gain_ref, shift_ref,
    w_up_ref, b_up_ref, w_down_ref,
    normed_ref, inverse_ref, low_ref, act_ref, slope_ref, part_ref,
    w_full, ctx_full, low_scr,
):
    step = pl.program_id(0)

    @pl.when(step == 0)
    def _():
        half = w_near_ref.shape[0]
        local = own_ref.shape[1]
        mine, side = core_ref[0], core_ref[1]
        here = pl.multiple_of(side * local, LANES)
        there = pl.multiple_of((1 - side) * local, LANES)
        near = pl.multiple_of(there + mine * half, 16)
        far = pl.multiple_of(there + (1 - mine) * half, 16)
        w_full[pl.ds(here, local), :] = w_own_ref[...]
        w_full[pl.ds(near, half), :] = w_near_ref[...].astype(LOW)
        w_full[pl.ds(far, half), :] = w_far_ref[...].astype(LOW)
        ctx_full[:, pl.ds(here, local)] = own_ref[...]
        ctx_full[:, pl.ds(there, local)] = far_ref[...].astype(LOW)
        attn = dot(ctx_full[...], w_full[...])
        normed, inverse = norm_rows(x_ref[...].astype(F32) + attn + row(b_out_ref))
        normed_ref[...] = normed
        inverse_ref[...] = jnp.broadcast_to(inverse, inverse_ref.shape)
        low = (normed * row(gain_ref) + row(shift_ref)).astype(LOW)
        low_ref[...] = low
        low_scr[...] = low

    pre = dot(low_scr[...], w_up_ref[...]) + row(b_up_ref)
    share = 0.5 * (1.0 + lax.erf(pre * 0.7071067811865476))
    act = (pre * share).astype(LOW)
    act_ref[...] = act
    slope_ref[...] = share + pre * jnp.exp(-0.5 * pre * pre) * 0.3989422804014327
    added = dot(act, w_down_ref[...])

    @pl.when(step == 0)
    def _():
        part_ref[...] = added

    @pl.when(step > 0)
    def _():
        part_ref[...] += added


def feed_back(
    own_ref, far_ref, normed_ref, gain1_ref, shift1_ref, b_down_ref, gain_ref, shift_ref, up_ref,
    slope_ref, w_up_ref, w_down_ref,
    out_ref, grad_ref, low_ref, pre_ref, part_ref, sums_ref, b_up_ref,
    low_scr,
):
    step = pl.program_id(0)

    @pl.when(step == 0)
    def _():
        hidden = normed_ref[...] * row(gain1_ref) + row(shift1_ref)
        normed, inverse = norm_rows(hidden + (own_ref[...] + far_ref[...]) + row(b_down_ref))
        gain = row(gain_ref)
        out_ref[...] = (normed * gain + row(shift_ref)).astype(LOW)
        upstream = up_ref[...].astype(F32)
        grad = norm_back(upstream, normed, inverse, gain)
        grad_ref[...] = grad
        low = grad.astype(LOW)
        low_ref[...] = low
        low_scr[...] = low
        sums_ref[0:1, :] = jnp.sum(upstream * normed, 0, keepdims=True)
        sums_ref[1:2, :] = jnp.sum(upstream, 0, keepdims=True)
        sums_ref[2:3, :] = jnp.sum(grad, 0, keepdims=True)
        sums_ref[3:8, :] = jnp.zeros((5, sums_ref.shape[1]), F32)

    pre = (dot_nt(low_scr[...], w_down_ref[...]) * slope_ref[...]).astype(LOW)
    pre_ref[...] = pre
    b_up_ref[...] = jnp.broadcast_to(jnp.sum(pre.astype(F32), 0, keepdims=True), b_up_ref.shape)
    added = dot_nt(pre, w_up_ref[...])

    @pl.when(step == 0)
    def _():
        part_ref[...] = added

    @pl.when(step > 0)
    def _():
        part_ref[...] += added


def attend_back(blocks, *refs):
    count = len(blocks)
    take = iter(refs)
    dr2, own, far, normed, inverse, sums2, up2 = ([next(take) for _ in range(count)] for _ in range(7))
    gain_ref, w_ref, q_ref, k_ref, v_ref, ctx_ref, lse_ref, lengths_ref, pad_ref = (next(take) for _ in range(9))
    dr1_ref, low_ref, e_ref, bias_ref = (next(take) for _ in range(4))
    rows = dr1_ref.shape[0]
    local = q_ref.shape[1]
    width = dr1_ref.shape[1]
    scale = float(HEAD) ** (-0.5)
    gain = row(gain_ref)
    totals = [jnp.zeros((1, width), F32)] * 3
    start = 0
    for i, size in enumerate(blocks):
        grad = dr2[i][...] + (own[i][...] + far[i][...])
        norm = normed[i][...]
        totals[0] = totals[0] + jnp.sum(grad * norm, 0, keepdims=True)
        totals[1] = totals[1] + jnp.sum(grad, 0, keepdims=True)
        dr1 = norm_back(grad, norm, inverse[i][:, 0:1], gain)
        totals[2] = totals[2] + jnp.sum(dr1, 0, keepdims=True)
        dr1_ref[start : start + size, :] = dr1
        low_ref[start : start + size, :] = dr1.astype(LOW)
        start += size
    bias_ref[...] = jnp.zeros(bias_ref.shape, F32)
    twos = sums2[0][...]
    ups = up2[0][0:1, :]
    for i in range(1, count):
        twos = twos + sums2[i][...]
        ups = ups + up2[i][0:1, :]
    bias_ref[0:3, 0:width] = twos[0:3]
    for i in range(3):
        bias_ref[3 + i : 4 + i, 0:width] = totals[i]
    wide_up = ups.shape[1]
    bias_ref[6:7, 0:wide_up] = ups
    d_ctx = dot_nt(low_ref[...], w_ref[...]).astype(LOW)
    mask = key_mask(lengths_ref, pad_ref, rows)
    sides = halves()
    for pair in range(local // LANES):
        span = slice(pair * LANES, (pair + 1) * LANES)
        query = q_ref[:, span]
        keys = k_ref[:, span]
        values = v_ref[:, span]
        grads = d_ctx[:, span]
        flipped = keys.T
        d_q = []
        d_k = jnp.zeros((rows, LANES), F32)
        d_v = jnp.zeros((rows, LANES), F32)
        for side in range(2):
            head = 2 * pair + side
            scores = dot_nt(keys * sides[side], query) + mask
            probs = jnp.exp(scores - lse_ref[head : head + 1, :])
            d_p = dot_nt(values * sides[side], grads)
            mixed = jnp.sum(probs * d_p, 0, keepdims=True)
            d_s = (probs * (d_p - mixed)).astype(LOW)
            d_k = d_k + dot(d_s, query * sides[side])
            d_v = d_v + dot(probs.astype(LOW), grads * sides[side])
            d_q.append(dot(flipped[side * HEAD : (side + 1) * HEAD], d_s))
        d_query = jnp.concatenate(d_q, 0).T.astype(LOW).astype(F32) * scale
        d_k = d_k.astype(LOW)
        d_v = d_v.astype(LOW)
        at = pair * LANES
        e_ref[:, at : at + LANES] = d_query.astype(LOW)
        e_ref[:, local + at : local + at + LANES] = d_k
        e_ref[:, 2 * local + at : 2 * local + at + LANES] = d_v
        bias_ref[7:8, at : at + LANES] = jnp.sum(d_query, 0, keepdims=True)
        bias_ref[7:8, local + at : local + at + LANES] = jnp.sum(d_v.astype(F32), 0, keepdims=True)
    e_ref[:, 3 * local : 4 * local] = ctx_ref[...]


def place_blocks(me, source, target, order, size):
    for i, block in enumerate(order):
        at = pl.multiple_of((me ^ block) * size, size)
        target[i * size : (i + 1) * size, :] = source[pl.ds(at, size), :]


def outer(order, size, splits, last, me_ref, *refs):
    lefts = refs[: len(splits)]
    extra, rest = (refs[len(splits)], refs[len(splits) + 1 :]) if last else (None, refs[len(splits) :])
    rights = rest[: len(splits)]
    send_ref, keep_ref, flipped, placed = rest[len(splits) :]
    step = pl.program_id(0)

    def place(index, source):
        if order is None:
            placed[index] = source
        else:
            flipped[...] = source
            place_blocks(me_ref[0], flipped, placed.at[index], order, size)

    @pl.when(step == 0)
    def _():
        place(0, jnp.concatenate([ref[...].T for ref in lefts], 1))
        if last:
            place(1, extra[...].T)

    if last:
        left = placed[jnp.where(step == pl.num_programs(0) - 1, 1, 0)]
    else:
        left = placed[0]
    right = jnp.concatenate([ref[...] for ref in rights], 0)
    half = send_ref.shape[0]
    send_ref[...] = dot(left[0:half], right)
    keep_ref[...] = dot(left[half:], right)


def back_tokens(e_ref, w_ref, out_ref):
    local = w_ref.shape[2]
    out_ref[...] = (
        dot_nt(e_ref[:, 0:local], w_ref[0])
        + dot_nt(e_ref[:, local : 2 * local], w_ref[1])
        + dot_nt(e_ref[:, 2 * local : 3 * local], w_ref[2])
    )


def on_device(
    tokens, lengths, pad_mask, w_qkv, b_qv, w_out, b_out, ln1_gain, ln1_bias,
    w_up, b_up, w_down, b_down, ln2_gain, ln2_bias, cotangent,
):
    rows, width = tokens.shape
    local = w_qkv.shape[2]
    heads = local // HEAD
    hidden = w_up.shape[1]
    ranks = lax.axis_size("dp")
    me = lax.axis_index("dp").astype(jnp.int32)
    me_arr = me.reshape(1)
    core_arr = jnp.stack([me % 2, lax.axis_index("tp").astype(jnp.int32)])
    size = width // ranks
    blocks = [LANES, rows - LANES] if rows > LANES else [rows]
    lse_rows = -(-heads // 8) * 8

    def swap_tp(array):
        pairs = [(i, i ^ 1) for i in range(lax.axis_size("tp"))]
        return lax.ppermute(array, "tp", pairs)

    def swap_dp(array, bits):
        return lax.ppermute(array, "dp", [(i, i ^ bits) for i in range(ranks)])

    def as_row(vector):
        return vector.reshape(1, -1)

    stages = []
    done = 1
    while done < ranks:
        ways = 2 if done < 4 else min(4, ranks // done)
        stages.append((done, ways))
        done *= ways
    order = [0]
    for step, ways in reversed(stages):
        order = [i * step + rest for i in range(ways) for rest in order]
    order = [p for p in order if p % 2 == 1] + [p for p in order if p % 2 == 0]
    fused = size % 16 == 0

    smem = pl.BlockSpec(memory_space=pltpu.SMEM)
    pad_row = as_row(pad_mask)

    low_rows = jax.ShapeDtypeStruct((rows, local), LOW)
    query, keys, values, context, context_wide, lse = pl.pallas_call(
        attend,
        out_shape=(
            low_rows, low_rows, low_rows, low_rows,
            jax.ShapeDtypeStruct((rows, local), F32),
            jax.ShapeDtypeStruct((lse_rows, rows), F32),
        ),
        in_specs=[pl.BlockSpec(memory_space=pltpu.VMEM)] * 3 + [smem, pl.BlockSpec(memory_space=pltpu.VMEM)],
        compiler_params=params(),
        cost_estimate=cost(2 * rows * width * 3 * local + 4 * rows * rows * local * 2, 6 * MIB, heads * rows * rows),
        name="attend",
    )(tokens, w_qkv, b_qv, lengths, pad_row)

    half = w_out.shape[0] // 2
    w_piece = lax.dynamic_slice_in_dim(w_out, (me % 2) * half, half, 0).astype(F32)
    w_near = swap_tp(w_piece)
    w_far = swap_dp(w_near, 1)
    context_far = swap_tp(context_wide)

    tile = min(hidden, 512)
    tiles = hidden // tile
    saved = []
    start = 0
    for block in blocks:
        index = start // block if start % block == 0 else None
        begin = start

        def cut(array):
            return lax.slice_in_dim(array, begin, begin + block, axis=0)

        own = jax.ShapeDtypeStruct
        outs = pl.pallas_call(
            feed,
            grid=(tiles,),
            out_shape=(
                own((block, width), F32), own((block, LANES), F32), own((block, width), LOW),
                own((block, hidden), LOW), own((block, hidden), F32), own((block, width), F32),
            ),
            in_specs=[
                smem, whole((block, width)), whole((block, local)), whole((block, local)),
                whole((local, width)), whole((half, width)), whole((half, width)),
                whole((1, width)), whole((1, width)), whole((1, width)),
                pl.BlockSpec((width, tile), lambda f: (0, f)),
                pl.BlockSpec((1, tile), lambda f: (0, f)),
                pl.BlockSpec((tile, width), lambda f: (f, 0)),
            ],
            out_specs=(
                whole((block, width)), whole((block, LANES)), whole((block, width)),
                pl.BlockSpec((block, tile), lambda f: (0, f)),
                pl.BlockSpec((block, tile), lambda f: (0, f)),
                whole((block, width)),
            ),
            scratch_shapes=[
                pltpu.VMEM((2 * local, width), LOW),
                pltpu.VMEM((block, 2 * local), LOW),
                pltpu.VMEM((block, width), LOW),
            ],
            compiler_params=params(),
            cost_estimate=cost(4 * block * width * (hidden + local), 8 * MIB, 2 * block * hidden),
            name="feed",
        )(
            core_arr, cut(tokens), cut(context), cut(context_far), w_out, w_near, w_far,
            as_row(b_out), as_row(ln1_gain), as_row(ln1_bias), w_up, as_row(b_up), w_down,
        )
        saved.append(outs + (swap_tp(outs[5]),))
        start += block

    back = []
    start = 0
    for block, (normed, inverse, low, act, slope, part, far) in zip(blocks, saved):
        own = jax.ShapeDtypeStruct
        outs = pl.pallas_call(
            feed_back,
            grid=(tiles,),
            out_shape=(
                own((block, width), LOW), own((block, width), F32), own((block, width), LOW),
                own((block, hidden), LOW), own((block, width), F32), own((8, width), F32), own((8, hidden), F32),
            ),
            in_specs=[whole((block, width))] * 3 + [whole((1, width))] * 5 + [
                whole((block, width)),
                pl.BlockSpec((block, tile), lambda f: (0, f)),
                pl.BlockSpec((width, tile), lambda f: (0, f)),
                pl.BlockSpec((tile, width), lambda f: (f, 0)),
            ],
            out_specs=(
                whole((block, width)), whole((block, width)), whole((block, width)),
                pl.BlockSpec((block, tile), lambda f: (0, f)),
                whole((block, width)), whole((8, width)),
                pl.BlockSpec((8, tile), lambda f: (0, f)),
            ),
            scratch_shapes=[pltpu.VMEM((block, width), LOW)],
            compiler_params=params(),
            cost_estimate=cost(4 * block * width * hidden, 8 * MIB),
            name="feed_back",
        )(
            part, far, normed, as_row(ln1_gain), as_row(ln1_bias), as_row(b_down), as_row(ln2_gain), as_row(ln2_bias),
            lax.slice_in_dim(cotangent, start, start + block, axis=0), slope, w_up, w_down,
        )
        back.append(outs + (swap_tp(outs[4]),))
        start += block

    layer_out = jnp.concatenate([outs[0] for outs in back], 0)

    def gradient(lefts, rights, splits, columns, step, extra=None):
        last = extra is not None
        halved = jax.ShapeDtypeStruct((width // 2, columns), F32)
        send, keep = pl.pallas_call(
            functools.partial(outer, order if fused else None, size, splits, last),
            grid=(columns // step,),
            out_shape=(halved, halved),
            in_specs=[smem]
            + [whole((split, width)) for split in splits]
            + ([whole((rows, width))] if last else [])
            + [pl.BlockSpec((split, step), lambda n: (0, n)) for split in splits],
            out_specs=(pl.BlockSpec((width // 2, step), lambda n: (0, n)),) * 2,
            scratch_shapes=[pltpu.VMEM((width, rows), LOW), pltpu.VMEM((2 if last else 1, width, rows), LOW)],
            compiler_params=params(),
            cost_estimate=cost(2 * rows * width * columns, 8 * MIB),
            name="outer",
        )(me_arr, *lefts, *([extra] if last else []), *rights)
        if not fused:
            full = jnp.concatenate([send, keep], 0).reshape(ranks, size, columns)
            full = jnp.take(full, jnp.array(order, jnp.int32) ^ me, axis=0).reshape(width, columns)
            send, keep = full[: width // 2], full[width // 2 :]
        return send, keep

    def scatter(send, keep):
        held = [keep, swap_dp(send, 1)]
        for step, ways in stages[1:]:
            share = held[0].shape[0] // ways
            came = []
            for way in range(1, ways):
                out = functools.reduce(jnp.add, [a[way * share : (way + 1) * share] for a in held])
                came.append(swap_dp(out, way * step))
            held = [a[:share] for a in held]
            if ways == 4:
                held = [functools.reduce(jnp.add, held) + came[0], came[1] + came[2]]
            else:
                held = held + came
        return functools.reduce(jnp.add, held)

    def total(array):
        for step, ways in stages:
            came = [swap_dp(array, way * step) for way in range(1, ways)]
            if ways == 4:
                array = (array + came[0]) + (came[1] + came[2])
            else:
                array = array + came[0]
        return array

    down = scatter(*gradient([o[2] for o in back], [s[3] for s in saved], blocks, hidden, tile))
    up = scatter(*gradient([s[2] for s in saved], [o[3] for o in back], blocks, hidden, tile))

    vmem = pl.BlockSpec(memory_space=pltpu.VMEM)
    wide = max(width, hidden, 2 * local)
    dr1, dr1_low, e, bias = pl.pallas_call(
        functools.partial(attend_back, blocks),
        out_shape=(
            jax.ShapeDtypeStruct((rows, width), F32), jax.ShapeDtypeStruct((rows, width), LOW),
            jax.ShapeDtypeStruct((rows, 4 * local), LOW), jax.ShapeDtypeStruct((8, wide), F32),
        ),
        in_specs=[vmem] * (7 * len(blocks) + 7) + [smem, vmem],
        compiler_params=params(),
        cost_estimate=cost(2 * rows * width * local + 10 * rows * rows * local * 2, 8 * MIB, heads * rows * rows),
        name="attend_back",
    )(
        *[o[1] for o in back], *[o[4] for o in back], *[o[7] for o in back],
        *[s[0] for s in saved], *[s[1] for s in saved], *[o[5] for o in back], *[o[6] for o in back],
        as_row(ln1_gain), w_out, query, keys, values, context, lse, lengths, pad_row,
    )
    bias = total(bias)
    mixed = scatter(*gradient([tokens], [e], [rows], 4 * local, local, dr1_low))
    part = pl.pallas_call(
        back_tokens,
        out_shape=jax.ShapeDtypeStruct((rows, width), F32),
        in_specs=[vmem] * 2,
        compiler_params=params(),
        cost_estimate=cost(6 * rows * width * local, 5 * MIB),
        name="back_tokens",
    )(e, w_qkv)
    d_tokens = dr1 + (part + swap_tp(part))
    d_w_qkv = mixed[:, : 3 * local].reshape(size, 3, local).transpose(1, 0, 2)
    return (
        layer_out,
        d_tokens,
        d_w_qkv,
        bias[7, : 2 * local].reshape(2, local),
        mixed[:, 3 * local :].T,
        bias[5, :width],
        bias[3, :width],
        bias[4, :width],
        up,
        bias[6, :hidden],
        down.T,
        bias[2, :width],
        bias[0, :width],
        bias[1, :width],
    )


def solution(mesh):
    placed = (
        P("dp", None), P("dp", None), P("dp"), P(None, None, "tp"), P(None, "tp"), P("tp", None),
        P(), P(), P(), P(None, "tp"), P("tp"), P("tp", None), P(), P(), P(), P("dp", None),
    )
    return jax.shard_map(
        on_device,
        mesh=mesh,
        in_specs=placed,
        out_specs=(
            P("dp", None), P("dp", None), P(None, "dp", "tp"), P(None, "tp"), P("tp", "dp"), P(), P(), P(),
            P("dp", "tp"), P("tp"), P("tp", "dp"), P(), P(), P(),
        ),
        check_vma=False,
    )
```

```python
import functools

import jax
import jax.numpy as jnp
from jax import lax
from jax.experimental import pallas as pl
from jax.experimental.pallas import tpu as pltpu
from jax.sharding import PartitionSpec as P

HEAD = 64
NEG_FILL = -1e30
EPS_NORM = 1e-12
LANES = 128
F32 = jnp.float32
LOW = jnp.bfloat16
MIB = 1 << 20


def dot(a, b):
    return lax.dot_general(a, b, (((1,), (0,)), ((), ())), preferred_element_type=F32)


def dot_nt(a, b):
    return lax.dot_general(a, b, (((1,), (1,)), ((), ())), preferred_element_type=F32)


def whole(shape):
    return pl.BlockSpec(shape, lambda *_: (0,) * len(shape))


def params(limit=24):
    return pltpu.CompilerParams(vmem_limit_bytes=limit * MIB)


def cost(micros):
    return pl.CostEstimate(flops=int(micros * 1e9), bytes_accessed=int(micros * 3e6), transcendentals=0)


def key_mask(lengths_ref, pad_ref, rows):
    seqs = lengths_ref.shape[1]
    key_at = lax.broadcasted_iota(jnp.int32, (rows, LANES), 0)
    query_at = lax.broadcasted_iota(jnp.int32, (8, rows), 1)
    key_seg = jnp.zeros((rows, LANES), jnp.int32)
    query_seg = jnp.zeros((8, rows), jnp.int32)
    end = jnp.int32(0)
    for i in range(seqs):
        end = end + lengths_ref[0, i]
        key_seg = key_seg + (key_at >= end).astype(jnp.int32)
        query_seg = query_seg + (query_at >= end).astype(jnp.int32)
    pad = jnp.broadcast_to(pad_ref[...].astype(F32), (LANES, rows)).T
    pieces = []
    for j in range(rows // LANES):
        span = slice(j * LANES, (j + 1) * LANES)
        same = key_seg == query_seg[0:1, span]
        usable = (pad == 1.0) | (key_at == query_at[0:1, span])
        pieces.append(jnp.where(same & usable, 0.0, NEG_FILL))
    return jnp.concatenate(pieces, 1)


def halves():
    lane = lax.broadcasted_iota(jnp.int32, (1, LANES), 1)
    left = (lane < HEAD).astype(F32)
    return left.astype(LOW), (1.0 - left).astype(LOW)


def project(place_ref, x_ref, w_ref, b_ref, w_out_ref, qkv_ref, piece_ref):
    local = w_ref.shape[2]
    scale = float(HEAD) ** (-0.5)
    part = piece_ref.shape[0]
    piece_ref[...] = w_out_ref[pl.ds(pl.multiple_of(place_ref[0] * part, 16), part), :].astype(F32)
    x = x_ref[...]
    qkv_ref[:, 0:local] = ((dot(x, w_ref[0]) + b_ref[0:1, :].astype(F32)) * scale).astype(LOW)
    qkv_ref[:, local : 2 * local] = dot(x, w_ref[1]).astype(LOW)
    qkv_ref[:, 2 * local :] = (dot(x, w_ref[2]) + b_ref[1:2, :].astype(F32)).astype(LOW)


def attend(blocks, qkv_ref, lengths_ref, pad_ref, ctx_ref, lse_ref, *wide_refs):
    rows = qkv_ref.shape[0]
    local = ctx_ref.shape[1]
    bias = key_mask(lengths_ref, pad_ref, rows)
    sides = halves()
    for pair in range(local // LANES):
        at = pair * LANES
        span = slice(at, at + LANES)
        query = qkv_ref[:, span]
        keys = qkv_ref[:, local + at : local + at + LANES]
        flipped = qkv_ref[:, 2 * local + at : 2 * local + at + LANES].T
        parts = []
        for side in range(2):
            scores = dot_nt(keys * sides[side], query) + bias
            top = jnp.max(scores, 0, keepdims=True)
            expo = jnp.exp(scores - top)
            total = jnp.sum(expo, 0, keepdims=True)
            probs = (expo * (1.0 / total)).astype(LOW)
            parts.append(dot(flipped[side * HEAD : (side + 1) * HEAD], probs))
            head = 2 * pair + side
            lse_ref[head : head + 1, :] = top + jnp.log(total)
        context = jnp.concatenate(parts, 0).T.astype(LOW)
        ctx_ref[:, span] = context
        start = 0
        for wide_ref, size in zip(wide_refs, blocks):
            wide_ref[:, span] = context[start : start + size].astype(F32)
            start += size


def norm_rows(value):
    centered = value - jnp.mean(value, -1, keepdims=True)
    inverse = lax.rsqrt(jnp.mean(centered * centered, -1, keepdims=True) + EPS_NORM)
    return centered * inverse, inverse


def norm_back(grad, normed, inverse, gain):
    scaled = grad * gain
    return inverse * (
        scaled
        - jnp.mean(scaled, -1, keepdims=True)
        - normed * jnp.mean(scaled * normed, -1, keepdims=True)
    )


def row(ref):
    return ref[...].astype(F32)


def feed(
    taken, place_ref, x_ref, own_ref, far_ref, w_own_ref, w_a_ref, w_b_ref, w_c_ref, w_d_ref,
    vec_ref, w_up_ref, b_up_ref, w_down_ref,
    normed_ref, inverse_ref, low_ref, act_ref, slope_ref, part_ref,
    w_full, ctx_full, low_scr,
):
    step = pl.program_id(0)

    @pl.when(step == 0)
    def _():
        part = w_a_ref.shape[0]
        local = own_ref.shape[1]
        mine, side = place_ref[0], place_ref[1]
        here = pl.multiple_of(side * local, LANES)
        there = pl.multiple_of((1 - side) * local, LANES)
        w_full[pl.ds(here, local), :] = w_own_ref[...]
        for bits, ref in ((0, w_a_ref), (2, w_b_ref), (1, w_c_ref), (3, w_d_ref)):
            at = pl.multiple_of(there + (mine ^ bits) * part, 16)
            w_full[pl.ds(at, part), :] = ref[...].astype(LOW)
        ctx_full[:, pl.ds(here, local)] = own_ref[taken, :]
        ctx_full[:, pl.ds(there, local)] = far_ref[...].astype(LOW)
        attn = dot(ctx_full[...], w_full[...])
        normed, inverse = norm_rows(x_ref[taken, :].astype(F32) + attn + vec_ref[0:1, :])
        normed_ref[...] = normed
        inverse_ref[...] = jnp.broadcast_to(inverse, inverse_ref.shape)
        low = (normed * vec_ref[1:2, :] + vec_ref[2:3, :]).astype(LOW)
        low_ref[...] = low
        low_scr[...] = low

    pre = dot(low_scr[...], w_up_ref[...]) + row(b_up_ref)
    share = 0.5 * (1.0 + lax.erf(pre * 0.7071067811865476))
    act = (pre * share).astype(LOW)
    act_ref[...] = act
    slope_ref[...] = share + pre * jnp.exp(-0.5 * pre * pre) * 0.3989422804014327
    added = dot(act, w_down_ref[...])

    @pl.when(step == 0)
    def _():
        part_ref[...] = added

    @pl.when(step > 0)
    def _():
        part_ref[...] += added


def feed_back(
    taken, own_ref, far_ref, normed_ref, vec_ref, up_ref,
    slope_ref, w_up_ref, w_down_ref,
    out_ref, grad_ref, low_ref, pre_ref, part_ref, sums_ref, b_up_ref,
    low_scr,
):
    step = pl.program_id(0)

    @pl.when(step == 0)
    def _():
        hidden = normed_ref[...] * vec_ref[1:2, :] + vec_ref[2:3, :]
        normed, inverse = norm_rows(hidden + (own_ref[...] + far_ref[...]) + vec_ref[3:4, :])
        gain = vec_ref[4:5, :]
        out_ref[...] = (normed * gain + vec_ref[5:6, :]).astype(LOW)
        upstream = up_ref[taken, :].astype(F32)
        grad = norm_back(upstream, normed, inverse, gain)
        grad_ref[...] = grad
        low = grad.astype(LOW)
        low_ref[...] = low
        low_scr[...] = low
        sums_ref[0:1, :] = jnp.sum(upstream * normed, 0, keepdims=True)
        sums_ref[1:2, :] = jnp.sum(upstream, 0, keepdims=True)
        sums_ref[2:3, :] = jnp.sum(grad, 0, keepdims=True)
        sums_ref[3:8, :] = jnp.zeros((5, sums_ref.shape[1]), F32)

    pre = (dot_nt(low_scr[...], w_down_ref[...]) * slope_ref[...]).astype(LOW)
    pre_ref[...] = pre
    b_up_ref[...] = jnp.broadcast_to(jnp.sum(pre.astype(F32), 0, keepdims=True), b_up_ref.shape)
    added = dot_nt(pre, w_up_ref[...])

    @pl.when(step == 0)
    def _():
        part_ref[...] = added

    @pl.when(step > 0)
    def _():
        part_ref[...] += added


def norm_one_back(blocks, *refs):
    count = len(blocks)
    take = iter(refs)
    dr2, own, far, normed, inverse, sums2, up2 = ([next(take) for _ in range(count)] for _ in range(7))
    vec_ref = next(take)
    dr1_ref, low_ref, bias_ref = (next(take) for _ in range(3))
    width = dr1_ref.shape[1]
    gain = vec_ref[1:2, :]
    totals = [jnp.zeros((1, width), F32)] * 3
    start = 0
    for i, size in enumerate(blocks):
        grad = dr2[i][...] + (own[i][...] + far[i][...])
        norm = normed[i][...]
        totals[0] = totals[0] + jnp.sum(grad * norm, 0, keepdims=True)
        totals[1] = totals[1] + jnp.sum(grad, 0, keepdims=True)
        dr1 = norm_back(grad, norm, inverse[i][:, 0:1], gain)
        totals[2] = totals[2] + jnp.sum(dr1, 0, keepdims=True)
        dr1_ref[start : start + size, :] = dr1
        low_ref[start : start + size, :] = dr1.astype(LOW)
        start += size
    bias_ref[...] = jnp.zeros(bias_ref.shape, F32)
    twos = sums2[0][...]
    ups = up2[0][0:1, :]
    for i in range(1, count):
        twos = twos + sums2[i][...]
        ups = ups + up2[i][0:1, :]
    bias_ref[0:3, 0:width] = twos[0:3]
    for i in range(3):
        bias_ref[3 + i : 4 + i, 0:width] = totals[i]
    bias_ref[6:7, 0 : ups.shape[1]] = ups


def attend_back(low_ref, w_ref, qkv_ref, ctx_ref, lse_ref, lengths_ref, pad_ref, so_far_ref, e_ref, bias_ref):
    rows = qkv_ref.shape[0]
    local = ctx_ref.shape[1]
    scale = float(HEAD) ** (-0.5)
    bias_ref[...] = so_far_ref[...]
    d_ctx = dot_nt(low_ref[...], w_ref[...]).astype(LOW)
    mask = key_mask(lengths_ref, pad_ref, rows)
    sides = halves()
    for pair in range(local // LANES):
        at = pair * LANES
        span = slice(at, at + LANES)
        query = qkv_ref[:, span]
        keys = qkv_ref[:, local + at : local + at + LANES]
        values = qkv_ref[:, 2 * local + at : 2 * local + at + LANES]
        grads = d_ctx[:, span]
        flipped = keys.T
        d_q = []
        d_k = jnp.zeros((rows, LANES), F32)
        d_v = jnp.zeros((rows, LANES), F32)
        for side in range(2):
            head = 2 * pair + side
            scores = dot_nt(keys * sides[side], query) + mask
            probs = jnp.exp(scores - lse_ref[head : head + 1, :])
            d_p = dot_nt(values * sides[side], grads)
            mixed = jnp.sum(probs * d_p, 0, keepdims=True)
            d_s = (probs * (d_p - mixed)).astype(LOW)
            d_k = d_k + dot(d_s, query * sides[side])
            d_v = d_v + dot(probs.astype(LOW), grads * sides[side])
            d_q.append(dot(flipped[side * HEAD : (side + 1) * HEAD], d_s))
        d_query = jnp.concatenate(d_q, 0).T.astype(LOW).astype(F32) * scale
        d_k = d_k.astype(LOW)
        d_v = d_v.astype(LOW)
        e_ref[:, at : at + LANES] = d_query.astype(LOW)
        e_ref[:, local + at : local + at + LANES] = d_k
        e_ref[:, 2 * local + at : 2 * local + at + LANES] = d_v
        bias_ref[7:8, at : at + LANES] = jnp.sum(d_query, 0, keepdims=True)
        bias_ref[7:8, local + at : local + at + LANES] = jnp.sum(d_v.astype(F32), 0, keepdims=True)
    e_ref[:, 3 * local : 4 * local] = ctx_ref[...]


def place_blocks(me, source, target, order, size):
    for i, block in enumerate(order):
        at = pl.multiple_of((me ^ block) * size, size)
        target[i * size : (i + 1) * size, :] = source[pl.ds(at, size), :]


def outer(order, size, splits, kinds, place_ref, *refs):
    count = len(splits)
    sides = max(kinds) + 1
    lefts = [refs[i * count : (i + 1) * count] for i in range(sides)]
    rights = refs[sides * count : (sides + 1) * count]
    high_ref, low_ref, keep_ref, flipped, placed = refs[-5:]
    step = pl.program_id(0)

    @pl.when(step == 0)
    def _():
        for index, group in enumerate(lefts):
            source = jnp.concatenate([ref[...] for ref in group], 0).T
            if order is None:
                placed[index] = source
            else:
                flipped[...] = source
                place_blocks(place_ref[2], flipped, placed.at[index], order, size)

    left = placed[0]
    if sides > 1:
        change = kinds.index(1)
        left = placed[jnp.where(step >= change, 1, 0)]
    right = jnp.concatenate([ref[...] for ref in rights], 0)
    part = high_ref.shape[0]
    low_ref[...] = dot(left[0:part], right)
    high_ref[...] = dot(left[part : 2 * part], right)
    keep_ref[...] = dot(left[2 * part :], right)


def fold(*refs):
    value = refs[0][...]
    for ref in refs[1:-1]:
        value = value + ref[...]
    refs[-1][...] = value


def back_tokens(e_ref, w_ref, out_ref):
    local = w_ref.shape[2]
    out_ref[...] = (
        dot_nt(e_ref[:, 0:local], w_ref[0])
        + dot_nt(e_ref[:, local : 2 * local], w_ref[1])
        + dot_nt(e_ref[:, 2 * local : 3 * local], w_ref[2])
    )


def join(dr1_ref, own_ref, far_ref, out_ref):
    out_ref[...] = dr1_ref[...] + (own_ref[...] + far_ref[...])


def spread(local, *refs):
    qkv_ref, out_ref = refs[-2:]
    value = refs[0][...]
    for ref in refs[1:-2]:
        value = value + ref[...]
    for i in range(3):
        qkv_ref[i] = value[:, i * local : (i + 1) * local]
    out_ref[...] = value[:, 3 * local :]


def chained(kernel, inputs, outputs):
    def body(*refs):
        refs[1 + inputs + outputs][...] = jnp.zeros((8, LANES), F32)
        kernel(*refs[1 : 1 + inputs + outputs], *refs[2 + inputs + outputs :])

    return body


def on_device(
    tokens, lengths, pad_mask, w_qkv, b_qv, w_out, b_out, ln1_gain, ln1_bias,
    w_up, b_up, w_down, b_down, ln2_gain, ln2_bias, cotangent,
):
    rows, width = tokens.shape
    local = w_qkv.shape[2]
    heads = local // HEAD
    hidden = w_up.shape[1]
    ranks = lax.axis_size("dp")
    me = lax.axis_index("dp").astype(jnp.int32)
    place_arr = jnp.stack([me % 4, lax.axis_index("tp").astype(jnp.int32), me])
    size = width // ranks
    blocks = [rows // 2] * 2 if rows % 32 == 0 else [rows]
    starts = [sum(blocks[:i]) for i in range(len(blocks))]
    lse_rows = -(-heads // 8) * 8
    shape = jax.ShapeDtypeStruct
    smem = pl.BlockSpec(memory_space=pltpu.SMEM)
    loose = pl.BlockSpec(memory_space=pl.ANY)
    mark = [None]

    def call(kernel, name, micros, operands, in_specs, out_shape, out_specs, grid=(1,), scratch=()):
        before = mark[0] if mark[0] is not None else operands[0]
        *outs, mark[0] = pl.pallas_call(
            chained(kernel, len(operands), len(out_shape)),
            grid=grid,
            out_shape=tuple(out_shape) + (shape((8, LANES), F32),),
            in_specs=[loose] + list(in_specs),
            out_specs=tuple(out_specs) + (whole((8, LANES)),),
            scratch_shapes=list(scratch),
            compiler_params=params(),
            cost_estimate=cost(micros),
            name=name,
        )(before, *operands)
        return outs

    def full(*arrays):
        return [whole(array.shape) for array in arrays]

    def swap_tp(array):
        pairs = [(i, i ^ 1) for i in range(lax.axis_size("tp"))]
        return lax.ppermute(array, "tp", pairs)

    def swap_dp(array, bits):
        return lax.ppermute(array, "dp", [(i, i ^ bits) for i in range(ranks)])

    stages = []
    while 1 << len(stages) < ranks:
        stages.append(1 << len(stages))
    order = [0]
    for bit in reversed(stages):
        order = order + [bit + rest for rest in order]
    order = order[ranks // 2 :] + order[: ranks // 2]
    fused = size % 16 == 0
    pad_row = pad_mask.reshape(1, rows)
    zero = jnp.zeros((width,), LOW)
    vectors = jnp.stack([b_out, ln1_gain, ln1_bias, b_down, ln2_gain, ln2_bias, zero, zero]).astype(F32)
    b_up_row = b_up.reshape(1, hidden)

    part = w_out.shape[0] // 4
    outs = [shape((rows, 3 * local), LOW), shape((part, width), F32)]
    qkv, piece = call(
        project, "project", 2, [place_arr, tokens, w_qkv, b_qv, w_out],
        [smem] + full(tokens, w_qkv, b_qv, w_out), outs, full(*outs),
    )
    w_a = swap_tp(piece)
    outs = [shape((rows, local), LOW), shape((lse_rows, rows), F32)] + [shape((block, local), F32) for block in blocks]
    context, lse, *wides = call(
        functools.partial(attend, blocks), "attend", 4, [qkv, lengths, pad_row],
        full(qkv) + [smem] + full(pad_row), outs, full(*outs),
    )
    fars = [swap_tp(wide) for wide in wides]
    w_b = swap_dp(w_a, 2)
    w_c, w_d = swap_dp(w_a, 1), swap_dp(w_b, 1)

    tile = min(hidden, 512)
    tiles = hidden // tile

    def columns(height, step):
        return pl.BlockSpec((height, step), lambda f: (0, f))

    down_spec = pl.BlockSpec((tile, width), lambda f: (f, 0))
    saved = []
    for begin, block, far in zip(starts, blocks, fars):
        outs = [
            shape((block, width), F32), shape((block, LANES), F32), shape((block, width), LOW),
            shape((block, hidden), LOW), shape((block, hidden), F32), shape((block, width), F32),
        ]
        outs = call(
            functools.partial(feed, slice(begin, begin + block)), "feed", 5,
            [place_arr, tokens, context, far, w_out, w_a, w_b, w_c, w_d, vectors, w_up, b_up_row, w_down],
            [smem] + full(tokens, context, far, w_out, w_a, w_b, w_c, w_d, vectors)
            + [columns(width, tile), columns(1, tile), down_spec],
            outs,
            full(*outs[:3]) + [columns(block, tile), columns(block, tile), whole((block, width))],
            grid=(tiles,),
            scratch=[
                pltpu.VMEM((2 * local, width), LOW),
                pltpu.VMEM((block, 2 * local), LOW),
                pltpu.VMEM((block, width), LOW),
            ],
        )
        saved.append(outs + [swap_tp(outs[5])])

    back = []
    for begin, block, (normed, inverse, low, act, slope, own, far) in zip(starts, blocks, saved):
        outs = [
            shape((block, width), LOW), shape((block, width), F32), shape((block, width), LOW),
            shape((block, hidden), LOW), shape((block, width), F32), shape((8, width), F32), shape((8, hidden), F32),
        ]
        outs = call(
            functools.partial(feed_back, slice(begin, begin + block)), "feed_back", 5,
            [own, far, normed, vectors, cotangent, slope, w_up, w_down],
            full(own, far, normed, vectors, cotangent) + [columns(block, tile), columns(width, tile), down_spec],
            outs,
            full(*outs[:3]) + [columns(block, tile)] + full(*outs[4:6]) + [columns(8, tile)],
            grid=(tiles,),
            scratch=[pltpu.VMEM((block, width), LOW)],
        )
        back.append(outs + [swap_tp(outs[4])])

    layer_out = jnp.concatenate([outs[0] for outs in back], 0)

    def gradient(lefts, rights, splits, kinds, step):
        wide = step * len(kinds)
        sides = max(kinds) + 1
        outs = [shape((width // 4, wide), F32), shape((width // 4, wide), F32), shape((width // 2, wide), F32)]
        high, low, keep = call(
            functools.partial(outer, order if fused else None, size, splits, kinds), "outer", 3,
            [place_arr, *lefts, *rights],
            [smem] + full(*lefts) + [columns(split, step) for split in splits],
            outs,
            [columns(width // 4, step), columns(width // 4, step), columns(width // 2, step)],
            grid=(len(kinds),),
            scratch=[pltpu.VMEM((width, rows), LOW), pltpu.VMEM((sides, width, rows), LOW)],
        )
        if not fused:
            every = jnp.concatenate([low, high, keep], 0).reshape(ranks, size, wide)
            every = jnp.take(every, jnp.array(order, jnp.int32) ^ me, axis=0).reshape(width, wide)
            low, high, keep = every[: width // 4], every[width // 4 : width // 2], every[width // 2 :]
        return high, low, keep

    def pick(held, begin, end):
        return [(array, first) for array, first in held if first <= begin and end <= first + array.shape[0]]

    def add(held, begin, end):
        wide = held[0][0].shape[1]
        inside = pick(held, begin, end)
        if not fused:
            return functools.reduce(jnp.add, [array[begin - first : end - first] for array, first in inside])

        def at(first):
            return pl.BlockSpec((size, wide), lambda n: (n + (begin - first) // size, 0))

        return call(
            fold, "fold", 1, [array for array, _ in inside], [at(first) for _, first in inside],
            [shape((end - begin, wide), F32)], [pl.BlockSpec((size, wide), lambda n: (n, 0))],
            grid=((end - begin) // size,),
        )[0]

    class Chunk:
        def __init__(self, high, low, keep):
            self.held = [(keep, 0), (swap_dp(high, stages[0]), width // 4), (swap_dp(low, stages[0]), 0)]
            self.stage = 0

        def high(self):
            self.stage += 1
            half = self.half = width // (4 << (self.stage - 1))
            if half > size:
                out = add(self.held, half + half // 2, 2 * half)
                self.came = [(swap_dp(out, stages[self.stage]), half // 2)]
            else:
                out = add(self.held, half, 2 * half)
                self.held = self.held + [(swap_dp(out, stages[self.stage]), 0)]

        def low(self):
            out = add(self.held, self.half, self.half + self.half // 2)
            self.held = self.held + self.came + [(swap_dp(out, stages[self.stage]), 0)]

        def rest(self):
            while self.stage < len(stages) - 1:
                self.high()
                if self.half > size:
                    self.low()
            return [(array, first) for array, first in self.held if first == 0]

    down = Chunk(*gradient([o[2] for o in back], [s[3] for s in saved], blocks, [0] * tiles, tile))
    up = Chunk(*gradient([s[2] for s in saved], [o[3] for o in back], blocks, [0] * tiles, tile))
    down.high()
    down.low()
    down.high()
    wide = max(width, hidden, 2 * local)
    outs = [shape((rows, width), F32), shape((rows, width), LOW), shape((8, wide), F32)]
    operands = [array for i in (1, 4, 7) for array in [o[i] for o in back]]
    operands += [array for i in (0, 1) for array in [s[i] for s in saved]]
    operands += [array for i in (5, 6) for array in [o[i] for o in back]] + [vectors]
    dr1, dr1_low, bias = call(
        functools.partial(norm_one_back, blocks), "norm_one_back", 2, operands, full(*operands), outs, full(*outs)
    )
    up.high()
    up.low()
    down.low()
    down.high()
    outs = [shape((rows, 4 * local), LOW), shape((8, wide), F32)]
    e, bias = call(
        attend_back, "attend_back", 6, [dr1_low, w_out, qkv, context, lse, lengths, pad_row, bias],
        full(dr1_low, w_out, qkv, context, lse) + [smem] + full(pad_row, bias), outs, full(*outs),
    )
    mixed = Chunk(*gradient([tokens, dr1_low], [e], [rows], [0, 0, 0, 1], local))

    def bias_step(bit):
        far = swap_dp(bias, bit)
        return call(fold, "fold", 1, [bias, far], full(bias, far), [shape(bias.shape, F32)], full(bias))[0]

    up.high()
    mixed.high()
    mixed.low()
    bias = bias_step(stages[0])
    outs = [shape((rows, width), F32)]
    (partial,) = call(back_tokens, "back_tokens", 2, [e, w_qkv], full(e, w_qkv), outs, full(*outs))
    partial_far = swap_tp(partial)
    up.low()
    bias = bias_step(stages[1])
    up.high()
    mixed.high()
    bias = bias_step(stages[2])
    outs = [shape((rows, width), F32)]
    third = pl.BlockSpec((blocks[0], width), lambda n: (n, 0))
    (d_tokens,) = call(
        join, "join", 2, [dr1, partial, partial_far], [third] * 3, outs, [third], grid=(rows // blocks[0],)
    )
    mixed.low()
    mixed.high()
    for bit in stages[3:]:
        bias = bias_step(bit)
    down, up, mixed = (chunk.rest() for chunk in (down, up, mixed))

    def finish(held):
        return functools.reduce(jnp.add, [array[:size] for array, _ in held])

    if fused:
        outs = [shape((3, size, local), F32), shape((size, local), F32)]
        block = pl.BlockSpec((size, 4 * local), lambda n: (0, 0))
        d_w_qkv, d_w_out = call(
            functools.partial(spread, local), "spread", 1, [array for array, _ in mixed],
            [block] * len(mixed), outs, full(*outs),
        )
    else:
        last = finish(mixed)
        d_w_qkv = last[:, : 3 * local].reshape(size, 3, local).transpose(1, 0, 2)
        d_w_out = last[:, 3 * local :]
    return (
        layer_out,
        d_tokens,
        d_w_qkv,
        bias[7, : 2 * local].reshape(2, local),
        d_w_out.T,
        bias[5, :width],
        bias[3, :width],
        bias[4, :width],
        finish(up),
        bias[6, :hidden],
        finish(down).T,
        bias[2, :width],
        bias[0, :width],
        bias[1, :width],
    )


def solution(mesh):
    placed = (
        P("dp", None), P("dp", None), P("dp"), P(None, None, "tp"), P(None, "tp"), P("tp", None),
        P(), P(), P(), P(None, "tp"), P("tp"), P("tp", None), P(), P(), P(), P("dp", None),
    )
    return jax.shard_map(
        on_device,
        mesh=mesh,
        in_specs=placed,
        out_specs=(
            P("dp", None), P("dp", None), P(None, "dp", "tp"), P(None, "tp"), P("tp", "dp"), P(), P(), P(),
            P("dp", "tp"), P("tp"), P("tp", "dp"), P(), P(), P(),
        ),
        check_vma=False,
    )
```

```python
import functools

import jax
import jax.numpy as jnp
from jax import lax
from jax.experimental import pallas as pl
from jax.experimental.pallas import tpu as pltpu
from jax.sharding import PartitionSpec as P

HEAD = 64
NEG_FILL = -1e30
EPS_NORM = 1e-12
LANES = 128
F32 = jnp.float32
LOW = jnp.bfloat16
MIB = 1 << 20


def dot(a, b):
    return lax.dot_general(a, b, (((1,), (0,)), ((), ())), preferred_element_type=F32)


def dot_nt(a, b):
    return lax.dot_general(a, b, (((1,), (1,)), ((), ())), preferred_element_type=F32)


def whole(shape):
    return pl.BlockSpec(shape, lambda *_: (0,) * len(shape))


def params(limit):
    return pltpu.CompilerParams(vmem_limit_bytes=limit * MIB)


def cost(flops):
    return pl.CostEstimate(flops=flops, bytes_accessed=10**6, transcendentals=0)


def key_mask(lengths_ref, pad_ref, rows):
    seqs = lengths_ref.shape[1]
    key_at = lax.broadcasted_iota(jnp.int32, (rows, LANES), 0)
    query_at = lax.broadcasted_iota(jnp.int32, (8, rows), 1)
    key_seg = jnp.zeros((rows, LANES), jnp.int32)
    query_seg = jnp.zeros((8, rows), jnp.int32)
    end = jnp.int32(0)
    for i in range(seqs):
        end = end + lengths_ref[0, i]
        key_seg = key_seg + (key_at >= end).astype(jnp.int32)
        query_seg = query_seg + (query_at >= end).astype(jnp.int32)
    pad = jnp.broadcast_to(pad_ref[...].astype(F32).reshape(1, rows), (LANES, rows)).T
    pieces = []
    for j in range(rows // LANES):
        span = slice(j * LANES, (j + 1) * LANES)
        same = key_seg == query_seg[0:1, span]
        usable = (pad == 1.0) | (key_at == query_at[0:1, span])
        pieces.append(jnp.where(same & usable, 0.0, NEG_FILL))
    return jnp.concatenate(pieces, 1)


def halves():
    lane = lax.broadcasted_iota(jnp.int32, (1, LANES), 1)
    left = (lane < HEAD).astype(F32)
    return left.astype(LOW), (1.0 - left).astype(LOW)


def fetch(sources, targets, sems):
    copies = [pltpu.make_async_copy(source, target, sems.at[i]) for i, (source, target) in enumerate(zip(sources, targets))]
    for copy in copies:
        copy.start()
    return copies


def attend(
    blocks, x_hbm, w_hbm, b_ref, lengths_ref, pad_ref, qkv_hbm, ctx_hbm, lse_ref, *rest
):
    wide_refs, (x_ref, w_ref, qkv_ref, ctx_ref, sems) = rest[:-5], rest[-5:]
    rows = x_ref.shape[0]
    local = w_ref.shape[2]
    scale = float(HEAD) ** (-0.5)
    came = fetch([x_hbm] + [w_hbm.at[i] for i in range(3)], [x_ref] + [w_ref.at[i] for i in range(3)], sems)
    bias = key_mask(lengths_ref, pad_ref, rows)
    sides = halves()
    came[0].wait()
    x = x_ref[...]
    came[1].wait()
    qkv_ref[:, 0:local] = ((dot(x, w_ref[0]) + b_ref[0:1, :].astype(F32)) * scale).astype(LOW)
    came[2].wait()
    qkv_ref[:, local : 2 * local] = dot(x, w_ref[1]).astype(LOW)
    came[3].wait()
    qkv_ref[:, 2 * local :] = (dot(x, w_ref[2]) + b_ref[1:2, :].astype(F32)).astype(LOW)
    saved = pltpu.make_async_copy(qkv_ref, qkv_hbm, sems.at[4])
    saved.start()
    for pair in range(local // LANES):
        at = pair * LANES
        span = slice(at, at + LANES)
        query = qkv_ref[:, span]
        keys = qkv_ref[:, local + at : local + at + LANES]
        flipped = qkv_ref[:, 2 * local + at : 2 * local + at + LANES].T
        parts = []
        for side in range(2):
            scores = dot_nt(keys * sides[side], query) + bias
            top = jnp.max(scores, 0, keepdims=True)
            expo = jnp.exp(scores - top)
            total = jnp.sum(expo, 0, keepdims=True)
            probs = (expo * (1.0 / total)).astype(LOW)
            parts.append(dot(flipped[side * HEAD : (side + 1) * HEAD], probs))
            head = 2 * pair + side
            lse_ref[head : head + 1, :] = top + jnp.log(total)
        context = jnp.concatenate(parts, 0).T.astype(LOW)
        ctx_ref[:, span] = context
        start = 0
        for wide_ref, size in zip(wide_refs, blocks):
            wide_ref[:, span] = context[start : start + size].astype(F32)
            start += size
    kept = pltpu.make_async_copy(ctx_ref, ctx_hbm, sems.at[5])
    kept.start()
    saved.wait()
    kept.wait()


def relay(in_ref, *refs):
    vectors = refs[:6]
    out_ref, vec_ref = refs[-2:]
    out_ref[...] = in_ref[...]
    vec_ref[...] = jnp.zeros(vec_ref.shape, F32)
    for i, ref in enumerate(vectors):
        vec_ref[i : i + 1, :] = ref[...].astype(F32).reshape(1, -1)


def norm_rows(value):
    centered = value - jnp.mean(value, -1, keepdims=True)
    inverse = lax.rsqrt(jnp.mean(centered * centered, -1, keepdims=True) + EPS_NORM)
    return centered * inverse, inverse


def norm_back(grad, normed, inverse, gain):
    scaled = grad * gain
    return inverse * (
        scaled
        - jnp.mean(scaled, -1, keepdims=True)
        - normed * jnp.mean(scaled * normed, -1, keepdims=True)
    )


def row(ref):
    return ref[...].astype(F32)


def feed(taken, tile, far_parts, place_ref, x_hbm, own_hbm, far_hbm, w_own_hbm, w_near_hbm, *refs):
    w_fars, refs = refs[:far_parts], refs[far_parts:]
    vec_ref, b_up_ref, w_up, w_down, normed_ref, inverse_ref, low_ref, act_ref, slope_ref, part_ref = refs[:10]
    x_ref, far_ref, w_far, w_full, ctx_full, sems = refs[10:]
    local = own_hbm.shape[1]
    half = w_near_hbm.shape[0]
    piece = half // far_parts
    hidden = w_up.shape[1]
    core, side = place_ref[0], place_ref[1]
    here = pl.multiple_of(side * local, LANES)
    there = pl.multiple_of((1 - side) * local, LANES)
    spans = [slice(at, at + tile) for at in range(0, hidden, tile)]
    sources = [w_own_hbm, own_hbm.at[taken], far_hbm, x_hbm.at[taken], w_near_hbm] + list(w_fars)
    targets = [w_full.at[pl.ds(here, local)], ctx_full.at[:, pl.ds(here, local)], far_ref, x_ref, w_far.at[0]]
    targets += [w_far.at[1, i * piece : (i + 1) * piece] for i in range(far_parts)]
    for copy in fetch(sources, targets, sems):
        copy.wait()
    for i in range(2):
        at = pl.multiple_of(there + (core ^ i) * half, 16)
        w_full[pl.ds(at, half), :] = w_far[i].astype(LOW)
    ctx_full[:, pl.ds(there, local)] = far_ref[...].astype(LOW)
    attn = dot(ctx_full[...], w_full[...])
    normed, inverse = norm_rows(x_ref[...].astype(F32) + attn + vec_ref[0:1, :])
    normed_ref[...] = normed
    inverse_ref[...] = jnp.broadcast_to(inverse, inverse_ref.shape)
    low = (normed * vec_ref[1:2, :] + vec_ref[2:3, :]).astype(LOW)
    low_ref[...] = low
    b_up = b_up_ref[...].astype(F32).reshape(1, -1)
    for i, span in enumerate(spans):
        pre = dot(low, w_up[:, span]) + b_up[:, span]
        share = 0.5 * (1.0 + lax.erf(pre * 0.7071067811865476))
        act = (pre * share).astype(LOW)
        act_ref[:, span] = act
        slope_ref[:, span] = share + pre * jnp.exp(-0.5 * pre * pre) * 0.3989422804014327
        added = dot(act, w_down[span, :])
        if i == 0:
            part_ref[...] = added
        else:
            part_ref[...] += added


def feed_back(
    taken, tile, own_ref, far_ref, normed_ref, vec_ref, slope_ref, up_hbm, w_up, w_down,
    out_ref, grad_ref, low_ref, pre_ref, part_ref, sums_ref, b_up_ref,
    up_ref, sems,
):
    hidden = w_up.shape[1]
    spans = [slice(at, at + tile) for at in range(0, hidden, tile)]
    came = fetch([up_hbm.at[taken]], [up_ref], sems)
    hidden_rows = normed_ref[...] * vec_ref[1:2, :] + vec_ref[2:3, :]
    normed, inverse = norm_rows(hidden_rows + (own_ref[...] + far_ref[...]) + vec_ref[3:4, :])
    gain = vec_ref[4:5, :]
    out_ref[...] = (normed * gain + vec_ref[5:6, :]).astype(LOW)
    came[0].wait()
    upstream = up_ref[...].astype(F32)
    grad = norm_back(upstream, normed, inverse, gain)
    grad_ref[...] = grad
    low = grad.astype(LOW)
    low_ref[...] = low
    sums_ref[0:1, :] = jnp.sum(upstream * normed, 0, keepdims=True)
    sums_ref[1:2, :] = jnp.sum(upstream, 0, keepdims=True)
    sums_ref[2:3, :] = jnp.sum(grad, 0, keepdims=True)
    sums_ref[3:8, :] = jnp.zeros((5, sums_ref.shape[1]), F32)
    for i, span in enumerate(spans):
        pre = (dot_nt(low, w_down[span, :]) * slope_ref[:, span]).astype(LOW)
        pre_ref[:, span] = pre
        b_up_ref[:, span] = jnp.broadcast_to(jnp.sum(pre.astype(F32), 0, keepdims=True), (8, tile))
        added = dot_nt(pre, w_up[:, span])
        if i == 0:
            part_ref[...] = added
        else:
            part_ref[...] += added


def norm_one_back(own_dr2, own_ref, far_ref, normed_ref, inverse_ref, sums_ref, b_up_ref, vec_ref, *refs):
    before, (dr1_ref, low_ref, bias_ref) = refs[:-3], refs[-3:]
    width = dr1_ref.shape[1]
    grad = own_dr2[...] + (own_ref[...] + far_ref[...])
    norm = normed_ref[...]
    dr1 = norm_back(grad, norm, inverse_ref[:, 0:1], vec_ref[1:2, :])
    dr1_ref[...] = dr1
    low_ref[...] = dr1.astype(LOW)
    bias_ref[...] = before[0][...] if before else jnp.zeros(bias_ref.shape, F32)
    bias_ref[0:3, 0:width] += sums_ref[0:3]
    for i, value in enumerate((grad * norm, grad, dr1)):
        bias_ref[3 + i : 4 + i, 0:width] += jnp.sum(value, 0, keepdims=True)
    bias_ref[6:7, 0 : b_up_ref.shape[1]] += b_up_ref[0:1, :]


def attend_back(
    count, *refs,
):
    attend_back_body(refs[:count], *refs[count:])


def attend_back_body(
    low_refs, w_hbm, qkv_hbm, ctx_hbm, lse_ref, lengths_ref, pad_ref, so_far_ref, e_ref, bias_ref,
    w_ref, qkv_ref, sems,
):
    rows, local = ctx_hbm.shape
    came = fetch([w_hbm, qkv_hbm, ctx_hbm], [w_ref, qkv_ref, e_ref.at[:, 3 * local : 4 * local]], sems)
    scale = float(HEAD) ** (-0.5)
    bias_ref[...] = so_far_ref[...]
    mask = key_mask(lengths_ref, pad_ref, rows)
    sides = halves()
    came[0].wait()
    d_ctx = dot_nt(jnp.concatenate([ref[...] for ref in low_refs], 0), w_ref[...]).astype(LOW)
    came[1].wait()
    for pair in range(local // LANES):
        at = pair * LANES
        span = slice(at, at + LANES)
        query = qkv_ref[:, span]
        keys = qkv_ref[:, local + at : local + at + LANES]
        values = qkv_ref[:, 2 * local + at : 2 * local + at + LANES]
        grads = d_ctx[:, span]
        flipped = keys.T
        d_q = []
        d_k = jnp.zeros((rows, LANES), F32)
        d_v = jnp.zeros((rows, LANES), F32)
        for side in range(2):
            head = 2 * pair + side
            scores = dot_nt(keys * sides[side], query) + mask
            probs = jnp.exp(scores - lse_ref[head : head + 1, :])
            d_p = dot_nt(values * sides[side], grads)
            mixed = jnp.sum(probs * d_p, 0, keepdims=True)
            d_s = (probs * (d_p - mixed)).astype(LOW)
            d_k = d_k + dot(d_s, query * sides[side])
            d_v = d_v + dot(probs.astype(LOW), grads * sides[side])
            d_q.append(dot(flipped[side * HEAD : (side + 1) * HEAD], d_s))
        d_query = jnp.concatenate(d_q, 0).T.astype(LOW).astype(F32) * scale
        d_k = d_k.astype(LOW)
        d_v = d_v.astype(LOW)
        e_ref[:, at : at + LANES] = d_query.astype(LOW)
        e_ref[:, local + at : local + at + LANES] = d_k
        e_ref[:, 2 * local + at : 2 * local + at + LANES] = d_v
        bias_ref[7:8, at : at + LANES] = jnp.sum(d_query, 0, keepdims=True)
        bias_ref[7:8, local + at : local + at + LANES] = jnp.sum(d_v.astype(F32), 0, keepdims=True)
    came[2].wait()


def place_blocks(me, source, target, order, size):
    for i, block in enumerate(order):
        at = pl.multiple_of((me ^ block) * size, size)
        target[i * size : (i + 1) * size, :] = source[pl.ds(at, size), :]


def outer(order, size, splits, kinds, more, place_ref, *refs):
    count = len(splits)
    sides = max(kinds) + 1
    lefts = [refs[:count]] + ([refs[count : count + more]] if more else [])
    rights = refs[count + more : 2 * count + more]
    *sent_refs, keep_ref, flipped, placed = refs[2 * count + more :]
    step = pl.program_id(0)

    @pl.when(step == 0)
    def _():
        for index, group in enumerate(lefts):
            source = jnp.concatenate([ref[...] for ref in group], 0).T
            if order is None:
                placed[index] = source
            else:
                flipped[...] = source
                place_blocks(place_ref[2], flipped, placed.at[index], order, size)

    left = placed[0]
    if sides > 1:
        change = kinds.index(1)
        left = placed[jnp.where(step >= change, 1, 0)]
    right = jnp.concatenate([ref[...] for ref in rights], 0)
    half = keep_ref.shape[0]
    part = half // len(sent_refs)
    for i, ref in enumerate(sent_refs):
        ref[...] = dot(left[i * part : (i + 1) * part], right)
    keep_ref[...] = dot(left[half:], right)


def fold(*refs):
    value = refs[0][...]
    for ref in refs[1:-1]:
        value = value + ref[...]
    refs[-1][...] = value


def fold_blocks(size, counts, *refs):
    out_ref = refs[-1]
    at = 0
    for i, count in enumerate(counts):
        value = refs[at][...]
        for ref in refs[at + 1 : at + count]:
            value = value + ref[...]
        out_ref[i * size : (i + 1) * size, :] = value
        at += count


def back_tokens(e_ref, w_hbm, out_ref, w_ref, sems):
    local = w_ref.shape[2]
    came = fetch([w_hbm.at[i] for i in range(3)], [w_ref.at[i] for i in range(3)], sems)
    for i in range(3):
        came[i].wait()
        added = dot_nt(e_ref[:, i * local : (i + 1) * local], w_ref[i])
        if i == 0:
            out_ref[...] = added
        else:
            out_ref[...] += added


def join(own_ref, far_ref, *refs):
    out_ref, start = refs[-1], 0
    for ref in refs[:-1]:
        span = slice(start, start + ref.shape[0])
        out_ref[span, :] = ref[...] + (own_ref[span, :] + far_ref[span, :])
        start += ref.shape[0]


def spread(local, *refs):
    count = len(refs) - 4
    parts, (qkv_ref, out_ref) = refs[:count], refs[count : count + 2]
    held, sems = refs[-2:]
    size = out_ref.shape[0]
    came = fetch([part.at[0:size] for part in parts], [held.at[i] for i in range(count)], sems)
    for copy in came:
        copy.wait()
    value = held[0]
    for i in range(1, count):
        value = value + held[i]
    for i in range(3):
        qkv_ref[i] = value[:, i * local : (i + 1) * local]
    out_ref[...] = value[:, 3 * local :]


def chained(kernel, inputs, outputs):
    def body(*refs):
        refs[1 + inputs + outputs][...] = jnp.zeros((8, LANES), F32)
        kernel(*refs[1 : 1 + inputs + outputs], *refs[2 + inputs + outputs :])

    return body


def on_device(
    tokens, lengths, pad_mask, w_qkv, b_qv, w_out, b_out, ln1_gain, ln1_bias,
    w_up, b_up, w_down, b_down, ln2_gain, ln2_bias, cotangent,
):
    rows, width = tokens.shape
    local = w_qkv.shape[2]
    heads = local // HEAD
    hidden = w_up.shape[1]
    ranks = lax.axis_size("dp")
    me = lax.axis_index("dp").astype(jnp.int32)
    place_arr = jnp.stack([me % 2, lax.axis_index("tp").astype(jnp.int32), me])
    size = width // ranks
    blocks = [rows // 2] * 2 if rows % 32 == 0 else [rows]
    starts = [sum(blocks[:i]) for i in range(len(blocks))]
    lse_rows = -(-heads // 8) * 8
    shape = jax.ShapeDtypeStruct
    smem = pl.BlockSpec(memory_space=pltpu.SMEM)
    loose = pl.BlockSpec(memory_space=pl.ANY)
    far_off = pl.BlockSpec(memory_space=pltpu.HBM)
    dma = pltpu.SemaphoreType.DMA
    mark = [None]

    def call(kernel, name, operands, in_specs, out_shape, out_specs, grid=(1,), scratch=(), limit=24, flops=10**10):
        before = mark[0] if mark[0] is not None else operands[0]
        *outs, mark[0] = pl.pallas_call(
            chained(kernel, len(operands), len(out_shape)),
            grid=grid,
            out_shape=tuple(out_shape) + (shape((8, LANES), F32),),
            in_specs=[loose] + list(in_specs),
            out_specs=tuple(out_specs) + (whole((8, LANES)),),
            scratch_shapes=list(scratch),
            compiler_params=params(limit),
            cost_estimate=cost(flops),
            name=name,
        )(before, *operands)
        return outs

    def full(*arrays):
        return [whole(array.shape) for array in arrays]

    def swap_tp(array):
        pairs = [(i, i ^ 1) for i in range(lax.axis_size("tp"))]
        return lax.ppermute(array, "tp", pairs)

    def swap_dp(array, bits):
        return lax.ppermute(array, "dp", [(i, i ^ bits) for i in range(ranks)])

    stages = []
    while 1 << len(stages) < ranks:
        stages.append(1 << len(stages))
    order = [0]
    for bit in reversed(stages):
        order = order + [bit + rest for rest in order]
    order = order[ranks // 2 :] + order[: ranks // 2]
    fused = size % 16 == 0
    pad_row = pad_mask
    half = w_out.shape[0] // 2
    w_near = swap_tp(lax.dynamic_slice_in_dim(w_out, (me % 2) * half, half, 0).astype(F32))
    outs = [shape((rows, 3 * local), LOW), shape((rows, local), LOW), shape((lse_rows, rows), F32)]
    outs += [shape((block, local), F32) for block in blocks]
    qkv, context, lse, *wides = call(
        functools.partial(attend, blocks), "attend", [tokens, w_qkv, b_qv, lengths, pad_row],
        [far_off] * 2 + full(b_qv) + [smem] + full(pad_row), outs, [far_off] * 2 + full(*outs[2:]),
        scratch=[
            pltpu.VMEM((rows, width), LOW),
            pltpu.VMEM((3, width, local), LOW),
            pltpu.VMEM((rows, 3 * local), LOW),
            pltpu.VMEM((rows, local), LOW),
            dma((6,)),
        ],
        limit=56,
    )
    fars = [swap_tp(wide) for wide in wides]
    near = pl.BlockSpec(memory_space=pltpu.VMEM)
    params_of = [b_out, ln1_gain, ln1_bias, b_down, ln2_gain, ln2_bias]
    outs = [shape(w_near.shape, F32), shape((8, width), F32)]
    w_near, vectors = call(
        relay, "relay", [w_near, *params_of, w_up, w_down],
        full(w_near, *params_of) + [near, near], outs, full(*outs),
    )
    far_parts = 3 if half % 48 == 0 else 1
    piece = half // far_parts
    w_fars = [swap_dp(w_near[i * piece : (i + 1) * piece], 1) for i in range(far_parts)]

    tile = min(hidden, 512)
    tiles = hidden // tile

    def columns(height, step):
        return pl.BlockSpec((height, step), lambda f: (0, f))

    saved = []
    for begin, block, far in zip(starts, blocks, fars):
        outs = [
            shape((block, width), F32), shape((block, LANES), F32), shape((block, width), LOW),
            shape((block, hidden), LOW), shape((block, hidden), F32), shape((block, width), F32),
        ]
        outs = call(
            functools.partial(feed, slice(begin, begin + block), tile, far_parts), "feed",
            [place_arr, tokens, context, far, w_out, w_near, *w_fars, vectors, b_up, w_up, w_down],
            [smem] + [far_off] * (5 + far_parts) + full(vectors, b_up) + [near] * 2,
            outs, full(*outs),
            scratch=[
                pltpu.VMEM((block, width), LOW),
                pltpu.VMEM((block, local), F32),
                pltpu.VMEM((2, half, width), F32),
                pltpu.VMEM((2 * local, width), LOW),
                pltpu.VMEM((block, 2 * local), LOW),
                dma((5 + far_parts,)),
            ],
        )
        saved.append(outs + [swap_tp(outs[5])])

    back = []
    for begin, block, (normed, inverse, low, act, slope, own, far) in zip(starts, blocks, saved):
        outs = [
            shape((block, width), LOW), shape((block, width), F32), shape((block, width), LOW),
            shape((block, hidden), LOW), shape((block, width), F32), shape((8, width), F32), shape((8, hidden), F32),
        ]
        outs = call(
            functools.partial(feed_back, slice(begin, begin + block), tile), "feed_back",
            [own, far, normed, vectors, slope, cotangent, w_up, w_down],
            full(own, far, normed, vectors, slope) + [far_off] + [near] * 2,
            outs, full(*outs),
            scratch=[pltpu.VMEM((block, width), LOW), dma((1,))],
        )
        back.append(outs + [swap_tp(outs[4])])

    layer_out = jnp.concatenate([outs[0] for outs in back], 0)

    def gradient(lefts, rights, splits, kinds, step, parts):
        wide = step * len(kinds)
        sides = max(kinds) + 1
        outs = [shape((width // 2 // parts, wide), F32)] * parts + [shape((width // 2, wide), F32)]
        outs = call(
            functools.partial(outer, order if fused else None, size, splits, kinds, len(lefts) - len(splits)), "outer",
            [place_arr, *lefts, *rights],
            [smem] + full(*lefts) + [columns(split, step) for split in splits],
            outs, [columns(out.shape[0], step) for out in outs],
            grid=(len(kinds),),
            scratch=[pltpu.VMEM((width, rows), LOW), pltpu.VMEM((sides, width, rows), LOW)],
        )
        if not fused:
            every = jnp.concatenate(outs, 0).reshape(ranks, size, wide)
            every = jnp.take(every, jnp.array(order, jnp.int32) ^ me, axis=0).reshape(width, wide)
            outs = [every[: width // 2], every[width // 2 :]]
        return outs

    def pick(held, begin, end):
        return [(array, first) for array, first in held if first <= begin and end <= first + array.shape[0]]

    def add(held, begin, end):
        wide = held[0][0].shape[1]
        if not fused:
            parts = []
            for row in range(begin, end, size):
                parts.append(functools.reduce(jnp.add, [a[row - f : row - f + size] for a, f in pick(held, row, row + size)]))
            return jnp.concatenate(parts, 0)
        operands, specs, counts = [], [], []
        for row in range(begin, end, size):
            inside = pick(held, row, row + size)
            counts.append(len(inside))
            for array, first in inside:
                operands.append(array)
                specs.append(pl.BlockSpec((size, wide), functools.partial(lambda index, n: (index, 0), (row - first) // size)))
        outs = [shape((end - begin, wide), F32)]
        return call(functools.partial(fold_blocks, size, counts), "fold", operands, specs, outs, full(*outs))[0]

    class Chunk:
        def __init__(self, outs):
            self.held, first = [(outs[-1], 0)], 0
            for out in outs[:-1]:
                self.held.append((swap_dp(out, stages[0]), first))
                first += out.shape[0]
            self.stage = 0

        def step(self):
            self.stage += 1
            half = width // (4 << (self.stage - 1))
            out = add(self.held, half, 2 * half)
            self.held = self.held + [(swap_dp(out, stages[self.stage]), 0)]

        def high(self):
            self.stage += 1
            half = self.half = width // (4 << (self.stage - 1))
            if half == size:
                self.stage -= 1
                self.step()
            else:
                out = add(self.held, half + half // 2, 2 * half)
                self.came = [(swap_dp(out, stages[self.stage]), half // 2)]

        def low(self):
            out = add(self.held, self.half, self.half + self.half // 2)
            self.held = self.held + self.came + [(swap_dp(out, stages[self.stage]), 0)]

        def last(self):
            self.rest()
            return add(self.held, 0, size)

        def rest(self):
            while self.stage < len(stages) - 1:
                self.step()
            return [(array, first) for array, first in self.held if first == 0]

    down = Chunk(gradient([o[2] for o in back], [s[3] for s in saved], blocks, [0] * tiles, tile, 1))
    wide = max(width, hidden, 2 * local)

    def first_norm(i):
        outs = [shape((blocks[i], width), F32), shape((blocks[i], width), LOW), shape((8, wide), F32)]
        operands = [back[i][1], back[i][4], back[i][7], saved[i][0], saved[i][1], back[i][5], back[i][6], vectors]
        operands += [norms[-1][2]] if norms else []
        norms.append(call(norm_one_back, "norm_one_back", operands, full(*operands), outs, full(*outs), flops=2 * 10**10 if i == 0 else 10**10))

    norms = []
    first_norm(0)
    down.step()
    first_norm(1)
    up = Chunk(gradient([s[2] for s in saved], [o[3] for o in back], blocks, [0] * tiles, tile, 1))
    dr1s, lows = [n[0] for n in norms], [n[1] for n in norms]
    outs = [shape((rows, 4 * local), LOW), shape((8, wide), F32)]
    operands = lows + [w_out, qkv, context, lse, lengths, pad_row, norms[-1][2]]
    e, bias = call(
        functools.partial(attend_back, len(lows)), "attend_back", operands,
        full(*lows) + [far_off] * 3 + full(lse) + [smem] + full(pad_row, norms[-1][2]), outs, full(*outs),
        scratch=[pltpu.VMEM((local, width), LOW), pltpu.VMEM((rows, 3 * local), LOW), dma((3,))],
    )
    mixed = Chunk(gradient([tokens] + lows, [e], [rows], [0, 0, 0, 1], local, 2))

    def bias_step(bit):
        far = swap_dp(bias, bit)
        return call(fold, "fold", [bias, far], full(bias, far), [shape(bias.shape, F32)], full(bias))[0]

    down.step()
    up.step()
    outs = [shape((rows, width), F32)]
    (partial,) = call(
        back_tokens, "back_tokens", [e, w_qkv], full(e) + [far_off], outs, full(*outs),
        scratch=[pltpu.VMEM((3, width, local), LOW), dma((3,))],
    )
    partial_far = swap_tp(partial)
    down.step()
    up.step()
    mixed.high()
    mixed.low()
    bias = bias_step(stages[0])
    down = down.last()
    up.step()
    mixed.high()
    mixed.low()
    bias = bias_step(stages[1])
    up = up.last()
    mixed.high()
    bias = bias_step(stages[2])
    mixed = mixed.rest()
    for bit in stages[3:]:
        bias = bias_step(bit)
    (d_tokens,) = call(
        join, "join", [partial, partial_far] + dr1s, full(partial, partial_far, *dr1s), outs, full(*outs)
    )

    def finish(held):
        return functools.reduce(jnp.add, [array[:size] for array, _ in held])

    if fused:
        outs = [shape((3, size, local), F32), shape((size, local), F32)]
        d_w_qkv, d_w_out = call(
            functools.partial(spread, local), "spread", [array for array, _ in mixed],
            [far_off] * len(mixed), outs, full(*outs),
            scratch=[pltpu.VMEM((len(mixed), size, 4 * local), F32), dma((len(mixed),))],
        )
    else:
        last = finish(mixed)
        d_w_qkv = last[:, : 3 * local].reshape(size, 3, local).transpose(1, 0, 2)
        d_w_out = last[:, 3 * local :]
    return (
        layer_out,
        d_tokens,
        d_w_qkv,
        bias[7, : 2 * local].reshape(2, local),
        d_w_out.T,
        bias[5, :width],
        bias[3, :width],
        bias[4, :width],
        up,
        bias[6, :hidden],
        down.T,
        bias[2, :width],
        bias[0, :width],
        bias[1, :width],
    )


def solution(mesh):
    placed = (
        P("dp", None), P("dp", None), P("dp"), P(None, None, "tp"), P(None, "tp"), P("tp", None),
        P(), P(), P(), P(None, "tp"), P("tp"), P("tp", None), P(), P(), P(), P("dp", None),
    )
    return jax.shard_map(
        on_device,
        mesh=mesh,
        in_specs=placed,
        out_specs=(
            P("dp", None), P("dp", None), P(None, "dp", "tp"), P(None, "tp"), P("tp", "dp"), P(), P(), P(),
            P("dp", "tp"), P("tp"), P("tp", "dp"), P(), P(), P(),
        ),
        check_vma=False,
    )
```

```python
import functools

import jax
import jax.numpy as jnp
from jax import lax
from jax.experimental import pallas as pl
from jax.experimental.pallas import tpu as pltpu
from jax.sharding import PartitionSpec as P

HEAD = 64
NEG_FILL = -1e30
EPS_NORM = 1e-12
LANES = 128
F32 = jnp.float32
LOW = jnp.bfloat16
MIB = 1 << 20


def dot(a, b):
    return lax.dot_general(a, b, (((1,), (0,)), ((), ())), preferred_element_type=F32)


def dot_nt(a, b):
    return lax.dot_general(a, b, (((1,), (1,)), ((), ())), preferred_element_type=F32)


def whole(shape):
    return pl.BlockSpec(shape, lambda *_: (0,) * len(shape))


def params(limit):
    return pltpu.CompilerParams(vmem_limit_bytes=limit * MIB)


def cost(flops):
    return pl.CostEstimate(flops=flops, bytes_accessed=10**6, transcendentals=0)


def key_mask(lengths_ref, pad_ref, rows):
    seqs = lengths_ref.shape[1]
    key_at = lax.broadcasted_iota(jnp.int32, (rows, LANES), 0)
    query_at = lax.broadcasted_iota(jnp.int32, (8, rows), 1)
    key_seg = jnp.zeros((rows, LANES), jnp.int32)
    query_seg = jnp.zeros((8, rows), jnp.int32)
    end = jnp.int32(0)
    for i in range(seqs):
        end = end + lengths_ref[0, i]
        key_seg = key_seg + (key_at >= end).astype(jnp.int32)
        query_seg = query_seg + (query_at >= end).astype(jnp.int32)
    pad = jnp.broadcast_to(pad_ref[...].astype(F32).reshape(1, rows), (LANES, rows)).T
    pieces = []
    for j in range(rows // LANES):
        span = slice(j * LANES, (j + 1) * LANES)
        same = key_seg == query_seg[0:1, span]
        usable = (pad == 1.0) | (key_at == query_at[0:1, span])
        pieces.append(jnp.where(same & usable, 0.0, NEG_FILL))
    return jnp.concatenate(pieces, 1)


def halves():
    lane = lax.broadcasted_iota(jnp.int32, (1, LANES), 1)
    left = (lane < HEAD).astype(F32)
    return left.astype(LOW), (1.0 - left).astype(LOW)


def fetch(sources, targets, sems):
    copies = [pltpu.make_async_copy(source, target, sems.at[i]) for i, (source, target) in enumerate(zip(sources, targets))]
    for copy in copies:
        copy.start()
    return copies


def attend(
    blocks, x_hbm, w_hbm, b_ref, lengths_ref, pad_ref, qkv_hbm, ctx_hbm, lse_ref, *rest
):
    wide_refs, (x_ref, w_ref, qkv_ref, ctx_ref, sems) = rest[:-5], rest[-5:]
    rows = x_ref.shape[0]
    local = w_ref.shape[2]
    scale = float(HEAD) ** (-0.5)
    came = fetch([x_hbm] + [w_hbm.at[i] for i in range(3)], [x_ref] + [w_ref.at[i] for i in range(3)], sems)
    bias = key_mask(lengths_ref, pad_ref, rows)
    sides = halves()
    came[0].wait()
    x = x_ref[...]
    came[1].wait()
    qkv_ref[:, 0:local] = ((dot(x, w_ref[0]) + b_ref[0:1, :].astype(F32)) * scale).astype(LOW)
    came[2].wait()
    qkv_ref[:, local : 2 * local] = dot(x, w_ref[1]).astype(LOW)
    came[3].wait()
    qkv_ref[:, 2 * local :] = (dot(x, w_ref[2]) + b_ref[1:2, :].astype(F32)).astype(LOW)
    saved = pltpu.make_async_copy(qkv_ref, qkv_hbm, sems.at[4])
    saved.start()
    for pair in range(local // LANES):
        at = pair * LANES
        span = slice(at, at + LANES)
        query = qkv_ref[:, span]
        keys = qkv_ref[:, local + at : local + at + LANES]
        flipped = qkv_ref[:, 2 * local + at : 2 * local + at + LANES].T
        parts = []
        for side in range(2):
            scores = dot_nt(keys * sides[side], query) + bias
            top = jnp.max(scores, 0, keepdims=True)
            expo = jnp.exp(scores - top)
            total = jnp.sum(expo, 0, keepdims=True)
            probs = (expo * (1.0 / total)).astype(LOW)
            parts.append(dot(flipped[side * HEAD : (side + 1) * HEAD], probs))
            head = 2 * pair + side
            lse_ref[head : head + 1, :] = top + jnp.log(total)
        context = jnp.concatenate(parts, 0).T.astype(LOW)
        ctx_ref[:, span] = context
        start = 0
        for wide_ref, size in zip(wide_refs, blocks):
            wide_ref[:, span] = context[start : start + size].astype(F32)
            start += size
    kept = pltpu.make_async_copy(ctx_ref, ctx_hbm, sems.at[5])
    kept.start()
    saved.wait()
    kept.wait()


def relay(in_ref, *refs):
    vectors = refs[:6]
    out_ref, vec_ref = refs[-2:]
    out_ref[...] = in_ref[...]
    vec_ref[...] = jnp.zeros(vec_ref.shape, F32)
    for i, ref in enumerate(vectors):
        vec_ref[i : i + 1, :] = ref[...].astype(F32).reshape(1, -1)


def norm_rows(value):
    centered = value - jnp.mean(value, -1, keepdims=True)
    inverse = lax.rsqrt(jnp.mean(centered * centered, -1, keepdims=True) + EPS_NORM)
    return centered * inverse, inverse


def norm_back(grad, normed, inverse, gain):
    scaled = grad * gain
    return inverse * (
        scaled
        - jnp.mean(scaled, -1, keepdims=True)
        - normed * jnp.mean(scaled * normed, -1, keepdims=True)
    )


def row(ref):
    return ref[...].astype(F32)


def feed(taken, tile, far_parts, streamed, place_ref, x_hbm, own_hbm, far_hbm, w_own_hbm, w_near_hbm, *refs):
    w_fars, refs = refs[:far_parts], refs[far_parts:]
    vec_hbm, b_up_ref, w_up, w_down, normed_ref, inverse_ref, low_ref, act_ref, slope_ref, part_ref = refs[:10]
    x_ref, far_ref, vec_ref, w_far, w_full, ctx_full, sems = refs[10:17]
    local = own_hbm.shape[1]
    half = w_near_hbm.shape[0]
    piece = half // far_parts
    hidden = w_up.shape[1]
    core, side = place_ref[0], place_ref[1]
    here = pl.multiple_of(side * local, LANES)
    there = pl.multiple_of((1 - side) * local, LANES)
    spans = [slice(at, at + tile) for at in range(0, hidden, tile)]
    sources = [w_near_hbm] + list(w_fars) + [w_own_hbm, own_hbm.at[taken], far_hbm, x_hbm.at[taken], vec_hbm]
    targets = [w_far.at[0]] + [w_far.at[1, i * piece : (i + 1) * piece] for i in range(far_parts)]
    targets += [w_full.at[pl.ds(here, local)], ctx_full.at[:, pl.ds(here, local)], far_ref, x_ref, vec_ref]
    needed = len(sources)
    if streamed:
        w_up_vmem, w_down_vmem = refs[17:]
        for span in spans:
            sources += [w_up.at[:, span], w_down.at[span]]
            targets += [w_up_vmem.at[:, span], w_down_vmem.at[span]]
        w_up, w_down = w_up_vmem, w_down_vmem
    came = fetch(sources, targets, sems)
    for copy in came[:needed]:
        copy.wait()
    for i in range(2):
        at = pl.multiple_of(there + (core ^ i) * half, 16)
        w_full[pl.ds(at, half), :] = w_far[i].astype(LOW)
    ctx_full[:, pl.ds(there, local)] = far_ref[...].astype(LOW)
    attn = dot(ctx_full[...], w_full[...])
    normed, inverse = norm_rows(x_ref[...].astype(F32) + attn + vec_ref[0:1, :])
    normed_ref[...] = normed
    inverse_ref[...] = jnp.broadcast_to(inverse, inverse_ref.shape)
    low = (normed * vec_ref[1:2, :] + vec_ref[2:3, :]).astype(LOW)
    low_ref[...] = low
    b_up = b_up_ref[...].astype(F32).reshape(1, -1)
    for i, span in enumerate(spans):
        if streamed:
            came[needed + 2 * i].wait()
        pre = dot(low, w_up[:, span]) + b_up[:, span]
        share = 0.5 * (1.0 + lax.erf(pre * 0.7071067811865476))
        act = (pre * share).astype(LOW)
        act_ref[:, span] = act
        slope_ref[:, span] = share + pre * jnp.exp(-0.5 * pre * pre) * 0.3989422804014327
        if streamed:
            came[needed + 2 * i + 1].wait()
        added = dot(act, w_down[span, :])
        if i == 0:
            part_ref[...] = added
        else:
            part_ref[...] += added


def feed_back(
    taken, tile, own_ref, far_ref, normed_ref, slope_ref, vec_hbm, up_hbm, w_up, w_down,
    out_ref, grad_ref, low_ref, pre_ref, part_ref, sums_ref, b_up_ref,
    vec_ref, up_ref, sems,
):
    hidden = w_up.shape[1]
    spans = [slice(at, at + tile) for at in range(0, hidden, tile)]
    came = fetch([up_hbm.at[taken], vec_hbm], [up_ref, vec_ref], sems)
    came[1].wait()
    hidden_rows = normed_ref[...] * vec_ref[1:2, :] + vec_ref[2:3, :]
    normed, inverse = norm_rows(hidden_rows + (own_ref[...] + far_ref[...]) + vec_ref[3:4, :])
    gain = vec_ref[4:5, :]
    out_ref[...] = (normed * gain + vec_ref[5:6, :]).astype(LOW)
    came[0].wait()
    upstream = up_ref[...].astype(F32)
    grad = norm_back(upstream, normed, inverse, gain)
    grad_ref[...] = grad
    low = grad.astype(LOW)
    low_ref[...] = low
    sums_ref[0:1, :] = jnp.sum(upstream * normed, 0, keepdims=True)
    sums_ref[1:2, :] = jnp.sum(upstream, 0, keepdims=True)
    sums_ref[2:3, :] = jnp.sum(grad, 0, keepdims=True)
    sums_ref[3:8, :] = jnp.zeros((5, sums_ref.shape[1]), F32)
    for i, span in enumerate(spans):
        pre = (dot_nt(low, w_down[span, :]) * slope_ref[:, span]).astype(LOW)
        pre_ref[:, span] = pre
        b_up_ref[:, span] = jnp.broadcast_to(jnp.sum(pre.astype(F32), 0, keepdims=True), (8, tile))
        added = dot_nt(pre, w_up[:, span])
        if i == 0:
            part_ref[...] = added
        else:
            part_ref[...] += added


def norm_one_back(own_dr2, own_ref, far_ref, normed_ref, inverse_ref, sums_ref, b_up_ref, vec_ref, *refs):
    before, (dr1_ref, low_ref, bias_ref) = refs[:-3], refs[-3:]
    width = dr1_ref.shape[1]
    grad = own_dr2[...] + (own_ref[...] + far_ref[...])
    norm = normed_ref[...]
    dr1 = norm_back(grad, norm, inverse_ref[:, 0:1], vec_ref[1:2, :])
    dr1_ref[...] = dr1
    low_ref[...] = dr1.astype(LOW)
    bias_ref[...] = before[0][...] if before else jnp.zeros(bias_ref.shape, F32)
    bias_ref[0:3, 0:width] += sums_ref[0:3]
    for i, value in enumerate((grad * norm, grad, dr1)):
        bias_ref[3 + i : 4 + i, 0:width] += jnp.sum(value, 0, keepdims=True)
    bias_ref[6:7, 0 : b_up_ref.shape[1]] += b_up_ref[0:1, :]


def attend_back(
    count, *refs,
):
    attend_back_body(refs[:count], *refs[count:])


def attend_back_body(
    low_refs, w_hbm, qkv_hbm, ctx_hbm, lse_ref, lengths_ref, pad_ref, so_far_ref, e_ref, bias_ref,
    w_ref, qkv_ref, sems,
):
    rows, local = ctx_hbm.shape
    came = fetch([w_hbm, qkv_hbm, ctx_hbm], [w_ref, qkv_ref, e_ref.at[:, 3 * local : 4 * local]], sems)
    scale = float(HEAD) ** (-0.5)
    bias_ref[...] = so_far_ref[...]
    mask = key_mask(lengths_ref, pad_ref, rows)
    sides = halves()
    came[0].wait()
    d_ctx = dot_nt(jnp.concatenate([ref[...] for ref in low_refs], 0), w_ref[...]).astype(LOW)
    came[1].wait()
    for pair in range(local // LANES):
        at = pair * LANES
        span = slice(at, at + LANES)
        query = qkv_ref[:, span]
        keys = qkv_ref[:, local + at : local + at + LANES]
        values = qkv_ref[:, 2 * local + at : 2 * local + at + LANES]
        grads = d_ctx[:, span]
        flipped = keys.T
        d_q = []
        d_k = jnp.zeros((rows, LANES), F32)
        d_v = jnp.zeros((rows, LANES), F32)
        for side in range(2):
            head = 2 * pair + side
            scores = dot_nt(keys * sides[side], query) + mask
            probs = jnp.exp(scores - lse_ref[head : head + 1, :])
            d_p = dot_nt(values * sides[side], grads)
            mixed = jnp.sum(probs * d_p, 0, keepdims=True)
            d_s = (probs * (d_p - mixed)).astype(LOW)
            d_k = d_k + dot(d_s, query * sides[side])
            d_v = d_v + dot(probs.astype(LOW), grads * sides[side])
            d_q.append(dot(flipped[side * HEAD : (side + 1) * HEAD], d_s))
        d_query = jnp.concatenate(d_q, 0).T.astype(LOW).astype(F32) * scale
        d_k = d_k.astype(LOW)
        d_v = d_v.astype(LOW)
        e_ref[:, at : at + LANES] = d_query.astype(LOW)
        e_ref[:, local + at : local + at + LANES] = d_k
        e_ref[:, 2 * local + at : 2 * local + at + LANES] = d_v
        bias_ref[7:8, at : at + LANES] = jnp.sum(d_query, 0, keepdims=True)
        bias_ref[7:8, local + at : local + at + LANES] = jnp.sum(d_v.astype(F32), 0, keepdims=True)
    came[2].wait()


def place_blocks(me, source, target, order, size):
    for i, block in enumerate(order):
        at = pl.multiple_of((me ^ block) * size, size)
        target[i * size : (i + 1) * size, :] = source[pl.ds(at, size), :]


def outer(order, size, splits, kinds, more, rides, place_ref, *refs):
    count = len(splits)
    sides = max(kinds) + 1
    lefts = [refs[:count]] + ([refs[count : count + more]] if more else [])
    rights = refs[count + more : 2 * count + more]
    rider = refs[2 * count + more] if rides else None
    *sent_refs, keep_ref, flipped, placed = refs[2 * count + more + rides :]
    step = pl.program_id(0)

    @pl.when(step == 0)
    def _():
        for index, group in enumerate(lefts):
            source = jnp.concatenate([ref[...] for ref in group], 0).T
            if order is None:
                placed[index] = source
            else:
                flipped[...] = source
                place_blocks(place_ref[2], flipped, placed.at[index], order, size)

    left = placed[0]
    if sides > 1:
        change = kinds.index(1)
        left = placed[jnp.where(step >= change, 1, 0)]
    right = jnp.concatenate([ref[...] for ref in rights], 0)
    half = left.shape[0] // 2
    part = half // len(sent_refs)
    for i, ref in enumerate(sent_refs):
        ref[0:part, :] = dot(left[i * part : (i + 1) * part], right)
    keep_ref[0:half, :] = dot(left[half:], right)
    if rides:
        sent_refs[-1][part:, :] = rider[...]
        keep_ref[half:, :] = rider[...]


def fold(*refs):
    value = refs[0][...]
    for ref in refs[1:-1]:
        value = value + ref[...]
    refs[-1][...] = value


def fold_blocks(counts, *refs):
    out_ref = refs[-1]
    at = start = 0
    for count in counts:
        value = refs[at][...]
        for ref in refs[at + 1 : at + count]:
            value = value + ref[...]
        end = start + value.shape[0]
        out_ref[start:end, :] = value
        at += count
        start = end


def back_tokens(e_ref, w_hbm, out_ref, w_ref, sems):
    local = w_ref.shape[2]
    came = fetch([w_hbm.at[i] for i in range(3)], [w_ref.at[i] for i in range(3)], sems)
    for i in range(3):
        came[i].wait()
        added = dot_nt(e_ref[:, i * local : (i + 1) * local], w_ref[i])
        if i == 0:
            out_ref[...] = added
        else:
            out_ref[...] += added


def join(own_ref, far_ref, *refs):
    out_ref, start = refs[-1], 0
    for ref in refs[:-1]:
        span = slice(start, start + ref.shape[0])
        out_ref[span, :] = ref[...] + (own_ref[span, :] + far_ref[span, :])
        start += ref.shape[0]


def spread(local, *refs):
    qkv_ref, out_ref = refs[-2:]
    value = refs[0][...]
    for ref in refs[1:-2]:
        value = value + ref[...]
    for i in range(3):
        qkv_ref[i] = value[:, i * local : (i + 1) * local]
    out_ref[...] = value[:, 3 * local :]


def chained(kernel, inputs, outputs):
    def body(*refs):
        refs[1 + inputs + outputs][...] = jnp.zeros((8, LANES), F32)
        kernel(*refs[1 : 1 + inputs + outputs], *refs[2 + inputs + outputs :])

    return body


def on_device(
    tokens, lengths, pad_mask, w_qkv, b_qv, w_out, b_out, ln1_gain, ln1_bias,
    w_up, b_up, w_down, b_down, ln2_gain, ln2_bias, cotangent,
):
    rows, width = tokens.shape
    local = w_qkv.shape[2]
    heads = local // HEAD
    hidden = w_up.shape[1]
    ranks = lax.axis_size("dp")
    me = lax.axis_index("dp").astype(jnp.int32)
    place_arr = jnp.stack([me % 2, lax.axis_index("tp").astype(jnp.int32), me])
    size = width // ranks
    blocks = [rows // 2] * 2 if rows % 32 == 0 else [rows]
    starts = [sum(blocks[:i]) for i in range(len(blocks))]
    lse_rows = -(-heads // 8) * 8
    shape = jax.ShapeDtypeStruct
    smem = pl.BlockSpec(memory_space=pltpu.SMEM)
    loose = pl.BlockSpec(memory_space=pl.ANY)
    far_off = pl.BlockSpec(memory_space=pltpu.HBM)
    dma = pltpu.SemaphoreType.DMA
    mark = [None]
    pace = [10**10]

    def call(kernel, name, operands, in_specs, out_shape, out_specs, grid=(1,), scratch=(), limit=24, flops=None):
        before = mark[0] if mark[0] is not None else operands[0]
        operands = [
            pltpu.with_memory_space_constraint(operand, pltpu.HBM) if spec is far_off else operand
            for operand, spec in zip(operands, in_specs)
        ]
        *outs, mark[0] = pl.pallas_call(
            chained(kernel, len(operands), len(out_shape)),
            grid=grid,
            out_shape=tuple(out_shape) + (shape((8, LANES), F32),),
            in_specs=[loose] + list(in_specs),
            out_specs=tuple(out_specs) + (whole((8, LANES)),),
            scratch_shapes=list(scratch),
            compiler_params=params(limit),
            cost_estimate=cost(pace[0] if flops is None else flops),
            name=name,
        )(before, *operands)
        return outs

    def full(*arrays):
        return [whole(array.shape) for array in arrays]

    def swap_tp(array):
        pairs = [(i, i ^ 1) for i in range(lax.axis_size("tp"))]
        return lax.ppermute(array, "tp", pairs)

    def swap_dp(array, bits):
        return lax.ppermute(array, "dp", [(i, i ^ bits) for i in range(ranks)])

    stages = []
    while 1 << len(stages) < ranks:
        stages.append(1 << len(stages))
    order = [0]
    for bit in reversed(stages):
        order = order + [bit + rest for rest in order]
    order = order[ranks // 2 :] + order[: ranks // 2]
    fused = size % 16 == 0
    pad_row = pad_mask
    half = w_out.shape[0] // 2
    w_near = swap_tp(lax.dynamic_slice_in_dim(w_out, (me % 2) * half, half, 0).astype(F32))
    outs = [shape((rows, 3 * local), LOW), shape((rows, local), LOW), shape((lse_rows, rows), F32)]
    outs += [shape((block, local), F32) for block in blocks]
    qkv, context, lse, *wides = call(
        functools.partial(attend, blocks), "attend", [tokens, w_qkv, b_qv, lengths, pad_row],
        [far_off] * 2 + full(b_qv) + [smem] + full(pad_row), outs, [far_off] * 2 + full(*outs[2:]),
        scratch=[
            pltpu.VMEM((rows, width), LOW),
            pltpu.VMEM((3, width, local), LOW),
            pltpu.VMEM((rows, 3 * local), LOW),
            pltpu.VMEM((rows, local), LOW),
            dma((6,)),
        ],
        limit=56,
    )
    fars = [swap_tp(wide) for wide in wides]
    near = pl.BlockSpec(memory_space=pltpu.VMEM)
    params_of = [b_out, ln1_gain, ln1_bias, b_down, ln2_gain, ln2_bias]
    outs = [shape(w_near.shape, F32), shape((8, width), F32)]
    w_near, vectors = call(
        relay, "relay", [w_near, *params_of], full(w_near, *params_of), outs, full(*outs)
    )
    far_parts = 3 if half % 48 == 0 else 1
    piece = half // far_parts
    w_fars = [swap_dp(w_near[i * piece : (i + 1) * piece], 1) for i in range(far_parts)]

    tile = min(hidden, 512)
    tiles = hidden // tile

    def columns(height, step):
        return pl.BlockSpec((height, step), lambda f: (0, f))

    saved = []
    for begin, block, far in zip(starts, blocks, fars):
        outs = [
            shape((block, width), F32), shape((block, LANES), F32), shape((block, width), LOW),
            shape((block, hidden), LOW), shape((block, hidden), F32), shape((block, width), F32),
        ]
        outs = call(
            functools.partial(feed, slice(begin, begin + block), tile, far_parts, begin == 0), "feed",
            [place_arr, tokens, context, far, w_out, w_near, *w_fars, vectors, b_up, w_up, w_down],
            [smem] + [far_off] * (6 + far_parts) + full(b_up) + [far_off if begin == 0 else near] * 2,
            outs, full(*outs),
            scratch=[
                pltpu.VMEM((block, width), LOW),
                pltpu.VMEM((block, local), F32),
                pltpu.VMEM((8, width), F32),
                pltpu.VMEM((2, half, width), F32),
                pltpu.VMEM((2 * local, width), LOW),
                pltpu.VMEM((block, 2 * local), LOW),
                dma((6 + far_parts + 2 * tiles,)),
            ]
            + ([pltpu.VMEM((width, hidden), LOW), pltpu.VMEM((hidden, width), LOW)] if begin == 0 else []),
        )
        saved.append(outs + [swap_tp(outs[5])])

    back = []
    for begin, block, (normed, inverse, low, act, slope, own, far) in zip(starts, blocks, saved):
        outs = [
            shape((block, width), LOW), shape((block, width), F32), shape((block, width), LOW),
            shape((block, hidden), LOW), shape((block, width), F32), shape((8, width), F32), shape((8, hidden), F32),
        ]
        outs = call(
            functools.partial(feed_back, slice(begin, begin + block), tile), "feed_back",
            [own, far, normed, slope, vectors, cotangent, w_up, w_down],
            full(own, far, normed, slope) + [far_off] * 2 + [near] * 2,
            outs, full(*outs),
            scratch=[pltpu.VMEM((8, width), F32), pltpu.VMEM((block, width), LOW), dma((2,))],
        )
        back.append(outs + [swap_tp(outs[4])])

    layer_out = jnp.concatenate([outs[0] for outs in back], 0)

    def gradient(lefts, rights, splits, kinds, step, rider=None):
        wide = step * len(kinds)
        sides = max(kinds) + 1
        riders = [] if rider is None else [rider]
        outs = [shape((width // 2 + 8 * len(riders), wide), F32)] * 2
        outs = call(
            functools.partial(
                outer, order if fused else None, size, splits, kinds, len(lefts) - len(splits), len(riders)
            ),
            "outer", [place_arr, *lefts, *rights, *riders],
            [smem] + full(*lefts) + [columns(split, step) for split in splits] + [columns(8, step) for _ in riders],
            outs, [columns(out.shape[0], step) for out in outs],
            grid=(len(kinds),),
            scratch=[pltpu.VMEM((width, rows), LOW), pltpu.VMEM((sides, width, rows), LOW)],
        )
        if not fused:
            every = jnp.concatenate([out[: width // 2] for out in outs], 0).reshape(ranks, size, wide)
            every = jnp.take(every, jnp.array(order, jnp.int32) ^ me, axis=0).reshape(width, wide)
            outs = [every[: width // 2], every[width // 2 :]]
            outs = [jnp.concatenate([out] + riders, 0) for out in outs]
        return outs

    def pick(held, begin, end):
        return [(array, first) for array, first in held if first <= begin and end <= first + array.shape[0]]

    def add(held, begin, end, flops=None, extra=()):
        wide = held[0][0].shape[1]
        if not fused:
            parts = []
            for row in range(begin, end, size):
                parts.append(functools.reduce(jnp.add, [a[row - f : row - f + size] for a, f in pick(held, row, row + size)]))
            if extra:
                parts.append(functools.reduce(jnp.add, [a[row : row + 8] for a, row in extra]))
            return jnp.concatenate(parts, 0)
        operands, specs, counts = [], [], []

        def take(array, row, height):
            operands.append(array)
            specs.append(pl.BlockSpec((height, wide), functools.partial(lambda index, n: (index, 0), row // height)))

        for row in range(begin, end, size):
            inside = pick(held, row, row + size)
            counts.append(len(inside))
            for array, first in inside:
                take(array, row - first, size)
        if extra:
            counts.append(len(extra))
            for array, row in extra:
                take(array, row, 8)
        outs = [shape((end - begin + (8 if extra else 0), wide), F32)]
        return call(functools.partial(fold_blocks, counts), "fold", operands, specs, outs, full(*outs), flops=flops)[0]

    def add_extra(extra):
        if not fused:
            return functools.reduce(jnp.add, [a[row : row + 8] for a, row in extra])
        wide = extra[0][0].shape[1]
        specs = [pl.BlockSpec((8, wide), functools.partial(lambda index, n: (index, 0), row // 8)) for _, row in extra]
        outs = [shape((8, wide), F32)]
        return call(fold, "fold", [array for array, _ in extra], specs, outs, full(*outs))[0]

    class Chunk:
        def __init__(self, outs, rides=False):
            sent, keep = outs
            came = swap_dp(sent, stages[0])
            self.held = [(keep, 0), (came, 0)]
            self.extra = [(keep, width // 2), (came, width // 2)] if rides else []
            self.stage = 0

        def send(self, begin, end, flops, rides):
            rides = rides and self.extra and self.stage < len(stages) - 1
            came = swap_dp(add(self.held, begin, end, flops, self.extra if rides else ()), stages[self.stage])
            if rides:
                self.extra = self.extra + [(came, end - begin)]
            return came

        def step(self, flops=None):
            self.stage += 1
            half = width // (4 << (self.stage - 1))
            self.held = self.held + [(self.send(half, 2 * half, flops, True), 0)]

        def high(self, flops=None):
            half = self.half = width // (4 << self.stage)
            if half == size:
                self.step(flops)
            else:
                self.stage += 1
                self.came = [(self.send(half + half // 2, 2 * half, flops, True), half // 2)]

        def low(self, flops=None):
            part = self.send(self.half, self.half + self.half // 2, flops, False)
            self.held = self.held + self.came + [(part, 0)]

        def all_but_last(self):
            self.held = [(add(self.held[:-1], 0, size), 0), self.held[-1]]

        def last(self, flops=None):
            self.rest()
            return add(self.held, 0, size, flops)

        def rest(self):
            while self.stage < len(stages) - 1:
                self.step()
            return [(array, first) for array, first in self.held if first == 0]

    down = Chunk(gradient([o[2] for o in back], [s[3] for s in saved], blocks, [0] * tiles, tile))
    wide = 4 * local

    def first_norm(i):
        outs = [shape((blocks[i], width), F32), shape((blocks[i], width), LOW), shape((8, wide), F32)]
        operands = [back[i][1], back[i][4], back[i][7], saved[i][0], saved[i][1], back[i][5], back[i][6], vectors]
        operands += [norms[-1][2]] if norms else []
        norms.append(call(norm_one_back, "norm_one_back", operands, full(*operands), outs, full(*outs), flops=2 * 10**10 if i == 0 else None))

    norms = []
    first_norm(0)
    down.high()
    down.low()
    first_norm(1)
    up = Chunk(gradient([s[2] for s in saved], [o[3] for o in back], blocks, [0] * tiles, tile))
    dr1s, lows = [n[0] for n in norms], [n[1] for n in norms]
    outs = [shape((rows, 4 * local), LOW), shape((8, wide), F32)]
    operands = lows + [w_out, qkv, context, lse, lengths, pad_row, norms[-1][2]]
    e, bias = call(
        functools.partial(attend_back, len(lows)), "attend_back", operands,
        full(*lows) + [far_off] * 3 + full(lse) + [smem] + full(pad_row, norms[-1][2]), outs, full(*outs),
        scratch=[pltpu.VMEM((local, width), LOW), pltpu.VMEM((rows, 3 * local), LOW), dma((3,))],
    )
    down.step(2 * 10**10)
    up.high()
    up.low()
    mixed = Chunk(rides=True, outs=gradient([tokens] + lows, [e], [rows], [0, 0, 0, 1], local, bias))

    outs = [shape((rows, width), F32)]
    (partial,) = call(
        back_tokens, "back_tokens", [e, w_qkv], full(e) + [far_off], outs, full(*outs),
        scratch=[pltpu.VMEM((3, width, local), LOW), dma((3,))],
    )
    pace[0] = 10**9
    partial_far = swap_tp(partial)
    pace[0] = 10**9
    down.step()
    up.step(2 * 10**10)
    mixed.high()
    mixed.low()
    down = down.last(5 * 10**9)
    up.step()
    mixed.high()
    mixed.low()
    up = up.last()
    while mixed.stage < len(stages) - 1:
        mixed.high()
        if mixed.half > size:
            mixed.low()
    bias = add_extra(mixed.extra)
    bias_far = swap_dp(bias, stages[-1])
    mixed.all_but_last()
    (d_tokens,) = call(
        join, "join", [partial, partial_far] + dr1s, full(partial, partial_far, *dr1s), outs, full(*outs)
    )
    (bias,) = call(fold, "fold", [bias, bias_far], full(bias, bias_far), [shape(bias.shape, F32)], full(bias))
    mixed = mixed.rest()

    def finish(held):
        return functools.reduce(jnp.add, [array[:size] for array, _ in held])

    if fused:
        outs = [shape((3, size, local), F32), shape((size, local), F32)]
        d_w_qkv, d_w_out = call(
            functools.partial(spread, local), "spread", [array for array, _ in mixed],
            [pl.BlockSpec((size, 4 * local), lambda n: (0, 0))] * len(mixed), outs, full(*outs),
        )
    else:
        last = finish(mixed)
        d_w_qkv = last[:, : 3 * local].reshape(size, 3, local).transpose(1, 0, 2)
        d_w_out = last[:, 3 * local :]
    return (
        layer_out,
        d_tokens,
        d_w_qkv,
        bias[7, : 2 * local].reshape(2, local),
        d_w_out.T,
        bias[5, :width],
        bias[3, :width],
        bias[4, :width],
        up,
        bias[6, :hidden],
        down.T,
        bias[2, :width],
        bias[0, :width],
        bias[1, :width],
    )


def solution(mesh):
    placed = (
        P("dp", None), P("dp", None), P("dp"), P(None, None, "tp"), P(None, "tp"), P("tp", None),
        P(), P(), P(), P(None, "tp"), P("tp"), P("tp", None), P(), P(), P(), P("dp", None),
    )
    return jax.shard_map(
        on_device,
        mesh=mesh,
        in_specs=placed,
        out_specs=(
            P("dp", None), P("dp", None), P(None, "dp", "tp"), P(None, "tp"), P("tp", "dp"), P(), P(), P(),
            P("dp", "tp"), P("tp"), P("tp", "dp"), P(), P(), P(),
        ),
        check_vma=False,
    )
```

```python
import functools

import jax
import jax.numpy as jnp
from jax import lax
from jax.experimental import pallas as pl
from jax.experimental.pallas import tpu as pltpu
from jax.sharding import PartitionSpec as P

HEAD = 64
NEG_FILL = -1e30
EPS_NORM = 1e-12
LANES = 128
F32 = jnp.float32
LOW = jnp.bfloat16
MIB = 1 << 20


def dot(a, b):
    return lax.dot_general(a, b, (((1,), (0,)), ((), ())), preferred_element_type=F32)


def dot_nt(a, b):
    return lax.dot_general(a, b, (((1,), (1,)), ((), ())), preferred_element_type=F32)


def whole(shape):
    return pl.BlockSpec(shape, lambda *_: (0,) * len(shape))


def params(limit):
    return pltpu.CompilerParams(vmem_limit_bytes=limit * MIB)


def cost(flops):
    return pl.CostEstimate(flops=flops, bytes_accessed=10**6, transcendentals=0)


def key_mask(lengths_ref, pad_ref, rows):
    seqs = lengths_ref.shape[1]
    key_at = lax.broadcasted_iota(jnp.int32, (rows, LANES), 0)
    query_at = lax.broadcasted_iota(jnp.int32, (8, rows), 1)
    key_seg = jnp.zeros((rows, LANES), jnp.int32)
    query_seg = jnp.zeros((8, rows), jnp.int32)
    end = jnp.int32(0)
    for i in range(seqs):
        end = end + lengths_ref[0, i]
        key_seg = key_seg + (key_at >= end).astype(jnp.int32)
        query_seg = query_seg + (query_at >= end).astype(jnp.int32)
    pad = jnp.broadcast_to(pad_ref[...].astype(F32).reshape(1, rows), (LANES, rows)).T
    pieces = []
    for j in range(rows // LANES):
        span = slice(j * LANES, (j + 1) * LANES)
        same = key_seg == query_seg[0:1, span]
        usable = (pad == 1.0) | (key_at == query_at[0:1, span])
        pieces.append(jnp.where(same & usable, 0.0, NEG_FILL))
    return jnp.concatenate(pieces, 1)


def halves():
    lane = lax.broadcasted_iota(jnp.int32, (1, LANES), 1)
    left = (lane < HEAD).astype(F32)
    return left.astype(LOW), (1.0 - left).astype(LOW)


def fetch(sources, targets, sems):
    copies = [pltpu.make_async_copy(source, target, sems.at[i]) for i, (source, target) in enumerate(zip(sources, targets))]
    for copy in copies:
        copy.start()
    return copies


def attend(
    blocks, x_hbm, w_hbm, b_ref, lengths_ref, pad_ref, qkv_hbm, ctx_hbm, lse_ref, *rest
):
    wide_refs, (x_ref, w_ref, qkv_ref, ctx_ref, sems) = rest[:-5], rest[-5:]
    rows = x_ref.shape[0]
    local = w_ref.shape[2]
    scale = float(HEAD) ** (-0.5)
    came = fetch([x_hbm] + [w_hbm.at[i] for i in range(3)], [x_ref] + [w_ref.at[i] for i in range(3)], sems)
    bias = key_mask(lengths_ref, pad_ref, rows)
    sides = halves()
    came[0].wait()
    x = x_ref[...]
    came[1].wait()
    qkv_ref[:, 0:local] = ((dot(x, w_ref[0]) + b_ref[0:1, :].astype(F32)) * scale).astype(LOW)
    came[2].wait()
    qkv_ref[:, local : 2 * local] = dot(x, w_ref[1]).astype(LOW)
    came[3].wait()
    qkv_ref[:, 2 * local :] = (dot(x, w_ref[2]) + b_ref[1:2, :].astype(F32)).astype(LOW)
    saved = pltpu.make_async_copy(qkv_ref, qkv_hbm, sems.at[4])
    saved.start()
    for pair in range(local // LANES):
        at = pair * LANES
        span = slice(at, at + LANES)
        query = qkv_ref[:, span]
        keys = qkv_ref[:, local + at : local + at + LANES]
        flipped = qkv_ref[:, 2 * local + at : 2 * local + at + LANES].T
        parts = []
        for side in range(2):
            scores = dot_nt(keys * sides[side], query) + bias
            top = jnp.max(scores, 0, keepdims=True)
            expo = jnp.exp(scores - top)
            total = jnp.sum(expo, 0, keepdims=True)
            probs = (expo * (1.0 / total)).astype(LOW)
            parts.append(dot(flipped[side * HEAD : (side + 1) * HEAD], probs))
            head = 2 * pair + side
            lse_ref[head : head + 1, :] = top + jnp.log(total)
        context = jnp.concatenate(parts, 0).T.astype(LOW)
        ctx_ref[:, span] = context
        start = 0
        for wide_ref, size in zip(wide_refs, blocks):
            wide_ref[:, span] = context[start : start + size].astype(F32)
            start += size
    kept = pltpu.make_async_copy(ctx_ref, ctx_hbm, sems.at[5])
    kept.start()
    saved.wait()
    kept.wait()


def relay(in_ref, *refs):
    vectors = refs[:6]
    out_ref, vec_ref = refs[-2:]
    out_ref[...] = in_ref[...]
    vec_ref[...] = jnp.zeros(vec_ref.shape, F32)
    for i, ref in enumerate(vectors):
        vec_ref[i : i + 1, :] = ref[...].astype(F32).reshape(1, -1)


def norm_rows(value):
    centered = value - jnp.mean(value, -1, keepdims=True)
    inverse = lax.rsqrt(jnp.mean(centered * centered, -1, keepdims=True) + EPS_NORM)
    return centered * inverse, inverse


def norm_back(grad, normed, inverse, gain):
    scaled = grad * gain
    return inverse * (
        scaled
        - jnp.mean(scaled, -1, keepdims=True)
        - normed * jnp.mean(scaled * normed, -1, keepdims=True)
    )


def row(ref):
    return ref[...].astype(F32)


def feed(taken, tile, far_parts, streamed, place_ref, x_hbm, own_hbm, far_hbm, w_own_hbm, w_near_hbm, *refs):
    w_fars, refs = refs[:far_parts], refs[far_parts:]
    vec_hbm, b_up_ref, w_up, w_down, normed_ref, inverse_ref, low_ref, act_ref, slope_ref, part_ref = refs[:10]
    x_ref, far_ref, vec_ref, w_far, w_full, ctx_full, sems = refs[10:17]
    local = own_hbm.shape[1]
    half = w_near_hbm.shape[0]
    piece = half // far_parts
    hidden = w_up.shape[1]
    core, side = place_ref[0], place_ref[1]
    here = pl.multiple_of(side * local, LANES)
    there = pl.multiple_of((1 - side) * local, LANES)
    spans = [slice(at, at + tile) for at in range(0, hidden, tile)]
    sources = [w_near_hbm] + list(w_fars) + [w_own_hbm, own_hbm.at[taken], far_hbm, x_hbm.at[taken], vec_hbm]
    targets = [w_far.at[0]] + [w_far.at[1, i * piece : (i + 1) * piece] for i in range(far_parts)]
    targets += [w_full.at[pl.ds(here, local)], ctx_full.at[:, pl.ds(here, local)], far_ref, x_ref, vec_ref]
    needed = len(sources)
    if streamed:
        w_up_vmem, w_down_vmem = refs[17:]
        for span in spans:
            sources += [w_up.at[:, span], w_down.at[span]]
            targets += [w_up_vmem.at[:, span], w_down_vmem.at[span]]
        w_up, w_down = w_up_vmem, w_down_vmem
    came = fetch(sources, targets, sems)
    for copy in came[:needed]:
        copy.wait()
    for i in range(2):
        at = pl.multiple_of(there + (core ^ i) * half, 16)
        w_full[pl.ds(at, half), :] = w_far[i].astype(LOW)
    ctx_full[:, pl.ds(there, local)] = far_ref[...].astype(LOW)
    attn = dot(ctx_full[...], w_full[...])
    normed, inverse = norm_rows(x_ref[...].astype(F32) + attn + vec_ref[0:1, :])
    normed_ref[...] = normed
    inverse_ref[...] = jnp.broadcast_to(inverse, inverse_ref.shape)
    low = (normed * vec_ref[1:2, :] + vec_ref[2:3, :]).astype(LOW)
    low_ref[...] = low
    b_up = b_up_ref[...].astype(F32).reshape(1, -1)
    for i, span in enumerate(spans):
        if streamed:
            came[needed + 2 * i].wait()
        pre = dot(low, w_up[:, span]) + b_up[:, span]
        share = 0.5 * (1.0 + lax.erf(pre * 0.7071067811865476))
        act = (pre * share).astype(LOW)
        act_ref[:, span] = act
        slope_ref[:, span] = share + pre * jnp.exp(-0.5 * pre * pre) * 0.3989422804014327
        if streamed:
            came[needed + 2 * i + 1].wait()
        added = dot(act, w_down[span, :])
        if i == 0:
            part_ref[...] = added
        else:
            part_ref[...] += added


def feed_back(
    taken, tile, own_ref, far_ref, normed_ref, slope_ref, vec_hbm, up_hbm, w_up, w_down,
    out_ref, grad_ref, low_ref, pre_ref, part_ref, sums_ref, b_up_ref,
    vec_ref, up_ref, sems,
):
    hidden = w_up.shape[1]
    spans = [slice(at, at + tile) for at in range(0, hidden, tile)]
    came = fetch([up_hbm.at[taken], vec_hbm], [up_ref, vec_ref], sems)
    came[1].wait()
    hidden_rows = normed_ref[...] * vec_ref[1:2, :] + vec_ref[2:3, :]
    normed, inverse = norm_rows(hidden_rows + (own_ref[...] + far_ref[...]) + vec_ref[3:4, :])
    gain = vec_ref[4:5, :]
    out_ref[...] = (normed * gain + vec_ref[5:6, :]).astype(LOW)
    came[0].wait()
    upstream = up_ref[...].astype(F32)
    grad = norm_back(upstream, normed, inverse, gain)
    grad_ref[...] = grad
    low = grad.astype(LOW)
    low_ref[...] = low
    sums_ref[0:1, :] = jnp.sum(upstream * normed, 0, keepdims=True)
    sums_ref[1:2, :] = jnp.sum(upstream, 0, keepdims=True)
    sums_ref[2:3, :] = jnp.sum(grad, 0, keepdims=True)
    sums_ref[3:8, :] = jnp.zeros((5, sums_ref.shape[1]), F32)
    for i, span in enumerate(spans):
        pre = (dot_nt(low, w_down[span, :]) * slope_ref[:, span]).astype(LOW)
        pre_ref[:, span] = pre
        b_up_ref[:, span] = jnp.broadcast_to(jnp.sum(pre.astype(F32), 0, keepdims=True), (8, tile))
        added = dot_nt(pre, w_up[:, span])
        if i == 0:
            part_ref[...] = added
        else:
            part_ref[...] += added


def norm_one_back(own_dr2, own_ref, far_ref, normed_ref, inverse_ref, sums_ref, b_up_ref, vec_ref, *refs):
    before, (dr1_ref, low_ref, bias_ref) = refs[:-3], refs[-3:]
    width = dr1_ref.shape[1]
    grad = own_dr2[...] + (own_ref[...] + far_ref[...])
    norm = normed_ref[...]
    dr1 = norm_back(grad, norm, inverse_ref[:, 0:1], vec_ref[1:2, :])
    dr1_ref[...] = dr1
    low_ref[...] = dr1.astype(LOW)
    bias_ref[...] = before[0][...] if before else jnp.zeros(bias_ref.shape, F32)
    bias_ref[0:3, 0:width] += sums_ref[0:3]
    for i, value in enumerate((grad * norm, grad, dr1)):
        bias_ref[3 + i : 4 + i, 0:width] += jnp.sum(value, 0, keepdims=True)
    bias_ref[6:7, 0 : b_up_ref.shape[1]] += b_up_ref[0:1, :]


def attend_back(
    count, *refs,
):
    attend_back_body(refs[:count], *refs[count:])


def attend_back_body(
    low_refs, w_hbm, qkv_hbm, ctx_hbm, lse_ref, lengths_ref, pad_ref, so_far_ref, e_ref, bias_ref,
    w_ref, qkv_ref, sems,
):
    rows, local = ctx_hbm.shape
    came = fetch([w_hbm, qkv_hbm, ctx_hbm], [w_ref, qkv_ref, e_ref.at[:, 3 * local : 4 * local]], sems)
    scale = float(HEAD) ** (-0.5)
    bias_ref[...] = so_far_ref[...]
    mask = key_mask(lengths_ref, pad_ref, rows)
    sides = halves()
    came[0].wait()
    d_ctx = dot_nt(jnp.concatenate([ref[...] for ref in low_refs], 0), w_ref[...]).astype(LOW)
    came[1].wait()
    for pair in range(local // LANES):
        at = pair * LANES
        span = slice(at, at + LANES)
        query = qkv_ref[:, span]
        keys = qkv_ref[:, local + at : local + at + LANES]
        values = qkv_ref[:, 2 * local + at : 2 * local + at + LANES]
        grads = d_ctx[:, span]
        flipped = keys.T
        d_q = []
        d_k = jnp.zeros((rows, LANES), F32)
        d_v = jnp.zeros((rows, LANES), F32)
        for side in range(2):
            head = 2 * pair + side
            scores = dot_nt(keys * sides[side], query) + mask
            probs = jnp.exp(scores - lse_ref[head : head + 1, :])
            d_p = dot_nt(values * sides[side], grads)
            mixed = jnp.sum(probs * d_p, 0, keepdims=True)
            d_s = (probs * (d_p - mixed)).astype(LOW)
            d_k = d_k + dot(d_s, query * sides[side])
            d_v = d_v + dot(probs.astype(LOW), grads * sides[side])
            d_q.append(dot(flipped[side * HEAD : (side + 1) * HEAD], d_s))
        d_query = jnp.concatenate(d_q, 0).T.astype(LOW).astype(F32) * scale
        d_k = d_k.astype(LOW)
        d_v = d_v.astype(LOW)
        e_ref[:, at : at + LANES] = d_query.astype(LOW)
        e_ref[:, local + at : local + at + LANES] = d_k
        e_ref[:, 2 * local + at : 2 * local + at + LANES] = d_v
        bias_ref[7:8, at : at + LANES] = jnp.sum(d_query, 0, keepdims=True)
        bias_ref[7:8, local + at : local + at + LANES] = jnp.sum(d_v.astype(F32), 0, keepdims=True)
    came[2].wait()


def place_blocks(me, source, target, order, size):
    for i, block in enumerate(order):
        at = pl.multiple_of((me ^ block) * size, size)
        target[i * size : (i + 1) * size, :] = source[pl.ds(at, size), :]


def outer(order, size, splits, kinds, more, rides, place_ref, *refs):
    count = len(splits)
    sides = max(kinds) + 1
    lefts = [refs[:count]] + ([refs[count : count + more]] if more else [])
    rights = refs[count + more : 2 * count + more]
    rider = refs[2 * count + more] if rides else None
    *sent_refs, keep_ref, flipped, placed = refs[2 * count + more + rides :]
    step = pl.program_id(0)

    @pl.when(step == 0)
    def _():
        for index, group in enumerate(lefts):
            source = jnp.concatenate([ref[...] for ref in group], 0).T
            if order is None:
                placed[index] = source
            else:
                flipped[...] = source
                place_blocks(place_ref[2], flipped, placed.at[index], order, size)

    left = placed[0]
    if sides > 1:
        change = kinds.index(1)
        left = placed[jnp.where(step >= change, 1, 0)]
    right = jnp.concatenate([ref[...] for ref in rights], 0)
    half = left.shape[0] // 2
    part = half // len(sent_refs)
    for i, ref in enumerate(sent_refs):
        ref[0:part, :] = dot(left[i * part : (i + 1) * part], right)
    keep_ref[0:half, :] = dot(left[half:], right)
    if rides:
        sent_refs[-1][part:, :] = rider[...]
        keep_ref[half:, :] = rider[...]


def fold(*refs):
    value = refs[0][...]
    for ref in refs[1:-1]:
        value = value + ref[...]
    refs[-1][...] = value


def fold_blocks(counts, *refs):
    out_ref = refs[-1]
    at = start = 0
    for count in counts:
        value = refs[at][...]
        for ref in refs[at + 1 : at + count]:
            value = value + ref[...]
        end = start + value.shape[0]
        out_ref[start:end, :] = value
        at += count
        start = end


def back_tokens(e_ref, w_hbm, out_ref, w_ref, sems):
    local = w_ref.shape[2]
    came = fetch([w_hbm.at[i] for i in range(3)], [w_ref.at[i] for i in range(3)], sems)
    for i in range(3):
        came[i].wait()
        added = dot_nt(e_ref[:, i * local : (i + 1) * local], w_ref[i])
        if i == 0:
            out_ref[...] = added
        else:
            out_ref[...] += added


def join(own_ref, far_ref, *refs):
    out_ref, start = refs[-1], 0
    for ref in refs[:-1]:
        span = slice(start, start + ref.shape[0])
        out_ref[span, :] = ref[...] + (own_ref[span, :] + far_ref[span, :])
        start += ref.shape[0]


def spread(local, *refs):
    qkv_ref, out_ref = refs[-2:]
    value = refs[0][...]
    for ref in refs[1:-2]:
        value = value + ref[...]
    for i in range(3):
        qkv_ref[i] = value[:, i * local : (i + 1) * local]
    out_ref[...] = value[:, 3 * local :]


def chained(kernel, inputs, outputs):
    def body(*refs):
        refs[1 + inputs + outputs][...] = jnp.zeros((8, LANES), F32)
        kernel(*refs[1 : 1 + inputs + outputs], *refs[2 + inputs + outputs :])

    return body


def on_device(
    tokens, lengths, pad_mask, w_qkv, b_qv, w_out, b_out, ln1_gain, ln1_bias,
    w_up, b_up, w_down, b_down, ln2_gain, ln2_bias, cotangent,
):
    rows, width = tokens.shape
    local = w_qkv.shape[2]
    heads = local // HEAD
    hidden = w_up.shape[1]
    ranks = lax.axis_size("dp")
    me = lax.axis_index("dp").astype(jnp.int32)
    place_arr = jnp.stack([me % 2, lax.axis_index("tp").astype(jnp.int32), me])
    size = width // ranks
    blocks = [rows // 2] * 2 if rows % 32 == 0 else [rows]
    starts = [sum(blocks[:i]) for i in range(len(blocks))]
    lse_rows = -(-heads // 8) * 8
    shape = jax.ShapeDtypeStruct
    smem = pl.BlockSpec(memory_space=pltpu.SMEM)
    loose = pl.BlockSpec(memory_space=pl.ANY)
    far_off = pl.BlockSpec(memory_space=pltpu.HBM)
    dma = pltpu.SemaphoreType.DMA
    mark = [None]
    pace = [10**10]

    def call(kernel, name, operands, in_specs, out_shape, out_specs, grid=(1,), scratch=(), limit=24, flops=None):
        before = mark[0] if mark[0] is not None else operands[0]
        operands = [
            pltpu.with_memory_space_constraint(operand, pltpu.HBM) if spec is far_off else operand
            for operand, spec in zip(operands, in_specs)
        ]
        *outs, mark[0] = pl.pallas_call(
            chained(kernel, len(operands), len(out_shape)),
            grid=grid,
            out_shape=tuple(out_shape) + (shape((8, LANES), F32),),
            in_specs=[loose] + list(in_specs),
            out_specs=tuple(out_specs) + (whole((8, LANES)),),
            scratch_shapes=list(scratch),
            compiler_params=params(limit),
            cost_estimate=cost(pace[0] if flops is None else flops),
            name=name,
        )(before, *operands)
        return outs

    def full(*arrays):
        return [whole(array.shape) for array in arrays]

    def swap_tp(array):
        pairs = [(i, i ^ 1) for i in range(lax.axis_size("tp"))]
        return lax.ppermute(array, "tp", pairs)

    def swap_dp(array, bits):
        return lax.ppermute(array, "dp", [(i, i ^ bits) for i in range(ranks)])

    stages = []
    while 1 << len(stages) < ranks:
        stages.append(1 << len(stages))
    order = [0]
    for bit in reversed(stages):
        order = order + [bit + rest for rest in order]
    order = order[ranks // 2 :] + order[: ranks // 2]
    fused = size % 16 == 0
    pad_row = pad_mask
    half = w_out.shape[0] // 2
    w_near = swap_tp(lax.dynamic_slice_in_dim(w_out, (me % 2) * half, half, 0).astype(F32))
    outs = [shape((rows, 3 * local), LOW), shape((rows, local), LOW), shape((lse_rows, rows), F32)]
    outs += [shape((block, local), F32) for block in blocks]
    qkv, context, lse, *wides = call(
        functools.partial(attend, blocks), "attend", [tokens, w_qkv, b_qv, lengths, pad_row],
        [far_off] * 2 + full(b_qv) + [smem] + full(pad_row), outs, [far_off] * 2 + full(*outs[2:]),
        scratch=[
            pltpu.VMEM((rows, width), LOW),
            pltpu.VMEM((3, width, local), LOW),
            pltpu.VMEM((rows, 3 * local), LOW),
            pltpu.VMEM((rows, local), LOW),
            dma((6,)),
        ],
        limit=56,
    )
    fars = [swap_tp(wide) for wide in wides]
    near = pl.BlockSpec(memory_space=pltpu.VMEM)
    params_of = [b_out, ln1_gain, ln1_bias, b_down, ln2_gain, ln2_bias]
    outs = [shape(w_near.shape, F32), shape((8, width), F32)]
    w_near, vectors = call(
        relay, "relay", [w_near, *params_of], full(w_near, *params_of), outs, full(*outs)
    )
    far_parts = 3 if half % 48 == 0 else 1
    piece = half // far_parts
    w_fars = [swap_dp(w_near[i * piece : (i + 1) * piece], 1) for i in range(far_parts)]

    tile = min(hidden, 512)
    tiles = hidden // tile

    def columns(height, step):
        return pl.BlockSpec((height, step), lambda f: (0, f))

    saved = []
    for begin, block, far in zip(starts, blocks, fars):
        outs = [
            shape((block, width), F32), shape((block, LANES), F32), shape((block, width), LOW),
            shape((block, hidden), LOW), shape((block, hidden), F32), shape((block, width), F32),
        ]
        outs = call(
            functools.partial(feed, slice(begin, begin + block), tile, far_parts, begin == 0), "feed",
            [place_arr, tokens, context, far, w_out, w_near, *w_fars, vectors, b_up, w_up, w_down],
            [smem] + [far_off] * (6 + far_parts) + full(b_up) + [far_off if begin == 0 else near] * 2,
            outs, full(*outs),
            scratch=[
                pltpu.VMEM((block, width), LOW),
                pltpu.VMEM((block, local), F32),
                pltpu.VMEM((8, width), F32),
                pltpu.VMEM((2, half, width), F32),
                pltpu.VMEM((2 * local, width), LOW),
                pltpu.VMEM((block, 2 * local), LOW),
                dma((6 + far_parts + 2 * tiles,)),
            ]
            + ([pltpu.VMEM((width, hidden), LOW), pltpu.VMEM((hidden, width), LOW)] if begin == 0 else []),
        )
        saved.append(outs + [swap_tp(outs[5])])

    back = []
    for begin, block, (normed, inverse, low, act, slope, own, far) in zip(starts, blocks, saved):
        outs = [
            shape((block, width), LOW), shape((block, width), F32), shape((block, width), LOW),
            shape((block, hidden), LOW), shape((block, width), F32), shape((8, width), F32), shape((8, hidden), F32),
        ]
        outs = call(
            functools.partial(feed_back, slice(begin, begin + block), tile), "feed_back",
            [own, far, normed, slope, vectors, cotangent, w_up, w_down],
            full(own, far, normed, slope) + [far_off] * 2 + [near] * 2,
            outs, full(*outs),
            scratch=[pltpu.VMEM((8, width), F32), pltpu.VMEM((block, width), LOW), dma((2,))],
        )
        back.append(outs + [swap_tp(outs[4])])

    layer_out = jnp.concatenate([outs[0] for outs in back], 0)

    def gradient(lefts, rights, splits, kinds, step, rider=None):
        wide = step * len(kinds)
        sides = max(kinds) + 1
        riders = [] if rider is None else [rider]
        outs = [shape((width // 2 + 8 * len(riders), wide), F32)] * 2
        outs = call(
            functools.partial(
                outer, order if fused else None, size, splits, kinds, len(lefts) - len(splits), len(riders)
            ),
            "outer", [place_arr, *lefts, *rights, *riders],
            [smem] + full(*lefts) + [columns(split, step) for split in splits] + [columns(8, step) for _ in riders],
            outs, [columns(out.shape[0], step) for out in outs],
            grid=(len(kinds),),
            scratch=[pltpu.VMEM((width, rows), LOW), pltpu.VMEM((sides, width, rows), LOW)],
        )
        if not fused:
            every = jnp.concatenate([out[: width // 2] for out in outs], 0).reshape(ranks, size, wide)
            every = jnp.take(every, jnp.array(order, jnp.int32) ^ me, axis=0).reshape(width, wide)
            outs = [every[: width // 2], every[width // 2 :]]
            outs = [jnp.concatenate([out] + riders, 0) for out in outs]
        return outs

    class Chunk:
        def __init__(self, outs, came, wide, column, bits, rides=False):
            keep = outs[1]
            self.wide = wide
            self.parts = {p: [(keep, p, column), (came, p, column)] for p in range(ranks // 2)}
            self.alive = list(self.parts)
            self.bits = list(bits)
            self.extra = [(keep, width // 16), (came, width // 16)] if rides else []

        def add(self, places, flops, rides=False):
            wide = self.wide
            if not fused:
                sums = []
                for p in places:
                    found = [
                        array[row * size : (row + 1) * size, column * wide : (column + 1) * wide]
                        for array, row, column in self.parts[p]
                    ]
                    sums.append(functools.reduce(jnp.add, found))
                if rides:
                    sums.append(functools.reduce(jnp.add, [a[8 * row : 8 * row + 8] for a, row in self.extra]))
                return jnp.concatenate(sums, 0)
            operands, specs, counts = [], [], []
            for p in places:
                counts.append(len(self.parts[p]))
                for array, row, column in self.parts[p]:
                    operands.append(array)
                    specs.append(pl.BlockSpec((size, wide), functools.partial(lambda r, c, n: (r, c), row, column)))
            if rides:
                counts.append(len(self.extra))
                for array, row in self.extra:
                    operands.append(array)
                    specs.append(pl.BlockSpec((8, wide), functools.partial(lambda r, n: (r, 0), row)))
            outs = [shape((len(places) * size + (8 if rides else 0), wide), F32)]
            return call(
                functools.partial(fold_blocks, counts), "fold", operands, specs, outs, full(*outs), flops=flops
            )[0]

        def weight(self, bit):
            return ranks // (2 * bit)

        def send(self, places, flops, rides):
            bit = self.bits[0]
            rides = rides and self.extra and len(self.bits) > 1
            came = swap_dp(self.add(places, flops, rides), bit)
            self.arrived = getattr(self, "arrived", [])
            for i, p in enumerate(places):
                self.arrived.append((p ^ self.weight(bit), (came, i, 0)))
            if rides:
                self.extra = self.extra + [(came, len(places) * size // 8)]

        def close(self):
            for p, part in self.arrived:
                self.parts[p].append(part)
            self.arrived = []
            weight = self.weight(self.bits.pop(0))
            self.alive = [p for p in self.alive if not p & weight]

        def leaving(self):
            weight = self.weight(self.bits[0])
            return [p for p in self.alive if p & weight]

        def step(self, flops=None):
            self.send(self.leaving(), flops, True)
            self.close()

        def high(self, flops=None):
            if len(self.bits) == 1:
                self.step(flops)
            else:
                after = self.weight(self.bits[1])
                self.send([p for p in self.leaving() if p & after], flops, True)

        def low(self, flops=None):
            after = self.weight(self.bits[1])
            self.send([p for p in self.leaving() if not p & after], flops, False)
            self.close()

        def rest(self):
            while self.bits:
                self.step()

        def all_but_last(self):
            last = self.parts[0].pop()
            self.parts[0] = [(self.add([0], None), 0, 0), last]

        def last(self, flops=None):
            self.rest()
            return self.add([0], flops)

    def add_extra(extra):
        if not fused:
            return functools.reduce(jnp.add, [a[8 * row : 8 * row + 8] for a, row in extra])
        wide = extra[0][0].shape[1]
        specs = [pl.BlockSpec((8, wide), functools.partial(lambda index, n: (index, 0), row)) for _, row in extra]
        outs = [shape((8, wide), F32)]
        return call(fold, "fold", [array for array, _ in extra], specs, outs, full(*outs))[0]

    straight, turned = stages[1:], stages[2:] + stages[1:2]
    outs = gradient([o[2] for o in back], [s[3] for s in saved], blocks, [0] * tiles, tile)
    came = swap_dp(outs[0], stages[0])
    down = Chunk(outs, came, hidden // 3 * 2, 0, straight)
    early = Chunk(outs, came, hidden // 3, 2, turned)
    wide = 4 * local

    def first_norm(i):
        outs = [shape((blocks[i], width), F32), shape((blocks[i], width), LOW), shape((8, wide), F32)]
        operands = [back[i][1], back[i][4], back[i][7], saved[i][0], saved[i][1], back[i][5], back[i][6], vectors]
        operands += [norms[-1][2]] if norms else []
        flops = 2 * 10**10 if i == 0 else None
        norms.append(call(norm_one_back, "norm_one_back", operands, full(*operands), outs, full(*outs), flops=flops))

    norms = []
    first_norm(0)
    down.high()
    down.low()
    early.step()
    outs = gradient([s[2] for s in saved], [o[3] for o in back], blocks, [0] * tiles, tile)
    up = Chunk(outs, swap_dp(outs[0], stages[0]), hidden, 0, straight)
    first_norm(1)
    early.step()
    down.step(2 * 10**10)
    up.high()
    up.low()
    pace[0] = 10**8
    dr1s, lows = [n[0] for n in norms], [n[1] for n in norms]
    outs = [shape((rows, 4 * local), LOW), shape((8, wide), F32)]
    operands = lows + [w_out, qkv, context, lse, lengths, pad_row, norms[-1][2]]
    e, bias = call(
        functools.partial(attend_back, len(lows)), "attend_back", operands,
        full(*lows) + [far_off] * 3 + full(lse) + [smem] + full(pad_row, norms[-1][2]), outs, full(*outs),
        scratch=[pltpu.VMEM((local, width), LOW), pltpu.VMEM((rows, 3 * local), LOW), dma((3,))],
    )
    outs = gradient([tokens] + lows, [e], [rows], [0, 0, 0, 1], local, bias)
    mixed = Chunk(outs, swap_dp(outs[0], stages[0]), wide, 0, straight, rides=True)

    while early.bits:
        early.step()
    outs = [shape((rows, width), F32)]
    (partial,) = call(
        back_tokens, "back_tokens", [e, w_qkv], full(e) + [far_off], outs, full(*outs),
        scratch=[pltpu.VMEM((3, width, local), LOW), dma((3,))],
    )
    pace[0] = 10**9
    partial_far = swap_tp(partial)
    down.step(2 * 10**10)
    up.step(2 * 10**10)
    mixed.high()
    mixed.low()
    down = down.last(5 * 10**9)
    up.step()
    mixed.high()
    mixed.low()
    up = up.last()
    mixed.rest()
    bias = add_extra(mixed.extra)
    bias_far = swap_dp(bias, stages[-1])
    mixed.all_but_last()
    early = early.last()
    (d_tokens,) = call(
        join, "join", [partial, partial_far] + dr1s, full(partial, partial_far, *dr1s), outs, full(*outs)
    )
    (bias,) = call(fold, "fold", [bias, bias_far], full(bias, bias_far), [shape(bias.shape, F32)], full(bias))
    if fused:
        outs = [shape((3, size, local), F32), shape((size, local), F32)]
        operands = [array for array, _, _ in mixed.parts[0]]
        d_w_qkv, d_w_out = call(
            functools.partial(spread, local), "spread", operands,
            [pl.BlockSpec((size, wide), lambda n: (0, 0))] * len(operands), outs, full(*outs),
        )
    else:
        last = mixed.add([0], None)
        d_w_qkv = last[:, : 3 * local].reshape(size, 3, local).transpose(1, 0, 2)
        d_w_out = last[:, 3 * local :]
    return (
        layer_out,
        d_tokens,
        d_w_qkv,
        bias[7, : 2 * local].reshape(2, local),
        d_w_out.T,
        bias[5, :width],
        bias[3, :width],
        bias[4, :width],
        up,
        bias[6, :hidden],
        jnp.concatenate([down.T, early.T], 0),
        bias[2, :width],
        bias[0, :width],
        bias[1, :width],
    )


def solution(mesh):
    placed = (
        P("dp", None), P("dp", None), P("dp"), P(None, None, "tp"), P(None, "tp"), P("tp", None),
        P(), P(), P(), P(None, "tp"), P("tp"), P("tp", None), P(), P(), P(), P("dp", None),
    )
    return jax.shard_map(
        on_device,
        mesh=mesh,
        in_specs=placed,
        out_specs=(
            P("dp", None), P("dp", None), P(None, "dp", "tp"), P(None, "tp"), P("tp", "dp"), P(), P(), P(),
            P("dp", "tp"), P("tp"), P("tp", "dp"), P(), P(), P(),
        ),
        check_vma=False,
    )
```

```python
import functools

import jax
import jax.numpy as jnp
from jax import lax
from jax.experimental import pallas as pl
from jax.experimental.pallas import tpu as pltpu
from jax.sharding import PartitionSpec as P

HEAD = 64
NEG_FILL = -1e30
EPS_NORM = 1e-12
LANES = 128
F32 = jnp.float32
LOW = jnp.bfloat16
MIB = 1 << 20


def dot(a, b):
    return lax.dot_general(a, b, (((1,), (0,)), ((), ())), preferred_element_type=F32)


def dot_nt(a, b):
    return lax.dot_general(a, b, (((1,), (1,)), ((), ())), preferred_element_type=F32)


def whole(shape):
    return pl.BlockSpec(shape, lambda *_: (0,) * len(shape))


def params(limit):
    return pltpu.CompilerParams(vmem_limit_bytes=limit * MIB)


def cost(flops):
    return pl.CostEstimate(flops=flops, bytes_accessed=10**6, transcendentals=0)


def key_mask(lengths_ref, pad_ref, rows):
    seqs = lengths_ref.shape[1]
    key_at = lax.broadcasted_iota(jnp.int32, (rows, LANES), 0)
    query_at = lax.broadcasted_iota(jnp.int32, (8, rows), 1)
    key_seg = jnp.zeros((rows, LANES), jnp.int32)
    query_seg = jnp.zeros((8, rows), jnp.int32)
    end = jnp.int32(0)
    for i in range(seqs):
        end = end + lengths_ref[0, i]
        key_seg = key_seg + (key_at >= end).astype(jnp.int32)
        query_seg = query_seg + (query_at >= end).astype(jnp.int32)
    pad = jnp.broadcast_to(pad_ref[...].astype(F32).reshape(1, rows), (LANES, rows)).T
    pieces = []
    for j in range(rows // LANES):
        span = slice(j * LANES, (j + 1) * LANES)
        same = key_seg == query_seg[0:1, span]
        usable = (pad == 1.0) | (key_at == query_at[0:1, span])
        pieces.append(jnp.where(same & usable, 0.0, NEG_FILL))
    return jnp.concatenate(pieces, 1)


def halves():
    lane = lax.broadcasted_iota(jnp.int32, (1, LANES), 1)
    left = (lane < HEAD).astype(F32)
    return left.astype(LOW), (1.0 - left).astype(LOW)


def fetch(sources, targets, sems):
    copies = [pltpu.make_async_copy(source, target, sems.at[i]) for i, (source, target) in enumerate(zip(sources, targets))]
    for copy in copies:
        copy.start()
    return copies


def attend(
    blocks, x_hbm, w_hbm, b_ref, lengths_ref, pad_ref, qkv_hbm, ctx_hbm, lse_ref, *rest
):
    wide_refs, (x_ref, w_ref, qkv_ref, ctx_ref, sems) = rest[:-5], rest[-5:]
    rows = x_ref.shape[0]
    local = w_ref.shape[2]
    scale = float(HEAD) ** (-0.5)
    came = fetch([x_hbm] + [w_hbm.at[i] for i in range(3)], [x_ref] + [w_ref.at[i] for i in range(3)], sems)
    bias = key_mask(lengths_ref, pad_ref, rows)
    sides = halves()
    came[0].wait()
    x = x_ref[...]
    came[1].wait()
    qkv_ref[:, 0:local] = ((dot(x, w_ref[0]) + b_ref[0:1, :].astype(F32)) * scale).astype(LOW)
    came[2].wait()
    qkv_ref[:, local : 2 * local] = dot(x, w_ref[1]).astype(LOW)
    came[3].wait()
    qkv_ref[:, 2 * local :] = (dot(x, w_ref[2]) + b_ref[1:2, :].astype(F32)).astype(LOW)
    saved = pltpu.make_async_copy(qkv_ref, qkv_hbm, sems.at[4])
    saved.start()
    for pair in range(local // LANES):
        at = pair * LANES
        span = slice(at, at + LANES)
        query = qkv_ref[:, span]
        keys = qkv_ref[:, local + at : local + at + LANES]
        flipped = qkv_ref[:, 2 * local + at : 2 * local + at + LANES].T
        parts = []
        for side in range(2):
            scores = dot_nt(keys * sides[side], query) + bias
            top = jnp.max(scores, 0, keepdims=True)
            expo = jnp.exp(scores - top)
            total = jnp.sum(expo, 0, keepdims=True)
            probs = (expo * (1.0 / total)).astype(LOW)
            parts.append(dot(flipped[side * HEAD : (side + 1) * HEAD], probs))
            head = 2 * pair + side
            lse_ref[head : head + 1, :] = top + jnp.log(total)
        context = jnp.concatenate(parts, 0).T.astype(LOW)
        ctx_ref[:, span] = context
        start = 0
        for wide_ref, size in zip(wide_refs, blocks):
            wide_ref[:, span] = context[start : start + size].astype(F32)
            start += size
    kept = pltpu.make_async_copy(ctx_ref, ctx_hbm, sems.at[5])
    kept.start()
    saved.wait()
    kept.wait()


def relay(in_ref, *refs):
    vectors = refs[:6]
    out_ref, vec_ref = refs[-2:]
    out_ref[...] = in_ref[...]
    vec_ref[...] = jnp.zeros(vec_ref.shape, F32)
    for i, ref in enumerate(vectors):
        vec_ref[i : i + 1, :] = ref[...].astype(F32).reshape(1, -1)


def norm_rows(value):
    centered = value - jnp.mean(value, -1, keepdims=True)
    inverse = lax.rsqrt(jnp.mean(centered * centered, -1, keepdims=True) + EPS_NORM)
    return centered * inverse, inverse


def norm_back(grad, normed, inverse, gain):
    scaled = grad * gain
    return inverse * (
        scaled
        - jnp.mean(scaled, -1, keepdims=True)
        - normed * jnp.mean(scaled * normed, -1, keepdims=True)
    )


def row(ref):
    return ref[...].astype(F32)


def feed(taken, tile, far_parts, streamed, place_ref, x_hbm, own_hbm, far_hbm, w_own_hbm, w_near_hbm, *refs):
    w_fars, refs = refs[:far_parts], refs[far_parts:]
    vec_hbm, b_up_ref, w_up, w_down, normed_ref, inverse_ref, low_ref, act_ref, pre_ref, part_ref = refs[:10]
    x_ref, far_ref, vec_ref, w_far, w_full, ctx_full, sems = refs[10:17]
    local = own_hbm.shape[1]
    half = w_near_hbm.shape[0]
    piece = half // far_parts
    hidden = w_up.shape[1]
    core, side = place_ref[0], place_ref[1]
    here = pl.multiple_of(side * local, LANES)
    there = pl.multiple_of((1 - side) * local, LANES)
    spans = [slice(at, at + tile) for at in range(0, hidden, tile)]
    sources = [w_near_hbm] + list(w_fars) + [w_own_hbm, own_hbm.at[taken], far_hbm, x_hbm.at[taken], vec_hbm]
    targets = [w_far.at[0]] + [w_far.at[1, i * piece : (i + 1) * piece] for i in range(far_parts)]
    targets += [w_full.at[pl.ds(here, local)], ctx_full.at[:, pl.ds(here, local)], far_ref, x_ref, vec_ref]
    needed = len(sources)
    if streamed:
        w_up_vmem, w_down_vmem = refs[17:]
        for span in spans:
            sources += [w_up.at[:, span], w_down.at[span]]
            targets += [w_up_vmem.at[:, span], w_down_vmem.at[span]]
        w_up, w_down = w_up_vmem, w_down_vmem
    came = fetch(sources, targets, sems)
    for copy in came[:needed]:
        copy.wait()
    for i in range(2):
        at = pl.multiple_of(there + (core ^ i) * half, 16)
        w_full[pl.ds(at, half), :] = w_far[i].astype(LOW)
    ctx_full[:, pl.ds(there, local)] = far_ref[...].astype(LOW)
    attn = dot(ctx_full[...], w_full[...])
    normed, inverse = norm_rows(x_ref[...].astype(F32) + attn + vec_ref[0:1, :])
    normed_ref[...] = normed
    inverse_ref[...] = jnp.broadcast_to(inverse, inverse_ref.shape)
    low = (normed * vec_ref[1:2, :] + vec_ref[2:3, :]).astype(LOW)
    low_ref[...] = low
    b_up = b_up_ref[...].astype(F32).reshape(1, -1)
    for i, span in enumerate(spans):
        if streamed:
            came[needed + 2 * i].wait()
        pre = dot(low, w_up[:, span]) + b_up[:, span]
        share = 0.5 * (1.0 + lax.erf(pre * 0.7071067811865476))
        act = (pre * share).astype(LOW)
        act_ref[:, span] = act
        pre_ref[:, span] = pre
        if streamed:
            came[needed + 2 * i + 1].wait()
        added = dot(act, w_down[span, :])
        if i == 0:
            part_ref[...] = added
        else:
            part_ref[...] += added


def slopes(pre_ref, out_ref):
    pre = pre_ref[...]
    share = 0.5 * (1.0 + lax.erf(pre * 0.7071067811865476))
    out_ref[...] = share + pre * jnp.exp(-0.5 * pre * pre) * 0.3989422804014327


def feed_back(
    taken, tile, own_ref, far_ref, normed_ref, slope_ref, vec_hbm, up_hbm, w_up, w_down,
    out_ref, grad_ref, low_ref, pre_ref, part_ref, sums_ref, b_up_ref,
    vec_ref, up_ref, sems,
):
    hidden = w_up.shape[1]
    spans = [slice(at, at + tile) for at in range(0, hidden, tile)]
    came = fetch([up_hbm.at[taken], vec_hbm], [up_ref, vec_ref], sems)
    came[1].wait()
    hidden_rows = normed_ref[...] * vec_ref[1:2, :] + vec_ref[2:3, :]
    normed, inverse = norm_rows(hidden_rows + (own_ref[...] + far_ref[...]) + vec_ref[3:4, :])
    gain = vec_ref[4:5, :]
    out_ref[...] = (normed * gain + vec_ref[5:6, :]).astype(LOW)
    came[0].wait()
    upstream = up_ref[...].astype(F32)
    grad = norm_back(upstream, normed, inverse, gain)
    grad_ref[...] = grad
    low = grad.astype(LOW)
    low_ref[...] = low
    sums_ref[0:1, :] = jnp.sum(upstream * normed, 0, keepdims=True)
    sums_ref[1:2, :] = jnp.sum(upstream, 0, keepdims=True)
    sums_ref[2:3, :] = jnp.sum(grad, 0, keepdims=True)
    sums_ref[3:8, :] = jnp.zeros((5, sums_ref.shape[1]), F32)
    for i, span in enumerate(spans):
        pre = (dot_nt(low, w_down[span, :]) * slope_ref[:, span]).astype(LOW)
        pre_ref[:, span] = pre
        b_up_ref[:, span] = jnp.broadcast_to(jnp.sum(pre.astype(F32), 0, keepdims=True), (8, tile))
        added = dot_nt(pre, w_up[:, span])
        if i == 0:
            part_ref[...] = added
        else:
            part_ref[...] += added


def norm_one_back(own_dr2, own_ref, far_ref, normed_ref, inverse_ref, sums_ref, b_up_ref, vec_ref, *refs):
    before, (dr1_ref, low_ref, bias_ref) = refs[:-3], refs[-3:]
    width = dr1_ref.shape[1]
    grad = own_dr2[...] + (own_ref[...] + far_ref[...])
    norm = normed_ref[...]
    dr1 = norm_back(grad, norm, inverse_ref[:, 0:1], vec_ref[1:2, :])
    dr1_ref[...] = dr1
    low_ref[...] = dr1.astype(LOW)
    bias_ref[...] = before[0][...] if before else jnp.zeros(bias_ref.shape, F32)
    bias_ref[0:3, 0:width] += sums_ref[0:3]
    for i, value in enumerate((grad * norm, grad, dr1)):
        bias_ref[3 + i : 4 + i, 0:width] += jnp.sum(value, 0, keepdims=True)
    bias_ref[6:7, 0 : b_up_ref.shape[1]] += b_up_ref[0:1, :]


def attend_back(
    count, *refs,
):
    attend_back_body(refs[:count], *refs[count:])


def attend_back_body(
    low_refs, w_hbm, qkv_hbm, ctx_hbm, lse_ref, lengths_ref, pad_ref, so_far_ref, e_ref, bias_ref,
    w_ref, qkv_ref, sems,
):
    rows, local = ctx_hbm.shape
    came = fetch([w_hbm, qkv_hbm, ctx_hbm], [w_ref, qkv_ref, e_ref.at[:, 3 * local : 4 * local]], sems)
    scale = float(HEAD) ** (-0.5)
    bias_ref[...] = so_far_ref[...]
    mask = key_mask(lengths_ref, pad_ref, rows)
    sides = halves()
    came[0].wait()
    d_ctx = dot_nt(jnp.concatenate([ref[...] for ref in low_refs], 0), w_ref[...]).astype(LOW)
    came[1].wait()
    for pair in range(local // LANES):
        at = pair * LANES
        span = slice(at, at + LANES)
        query = qkv_ref[:, span]
        keys = qkv_ref[:, local + at : local + at + LANES]
        values = qkv_ref[:, 2 * local + at : 2 * local + at + LANES]
        grads = d_ctx[:, span]
        flipped = keys.T
        d_q = []
        d_k = jnp.zeros((rows, LANES), F32)
        d_v = jnp.zeros((rows, LANES), F32)
        for side in range(2):
            head = 2 * pair + side
            scores = dot_nt(keys * sides[side], query) + mask
            probs = jnp.exp(scores - lse_ref[head : head + 1, :])
            d_p = dot_nt(values * sides[side], grads)
            mixed = jnp.sum(probs * d_p, 0, keepdims=True)
            d_s = (probs * (d_p - mixed)).astype(LOW)
            d_k = d_k + dot(d_s, query * sides[side])
            d_v = d_v + dot(probs.astype(LOW), grads * sides[side])
            d_q.append(dot(flipped[side * HEAD : (side + 1) * HEAD], d_s))
        d_query = jnp.concatenate(d_q, 0).T.astype(LOW).astype(F32) * scale
        d_k = d_k.astype(LOW)
        d_v = d_v.astype(LOW)
        e_ref[:, at : at + LANES] = d_query.astype(LOW)
        e_ref[:, local + at : local + at + LANES] = d_k
        e_ref[:, 2 * local + at : 2 * local + at + LANES] = d_v
        bias_ref[7:8, at : at + LANES] = jnp.sum(d_query, 0, keepdims=True)
        bias_ref[7:8, local + at : local + at + LANES] = jnp.sum(d_v.astype(F32), 0, keepdims=True)
    came[2].wait()


def place_blocks(me, source, target, order, size):
    for i, block in enumerate(order):
        at = pl.multiple_of((me ^ block) * size, size)
        target[i * size : (i + 1) * size, :] = source[pl.ds(at, size), :]


def outer(order, size, splits, kinds, more, rides, place_ref, *refs):
    count = len(splits)
    sides = max(kinds) + 1
    lefts = [refs[:count]] + ([refs[count : count + more]] if more else [])
    rights = refs[count + more : 2 * count + more]
    rider = refs[2 * count + more] if rides else None
    *sent_refs, keep_ref, flipped, placed = refs[2 * count + more + rides :]
    step = pl.program_id(0)

    @pl.when(step == 0)
    def _():
        for index, group in enumerate(lefts):
            source = jnp.concatenate([ref[...] for ref in group], 0).T
            if order is None:
                placed[index] = source
            else:
                flipped[...] = source
                place_blocks(place_ref[2], flipped, placed.at[index], order, size)

    left = placed[0]
    if sides > 1:
        change = kinds.index(1)
        left = placed[jnp.where(step >= change, 1, 0)]
    right = jnp.concatenate([ref[...] for ref in rights], 0)
    half = left.shape[0] // 2
    part = half // len(sent_refs)
    for i, ref in enumerate(sent_refs):
        ref[0:part, :] = dot(left[i * part : (i + 1) * part], right)
    keep_ref[0:half, :] = dot(left[half:], right)
    if rides:
        sent_refs[-1][part:, :] = rider[...]
        keep_ref[half:, :] = rider[...]


def fold(*refs):
    value = refs[0][...]
    for ref in refs[1:-1]:
        value = value + ref[...]
    refs[-1][...] = value


def fold_blocks(counts, *refs):
    out_ref = refs[-1]
    at = start = 0
    for count in counts:
        value = refs[at][...]
        for ref in refs[at + 1 : at + count]:
            value = value + ref[...]
        end = start + value.shape[0]
        out_ref[start:end, :] = value
        at += count
        start = end


def back_tokens(e_ref, w_hbm, out_ref, w_ref, sems):
    local = w_ref.shape[2]
    came = fetch([w_hbm.at[i] for i in range(3)], [w_ref.at[i] for i in range(3)], sems)
    for i in range(3):
        came[i].wait()
        added = dot_nt(e_ref[:, i * local : (i + 1) * local], w_ref[i])
        if i == 0:
            out_ref[...] = added
        else:
            out_ref[...] += added


def join(own_ref, far_ref, *refs):
    out_ref, start = refs[-1], 0
    for ref in refs[:-1]:
        span = slice(start, start + ref.shape[0])
        out_ref[span, :] = ref[...] + (own_ref[span, :] + far_ref[span, :])
        start += ref.shape[0]


def spread(local, *refs):
    qkv_ref, out_ref = refs[-2:]
    value = refs[0][...]
    for ref in refs[1:-2]:
        value = value + ref[...]
    for i in range(3):
        qkv_ref[i] = value[:, i * local : (i + 1) * local]
    out_ref[...] = value[:, 3 * local :]


def chained(kernel, inputs, outputs):
    def body(*refs):
        refs[1 + inputs + outputs][...] = jnp.zeros((8, LANES), F32)
        kernel(*refs[1 : 1 + inputs + outputs], *refs[2 + inputs + outputs :])

    return body


def on_device(
    tokens, lengths, pad_mask, w_qkv, b_qv, w_out, b_out, ln1_gain, ln1_bias,
    w_up, b_up, w_down, b_down, ln2_gain, ln2_bias, cotangent,
):
    rows, width = tokens.shape
    local = w_qkv.shape[2]
    heads = local // HEAD
    hidden = w_up.shape[1]
    ranks = lax.axis_size("dp")
    me = lax.axis_index("dp").astype(jnp.int32)
    place_arr = jnp.stack([me % 2, lax.axis_index("tp").astype(jnp.int32), me])
    size = width // ranks
    blocks = [rows // 2] * 2 if rows % 32 == 0 else [rows]
    starts = [sum(blocks[:i]) for i in range(len(blocks))]
    lse_rows = -(-heads // 8) * 8
    shape = jax.ShapeDtypeStruct
    smem = pl.BlockSpec(memory_space=pltpu.SMEM)
    loose = pl.BlockSpec(memory_space=pl.ANY)
    far_off = pl.BlockSpec(memory_space=pltpu.HBM)
    dma = pltpu.SemaphoreType.DMA
    mark = [None]
    pace = [10**10]

    def call(kernel, name, operands, in_specs, out_shape, out_specs, grid=(1,), scratch=(), limit=24, flops=None):
        before = mark[0] if mark[0] is not None else operands[0]
        operands = [
            pltpu.with_memory_space_constraint(operand, pltpu.HBM) if spec is far_off else operand
            for operand, spec in zip(operands, in_specs)
        ]
        *outs, mark[0] = pl.pallas_call(
            chained(kernel, len(operands), len(out_shape)),
            grid=grid,
            out_shape=tuple(out_shape) + (shape((8, LANES), F32),),
            in_specs=[loose] + list(in_specs),
            out_specs=tuple(out_specs) + (whole((8, LANES)),),
            scratch_shapes=list(scratch),
            compiler_params=params(limit),
            cost_estimate=cost(pace[0] if flops is None else flops),
            name=name,
        )(before, *operands)
        return outs

    def full(*arrays):
        return [whole(array.shape) for array in arrays]

    def swap_tp(array):
        pairs = [(i, i ^ 1) for i in range(lax.axis_size("tp"))]
        return lax.ppermute(array, "tp", pairs)

    def swap_dp(array, bits):
        return lax.ppermute(array, "dp", [(i, i ^ bits) for i in range(ranks)])

    stages = []
    while 1 << len(stages) < ranks:
        stages.append(1 << len(stages))
    order = [0]
    for bit in reversed(stages):
        order = order + [bit + rest for rest in order]
    order = order[ranks // 2 :] + order[: ranks // 2]
    fused = size % 16 == 0
    pad_row = pad_mask
    half = w_out.shape[0] // 2
    w_near = swap_tp(lax.dynamic_slice_in_dim(w_out, (me % 2) * half, half, 0).astype(F32))
    outs = [shape((rows, 3 * local), LOW), shape((rows, local), LOW), shape((lse_rows, rows), F32)]
    outs += [shape((block, local), F32) for block in blocks]
    qkv, context, lse, *wides = call(
        functools.partial(attend, blocks), "attend", [tokens, w_qkv, b_qv, lengths, pad_row],
        [far_off] * 2 + full(b_qv) + [smem] + full(pad_row), outs, [far_off] * 2 + full(*outs[2:]),
        scratch=[
            pltpu.VMEM((rows, width), LOW),
            pltpu.VMEM((3, width, local), LOW),
            pltpu.VMEM((rows, 3 * local), LOW),
            pltpu.VMEM((rows, local), LOW),
            dma((6,)),
        ],
        limit=56,
    )
    fars = [swap_tp(wide) for wide in wides]
    near = pl.BlockSpec(memory_space=pltpu.VMEM)
    params_of = [b_out, ln1_gain, ln1_bias, b_down, ln2_gain, ln2_bias]
    outs = [shape(w_near.shape, F32), shape((8, width), F32)]
    w_near, vectors = call(
        relay, "relay", [w_near, *params_of], full(w_near, *params_of), outs, full(*outs)
    )
    far_parts = 3 if half % 48 == 0 else 1
    piece = half // far_parts
    w_fars = [swap_dp(w_near[i * piece : (i + 1) * piece], 1) for i in range(far_parts)]

    tile = min(hidden, 512)
    tiles = hidden // tile

    def columns(height, step):
        return pl.BlockSpec((height, step), lambda f: (0, f))

    saved = []
    for begin, block, far in zip(starts, blocks, fars):
        outs = [
            shape((block, width), F32), shape((block, LANES), F32), shape((block, width), LOW),
            shape((block, hidden), LOW), shape((block, hidden), F32), shape((block, width), F32),
        ]
        outs = call(
            functools.partial(feed, slice(begin, begin + block), tile, far_parts, begin == 0), "feed",
            [place_arr, tokens, context, far, w_out, w_near, *w_fars, vectors, b_up, w_up, w_down],
            [smem] + [far_off] * (6 + far_parts) + full(b_up) + [far_off if begin == 0 else near] * 2,
            outs, full(*outs),
            scratch=[
                pltpu.VMEM((block, width), LOW),
                pltpu.VMEM((block, local), F32),
                pltpu.VMEM((8, width), F32),
                pltpu.VMEM((2, half, width), F32),
                pltpu.VMEM((2 * local, width), LOW),
                pltpu.VMEM((block, 2 * local), LOW),
                dma((6 + far_parts + 2 * tiles,)),
            ]
            + ([pltpu.VMEM((width, hidden), LOW), pltpu.VMEM((hidden, width), LOW)] if begin == 0 else []),
        )
        saved.append(outs + [swap_tp(outs[5])])

    slope_of = [
        call(slopes, "slopes", [s[4]], full(s[4]), [shape(s[4].shape, F32)], full(s[4]))[0] for s in saved
    ]
    back = []
    for begin, block, slope, (normed, inverse, low, act, _, own, far) in zip(starts, blocks, slope_of, saved):
        outs = [
            shape((block, width), LOW), shape((block, width), F32), shape((block, width), LOW),
            shape((block, hidden), LOW), shape((block, width), F32), shape((8, width), F32), shape((8, hidden), F32),
        ]
        outs = call(
            functools.partial(feed_back, slice(begin, begin + block), tile), "feed_back",
            [own, far, normed, slope, vectors, cotangent, w_up, w_down],
            full(own, far, normed, slope) + [far_off] * 2 + [near] * 2,
            outs, full(*outs),
            scratch=[pltpu.VMEM((8, width), F32), pltpu.VMEM((block, width), LOW), dma((2,))],
        )
        back.append(outs + [swap_tp(outs[4])])

    layer_out = jnp.concatenate([outs[0] for outs in back], 0)

    def gradient(lefts, rights, splits, kinds, step, rider=None):
        wide = step * len(kinds)
        sides = max(kinds) + 1
        riders = [] if rider is None else [rider]
        outs = [shape((width // 2 + 8 * len(riders), wide), F32)] * 2
        outs = call(
            functools.partial(
                outer, order if fused else None, size, splits, kinds, len(lefts) - len(splits), len(riders)
            ),
            "outer", [place_arr, *lefts, *rights, *riders],
            [smem] + full(*lefts) + [columns(split, step) for split in splits] + [columns(8, step) for _ in riders],
            outs, [columns(out.shape[0], step) for out in outs],
            grid=(len(kinds),),
            scratch=[pltpu.VMEM((width, rows), LOW), pltpu.VMEM((sides, width, rows), LOW)],
        )
        if not fused:
            every = jnp.concatenate([out[: width // 2] for out in outs], 0).reshape(ranks, size, wide)
            every = jnp.take(every, jnp.array(order, jnp.int32) ^ me, axis=0).reshape(width, wide)
            outs = [every[: width // 2], every[width // 2 :]]
            outs = [jnp.concatenate([out] + riders, 0) for out in outs]
        return outs

    class Chunk:
        def __init__(self, outs, came, wide, column, bits, rides=False):
            keep = outs[1]
            self.wide = wide
            self.parts = {p: [(keep, p, column), (came, p, column)] for p in range(ranks // 2)}
            self.alive = list(self.parts)
            self.bits = list(bits)
            self.extra = [(keep, width // 16), (came, width // 16)] if rides else []

        def add(self, places, flops, rides=False):
            wide = self.wide
            if not fused:
                sums = []
                for p in places:
                    found = [
                        array[row * size : (row + 1) * size, column * wide : (column + 1) * wide]
                        for array, row, column in self.parts[p]
                    ]
                    sums.append(functools.reduce(jnp.add, found))
                if rides:
                    sums.append(functools.reduce(jnp.add, [a[8 * row : 8 * row + 8] for a, row in self.extra]))
                return jnp.concatenate(sums, 0)
            operands, specs, counts = [], [], []
            for p in places:
                counts.append(len(self.parts[p]))
                for array, row, column in self.parts[p]:
                    operands.append(array)
                    specs.append(pl.BlockSpec((size, wide), functools.partial(lambda r, c, n: (r, c), row, column)))
            if rides:
                counts.append(len(self.extra))
                for array, row in self.extra:
                    operands.append(array)
                    specs.append(pl.BlockSpec((8, wide), functools.partial(lambda r, n: (r, 0), row)))
            outs = [shape((len(places) * size + (8 if rides else 0), wide), F32)]
            return call(
                functools.partial(fold_blocks, counts), "fold", operands, specs, outs, full(*outs), flops=flops
            )[0]

        def weight(self, bit):
            return ranks // (2 * bit)

        def send(self, places, flops, rides):
            bit = self.bits[0]
            rides = rides and self.extra and len(self.bits) > 1
            came = swap_dp(self.add(places, flops, rides), bit)
            self.arrived = getattr(self, "arrived", [])
            for i, p in enumerate(places):
                self.arrived.append((p ^ self.weight(bit), (came, i, 0)))
            if rides:
                self.extra = self.extra + [(came, len(places) * size // 8)]

        def close(self):
            for p, part in self.arrived:
                self.parts[p].append(part)
            self.arrived = []
            weight = self.weight(self.bits.pop(0))
            self.alive = [p for p in self.alive if not p & weight]

        def leaving(self):
            weight = self.weight(self.bits[0])
            return [p for p in self.alive if p & weight]

        def step(self, flops=None):
            self.send(self.leaving(), flops, True)
            self.close()

        def high(self, flops=None):
            if len(self.bits) == 1:
                self.step(flops)
            else:
                after = self.weight(self.bits[1])
                self.send([p for p in self.leaving() if p & after], flops, True)

        def low(self, flops=None):
            after = self.weight(self.bits[1])
            self.send([p for p in self.leaving() if not p & after], flops, False)
            self.close()

        def rest(self):
            while self.bits:
                self.step()

        def all_but_last(self):
            last = self.parts[0].pop()
            self.parts[0] = [(self.add([0], None), 0, 0), last]

        def last(self, flops=None):
            self.rest()
            return self.add([0], flops)

    def add_extra(extra):
        if not fused:
            return functools.reduce(jnp.add, [a[8 * row : 8 * row + 8] for a, row in extra])
        wide = extra[0][0].shape[1]
        specs = [pl.BlockSpec((8, wide), functools.partial(lambda index, n: (index, 0), row)) for _, row in extra]
        outs = [shape((8, wide), F32)]
        return call(fold, "fold", [array for array, _ in extra], specs, outs, full(*outs))[0]

    straight, turned = stages[1:], stages[2:] + stages[1:2]
    outs = gradient([o[2] for o in back], [s[3] for s in saved], blocks, [0] * tiles, tile)
    came = swap_dp(outs[0], stages[0])
    down = Chunk(outs, came, hidden // 3 * 2, 0, straight)
    early = Chunk(outs, came, hidden // 3, 2, turned)
    wide = 4 * local

    def first_norm(i):
        outs = [shape((blocks[i], width), F32), shape((blocks[i], width), LOW), shape((8, wide), F32)]
        operands = [back[i][1], back[i][4], back[i][7], saved[i][0], saved[i][1], back[i][5], back[i][6], vectors]
        operands += [norms[-1][2]] if norms else []
        flops = 2 * 10**10 if i == 0 else None
        norms.append(call(norm_one_back, "norm_one_back", operands, full(*operands), outs, full(*outs), flops=flops))

    norms = []
    first_norm(0)
    down.high()
    early.step()
    outs = gradient([s[2] for s in saved], [o[3] for o in back], blocks, [0] * tiles, tile)
    up = Chunk(outs, swap_dp(outs[0], stages[0]), hidden, 0, straight)
    down.low()
    pace[0] = 10**10
    early.step()
    down.step(2 * 10**10)
    up.high()
    first_norm(1)
    pace[0] = 10**8
    dr1s, lows = [n[0] for n in norms], [n[1] for n in norms]
    outs = [shape((rows, 4 * local), LOW), shape((8, wide), F32)]
    operands = lows + [w_out, qkv, context, lse, lengths, pad_row, norms[-1][2]]
    e, bias = call(
        functools.partial(attend_back, len(lows)), "attend_back", operands,
        full(*lows) + [far_off] * 3 + full(lse) + [smem] + full(pad_row, norms[-1][2]), outs, full(*outs),
        scratch=[pltpu.VMEM((local, width), LOW), pltpu.VMEM((rows, 3 * local), LOW), dma((3,))],
    )
    up.low()
    outs = gradient([tokens] + lows, [e], [rows], [0, 0, 0, 1], local, bias)
    mixed = Chunk(outs, swap_dp(outs[0], stages[0]), wide, 0, straight, rides=True)

    while early.bits:
        early.step()
    down.step(5 * 10**9)
    up.step(4 * 10**10)
    mixed.high()
    mixed.low()
    outs = [shape((rows, width), F32)]
    (partial,) = call(
        back_tokens, "back_tokens", [e, w_qkv], full(e) + [far_off], outs, full(*outs),
        scratch=[pltpu.VMEM((3, width, local), LOW), dma((3,))],
    )
    pace[0] = 10**9
    partial_far = swap_tp(partial)
    down = down.last(5 * 10**9)
    up.step()
    mixed.high()
    mixed.low()
    up = up.last()
    mixed.rest()
    bias = add_extra(mixed.extra)
    bias_far = swap_dp(bias, stages[-1])
    mixed.all_but_last()
    early = early.last()
    (d_tokens,) = call(
        join, "join", [partial, partial_far] + dr1s, full(partial, partial_far, *dr1s), outs, full(*outs)
    )
    (bias,) = call(fold, "fold", [bias, bias_far], full(bias, bias_far), [shape(bias.shape, F32)], full(bias))
    if fused:
        outs = [shape((3, size, local), F32), shape((size, local), F32)]
        operands = [array for array, _, _ in mixed.parts[0]]
        d_w_qkv, d_w_out = call(
            functools.partial(spread, local), "spread", operands,
            [pl.BlockSpec((size, wide), lambda n: (0, 0))] * len(operands), outs, full(*outs),
        )
    else:
        last = mixed.add([0], None)
        d_w_qkv = last[:, : 3 * local].reshape(size, 3, local).transpose(1, 0, 2)
        d_w_out = last[:, 3 * local :]
    return (
        layer_out,
        d_tokens,
        d_w_qkv,
        bias[7, : 2 * local].reshape(2, local),
        d_w_out.T,
        bias[5, :width],
        bias[3, :width],
        bias[4, :width],
        up,
        bias[6, :hidden],
        jnp.concatenate([down.T, early.T], 0),
        bias[2, :width],
        bias[0, :width],
        bias[1, :width],
    )


def solution(mesh):
    placed = (
        P("dp", None), P("dp", None), P("dp"), P(None, None, "tp"), P(None, "tp"), P("tp", None),
        P(), P(), P(), P(None, "tp"), P("tp"), P("tp", None), P(), P(), P(), P("dp", None),
    )
    return jax.shard_map(
        on_device,
        mesh=mesh,
        in_specs=placed,
        out_specs=(
            P("dp", None), P("dp", None), P(None, "dp", "tp"), P(None, "tp"), P("tp", "dp"), P(), P(), P(),
            P("dp", "tp"), P("tp"), P("tp", "dp"), P(), P(), P(),
        ),
        check_vma=False,
    )
```

```python
import functools

import jax
import jax.numpy as jnp
from jax import lax
from jax.experimental import pallas as pl
from jax.experimental.pallas import tpu as pltpu
from jax.sharding import PartitionSpec as P

HEAD = 64
NEG_FILL = -1e30
EPS_NORM = 1e-12
LANES = 128
F32 = jnp.float32
LOW = jnp.bfloat16
MIB = 1 << 20


def dot(a, b):
    return lax.dot_general(a, b, (((1,), (0,)), ((), ())), preferred_element_type=F32)


def dot_nt(a, b):
    return lax.dot_general(a, b, (((1,), (1,)), ((), ())), preferred_element_type=F32)


def whole(shape):
    return pl.BlockSpec(shape, lambda *_: (0,) * len(shape))


def params(limit):
    return pltpu.CompilerParams(vmem_limit_bytes=limit * MIB)


def cost(flops):
    return pl.CostEstimate(flops=flops, bytes_accessed=10**6, transcendentals=0)


def key_mask(lengths_ref, pad_ref, rows):
    seqs = lengths_ref.shape[1]
    key_at = lax.broadcasted_iota(jnp.int32, (rows, LANES), 0)
    query_at = lax.broadcasted_iota(jnp.int32, (8, rows), 1)
    key_seg = jnp.zeros((rows, LANES), jnp.int32)
    query_seg = jnp.zeros((8, rows), jnp.int32)
    end = jnp.int32(0)
    for i in range(seqs):
        end = end + lengths_ref[0, i]
        key_seg = key_seg + (key_at >= end).astype(jnp.int32)
        query_seg = query_seg + (query_at >= end).astype(jnp.int32)
    pad = jnp.broadcast_to(pad_ref[...].astype(F32).reshape(1, rows), (LANES, rows)).T
    pieces = []
    for j in range(rows // LANES):
        span = slice(j * LANES, (j + 1) * LANES)
        same = key_seg == query_seg[0:1, span]
        usable = (pad == 1.0) | (key_at == query_at[0:1, span])
        pieces.append(jnp.where(same & usable, 0.0, NEG_FILL))
    return jnp.concatenate(pieces, 1)


def halves():
    lane = lax.broadcasted_iota(jnp.int32, (1, LANES), 1)
    left = (lane < HEAD).astype(F32)
    return left.astype(LOW), (1.0 - left).astype(LOW)


def fetch(sources, targets, sems):
    copies = [pltpu.make_async_copy(source, target, sems.at[i]) for i, (source, target) in enumerate(zip(sources, targets))]
    for copy in copies:
        copy.start()
    return copies


def attend(
    blocks, x_hbm, w_hbm, b_ref, lengths_ref, pad_ref, qkv_hbm, ctx_hbm, lse_ref, *rest
):
    wide_refs, (x_ref, w_ref, qkv_ref, ctx_ref, sems) = rest[:-5], rest[-5:]
    rows = x_ref.shape[0]
    local = w_ref.shape[2]
    scale = float(HEAD) ** (-0.5)
    came = fetch([x_hbm] + [w_hbm.at[i] for i in range(3)], [x_ref] + [w_ref.at[i] for i in range(3)], sems)
    bias = key_mask(lengths_ref, pad_ref, rows)
    sides = halves()
    came[0].wait()
    x = x_ref[...]
    came[1].wait()
    qkv_ref[:, 0:local] = ((dot(x, w_ref[0]) + b_ref[0:1, :].astype(F32)) * scale).astype(LOW)
    came[2].wait()
    qkv_ref[:, local : 2 * local] = dot(x, w_ref[1]).astype(LOW)
    came[3].wait()
    qkv_ref[:, 2 * local :] = (dot(x, w_ref[2]) + b_ref[1:2, :].astype(F32)).astype(LOW)
    saved = pltpu.make_async_copy(qkv_ref, qkv_hbm, sems.at[4])
    saved.start()
    for pair in range(local // LANES):
        at = pair * LANES
        span = slice(at, at + LANES)
        query = qkv_ref[:, span]
        keys = qkv_ref[:, local + at : local + at + LANES]
        flipped = qkv_ref[:, 2 * local + at : 2 * local + at + LANES].T
        parts = []
        for side in range(2):
            scores = dot_nt(keys * sides[side], query) + bias
            top = jnp.max(scores, 0, keepdims=True)
            expo = jnp.exp(scores - top)
            total = jnp.sum(expo, 0, keepdims=True)
            probs = (expo * (1.0 / total)).astype(LOW)
            parts.append(dot(flipped[side * HEAD : (side + 1) * HEAD], probs))
            head = 2 * pair + side
            lse_ref[head : head + 1, :] = top + jnp.log(total)
        context = jnp.concatenate(parts, 0).T.astype(LOW)
        ctx_ref[:, span] = context
        start = 0
        for wide_ref, size in zip(wide_refs, blocks):
            wide_ref[:, span] = context[start : start + size].astype(F32)
            start += size
    kept = pltpu.make_async_copy(ctx_ref, ctx_hbm, sems.at[5])
    kept.start()
    saved.wait()
    kept.wait()


def relay(in_ref, *refs):
    vectors = refs[:6]
    out_ref, vec_ref = refs[-2:]
    out_ref[...] = in_ref[...]
    vec_ref[...] = jnp.zeros(vec_ref.shape, F32)
    for i, ref in enumerate(vectors):
        vec_ref[i : i + 1, :] = ref[...].astype(F32).reshape(1, -1)


def norm_rows(value):
    centered = value - jnp.mean(value, -1, keepdims=True)
    inverse = lax.rsqrt(jnp.mean(centered * centered, -1, keepdims=True) + EPS_NORM)
    return centered * inverse, inverse


def norm_back(grad, normed, inverse, gain):
    scaled = grad * gain
    return inverse * (
        scaled
        - jnp.mean(scaled, -1, keepdims=True)
        - normed * jnp.mean(scaled * normed, -1, keepdims=True)
    )


def row(ref):
    return ref[...].astype(F32)


def gather(far_parts, place_ref, w_own_hbm, w_near_ref, *refs):
    w_fars, (out_ref, sems) = refs[:far_parts], refs[far_parts:]
    local = w_own_hbm.shape[0]
    half = w_near_ref.shape[0]
    core, side = place_ref[0], place_ref[1]
    here = pl.multiple_of(side * local, LANES)
    there = pl.multiple_of((1 - side) * local, LANES)
    (came,) = fetch([w_own_hbm], [out_ref.at[pl.ds(here, local)]], sems)
    out_ref[pl.ds(pl.multiple_of(there + core * half, 16), half), :] = w_near_ref[...].astype(LOW)
    at = there + (1 - core) * half
    for ref in w_fars:
        size = ref.shape[0]
        out_ref[pl.ds(pl.multiple_of(at, 16), size), :] = ref[...].astype(LOW)
        at = at + size
    came.wait()


def feed(taken, tile, streamed, place_ref, far_ref, w_full, x_hbm, own_hbm, *refs):
    vec_hbm, b_up_ref, w_up, w_down = refs[:4]
    normed_ref, inverse_ref, low_ref, act_ref, pre_ref, part_ref, base_ref = refs[4:11]
    x_ref, vec_ref, ctx_full, sems = refs[11:15]
    local = own_hbm.shape[1]
    hidden = w_up.shape[1]
    side = place_ref[1]
    here = pl.multiple_of(side * local, LANES)
    there = pl.multiple_of((1 - side) * local, LANES)
    spans = [slice(at, at + tile) for at in range(0, hidden, tile)]
    sources = [own_hbm.at[taken], x_hbm.at[taken], vec_hbm]
    targets = [ctx_full.at[:, pl.ds(here, local)], x_ref, vec_ref]
    needed = len(sources)
    if streamed:
        w_up_vmem, w_down_vmem = refs[15:]
        for span in spans:
            sources += [w_up.at[:, span], w_down.at[span]]
            targets += [w_up_vmem.at[:, span], w_down_vmem.at[span]]
        w_up, w_down = w_up_vmem, w_down_vmem
    came = fetch(sources, targets, sems)
    ctx_full[:, pl.ds(there, local)] = far_ref[...].astype(LOW)
    for copy in came[:needed]:
        copy.wait()
    attn = dot(ctx_full[...], w_full[...])
    normed, inverse = norm_rows(x_ref[...].astype(F32) + attn + vec_ref[0:1, :])
    normed_ref[...] = normed
    inverse_ref[...] = jnp.broadcast_to(inverse, inverse_ref.shape)
    hidden_rows = normed * vec_ref[1:2, :] + vec_ref[2:3, :]
    base_ref[...] = hidden_rows + vec_ref[3:4, :]
    low = hidden_rows.astype(LOW)
    low_ref[...] = low
    b_up = b_up_ref[...].astype(F32).reshape(1, -1)
    for i, span in enumerate(spans):
        if streamed:
            came[needed + 2 * i].wait()
        pre = dot(low, w_up[:, span]) + b_up[:, span]
        share = 0.5 * (1.0 + lax.erf(pre * 0.7071067811865476))
        act = (pre * share).astype(LOW)
        act_ref[:, span] = act
        pre_ref[:, span] = pre
        if streamed:
            came[needed + 2 * i + 1].wait()
        added = dot(act, w_down[span, :])
        if i == 0:
            part_ref[...] = added
        else:
            part_ref[...] += added


def slopes(pre_ref, out_ref):
    pre = pre_ref[...]
    share = 0.5 * (1.0 + lax.erf(pre * 0.7071067811865476))
    out_ref[...] = share + pre * jnp.exp(-0.5 * pre * pre) * 0.3989422804014327


def feed_back(
    taken, tile, own_ref, far_ref, base_ref, slope_ref, vec_hbm, up_hbm, w_up, w_down,
    out_ref, grad_ref, low_ref, pre_ref, part_ref, sums_ref, b_up_ref,
    vec_ref, up_ref, sems,
):
    hidden = w_up.shape[1]
    spans = [slice(at, at + tile) for at in range(0, hidden, tile)]
    came = fetch([up_hbm.at[taken], vec_hbm], [up_ref, vec_ref], sems)
    normed, inverse = norm_rows(base_ref[...] + (own_ref[...] + far_ref[...]))
    came[1].wait()
    gain = vec_ref[4:5, :]
    out_ref[...] = (normed * gain + vec_ref[5:6, :]).astype(LOW)
    came[0].wait()
    upstream = up_ref[...].astype(F32)
    grad = norm_back(upstream, normed, inverse, gain)
    grad_ref[...] = grad
    low = grad.astype(LOW)
    low_ref[...] = low
    sums_ref[0:1, :] = jnp.sum(upstream * normed, 0, keepdims=True)
    sums_ref[1:2, :] = jnp.sum(upstream, 0, keepdims=True)
    sums_ref[2:3, :] = jnp.sum(grad, 0, keepdims=True)
    sums_ref[3:8, :] = jnp.zeros((5, sums_ref.shape[1]), F32)
    for i, span in enumerate(spans):
        pre = (dot_nt(low, w_down[span, :]) * slope_ref[:, span]).astype(LOW)
        pre_ref[:, span] = pre
        b_up_ref[:, span] = jnp.broadcast_to(jnp.sum(pre.astype(F32), 0, keepdims=True), (8, tile))
        added = dot_nt(pre, w_up[:, span])
        if i == 0:
            part_ref[...] = added
        else:
            part_ref[...] += added


def norm_one_back(own_dr2, own_ref, far_ref, normed_ref, inverse_ref, sums_ref, b_up_ref, vec_ref, *refs):
    before, (dr1_ref, low_ref, bias_ref) = refs[:-3], refs[-3:]
    width = dr1_ref.shape[1]
    grad = own_dr2[...] + (own_ref[...] + far_ref[...])
    norm = normed_ref[...]
    dr1 = norm_back(grad, norm, inverse_ref[:, 0:1], vec_ref[1:2, :])
    dr1_ref[...] = dr1
    low_ref[...] = dr1.astype(LOW)
    bias_ref[...] = before[0][...] if before else jnp.zeros(bias_ref.shape, F32)
    bias_ref[0:3, 0:width] += sums_ref[0:3]
    for i, value in enumerate((grad * norm, grad, dr1)):
        bias_ref[3 + i : 4 + i, 0:width] += jnp.sum(value, 0, keepdims=True)
    bias_ref[6:7, 0 : b_up_ref.shape[1]] += b_up_ref[0:1, :]


def attend_back(
    count, *refs,
):
    attend_back_body(refs[:count], *refs[count:])


def attend_back_body(
    low_refs, w_hbm, qkv_hbm, ctx_hbm, lse_ref, lengths_ref, pad_ref, so_far_ref, e_ref, bias_ref,
    w_ref, qkv_ref, sems,
):
    rows, local = ctx_hbm.shape
    came = fetch([w_hbm, qkv_hbm, ctx_hbm], [w_ref, qkv_ref, e_ref.at[:, 3 * local : 4 * local]], sems)
    scale = float(HEAD) ** (-0.5)
    bias_ref[...] = so_far_ref[...]
    mask = key_mask(lengths_ref, pad_ref, rows)
    sides = halves()
    came[0].wait()
    d_ctx = dot_nt(jnp.concatenate([ref[...] for ref in low_refs], 0), w_ref[...]).astype(LOW)
    came[1].wait()
    for pair in range(local // LANES):
        at = pair * LANES
        span = slice(at, at + LANES)
        query = qkv_ref[:, span]
        keys = qkv_ref[:, local + at : local + at + LANES]
        values = qkv_ref[:, 2 * local + at : 2 * local + at + LANES]
        grads = d_ctx[:, span]
        flipped = keys.T
        d_q = []
        d_k = jnp.zeros((rows, LANES), F32)
        d_v = jnp.zeros((rows, LANES), F32)
        for side in range(2):
            head = 2 * pair + side
            scores = dot_nt(keys * sides[side], query) + mask
            probs = jnp.exp(scores - lse_ref[head : head + 1, :])
            d_p = dot_nt(values * sides[side], grads)
            mixed = jnp.sum(probs * d_p, 0, keepdims=True)
            d_s = (probs * (d_p - mixed)).astype(LOW)
            d_k = d_k + dot(d_s, query * sides[side])
            d_v = d_v + dot(probs.astype(LOW), grads * sides[side])
            d_q.append(dot(flipped[side * HEAD : (side + 1) * HEAD], d_s))
        d_query = jnp.concatenate(d_q, 0).T.astype(LOW).astype(F32) * scale
        d_k = d_k.astype(LOW)
        d_v = d_v.astype(LOW)
        e_ref[:, at : at + LANES] = d_query.astype(LOW)
        e_ref[:, local + at : local + at + LANES] = d_k
        e_ref[:, 2 * local + at : 2 * local + at + LANES] = d_v
        bias_ref[7:8, at : at + LANES] = jnp.sum(d_query, 0, keepdims=True)
        bias_ref[7:8, local + at : local + at + LANES] = jnp.sum(d_v.astype(F32), 0, keepdims=True)
    came[2].wait()


def place_blocks(me, source, target, order, size):
    for i, block in enumerate(order):
        at = pl.multiple_of((me ^ block) * size, size)
        target[i * size : (i + 1) * size, :] = source[pl.ds(at, size), :]


def outer(order, size, splits, kinds, more, rides, place_ref, *refs):
    count = len(splits)
    sides = max(kinds) + 1
    lefts = [refs[:count]] + ([refs[count : count + more]] if more else [])
    rights = refs[count + more : 2 * count + more]
    rider = refs[2 * count + more] if rides else None
    *sent_refs, keep_ref, flipped, placed = refs[2 * count + more + rides :]
    step = pl.program_id(0)

    @pl.when(step == 0)
    def _():
        for index, group in enumerate(lefts):
            source = jnp.concatenate([ref[...] for ref in group], 0).T
            if order is None:
                placed[index] = source
            else:
                flipped[...] = source
                place_blocks(place_ref[2], flipped, placed.at[index], order, size)

    left = placed[0]
    if sides > 1:
        change = kinds.index(1)
        left = placed[jnp.where(step >= change, 1, 0)]
    right = jnp.concatenate([ref[...] for ref in rights], 0)
    half = left.shape[0] // 2
    part = half // len(sent_refs)
    for i, ref in enumerate(sent_refs):
        ref[0:part, :] = dot(left[i * part : (i + 1) * part], right)
    keep_ref[0:half, :] = dot(left[half:], right)
    if rides:
        sent_refs[-1][part:, :] = rider[...]
        keep_ref[half:, :] = rider[...]


def fold(*refs):
    value = refs[0][...]
    for ref in refs[1:-1]:
        value = value + ref[...]
    refs[-1][...] = value


def fold_blocks(counts, *refs):
    out_ref = refs[-1]
    at = start = 0
    for count in counts:
        value = refs[at][...]
        for ref in refs[at + 1 : at + count]:
            value = value + ref[...]
        end = start + value.shape[0]
        out_ref[start:end, :] = value
        at += count
        start = end


def back_tokens(e_ref, w_hbm, out_ref, w_ref, sems):
    local = w_ref.shape[2]
    came = fetch([w_hbm.at[i] for i in range(3)], [w_ref.at[i] for i in range(3)], sems)
    for i in range(3):
        came[i].wait()
        added = dot_nt(e_ref[:, i * local : (i + 1) * local], w_ref[i])
        if i == 0:
            out_ref[...] = added
        else:
            out_ref[...] += added


def join(own_ref, far_ref, *refs):
    out_ref, start = refs[-1], 0
    for ref in refs[:-1]:
        span = slice(start, start + ref.shape[0])
        out_ref[span, :] = ref[...] + (own_ref[span, :] + far_ref[span, :])
        start += ref.shape[0]


def spread(local, *refs):
    qkv_ref, out_ref = refs[-2:]
    value = refs[0][...]
    for ref in refs[1:-2]:
        value = value + ref[...]
    for i in range(3):
        qkv_ref[i] = value[:, i * local : (i + 1) * local]
    out_ref[...] = value[:, 3 * local :]


def chained(kernel, inputs, outputs):
    def body(*refs):
        refs[1 + inputs + outputs][...] = jnp.zeros((8, LANES), F32)
        kernel(*refs[1 : 1 + inputs + outputs], *refs[2 + inputs + outputs :])

    return body


def on_device(
    tokens, lengths, pad_mask, w_qkv, b_qv, w_out, b_out, ln1_gain, ln1_bias,
    w_up, b_up, w_down, b_down, ln2_gain, ln2_bias, cotangent,
):
    rows, width = tokens.shape
    local = w_qkv.shape[2]
    heads = local // HEAD
    hidden = w_up.shape[1]
    ranks = lax.axis_size("dp")
    me = lax.axis_index("dp").astype(jnp.int32)
    place_arr = jnp.stack([me % 2, lax.axis_index("tp").astype(jnp.int32), me])
    size = width // ranks
    blocks = [rows // 2] * 2 if rows % 32 == 0 else [rows]
    starts = [sum(blocks[:i]) for i in range(len(blocks))]
    lse_rows = -(-heads // 8) * 8
    shape = jax.ShapeDtypeStruct
    smem = pl.BlockSpec(memory_space=pltpu.SMEM)
    loose = pl.BlockSpec(memory_space=pl.ANY)
    far_off = pl.BlockSpec(memory_space=pltpu.HBM)
    dma = pltpu.SemaphoreType.DMA
    mark = [None]
    pace = [10**10]

    def call(kernel, name, operands, in_specs, out_shape, out_specs, grid=(1,), scratch=(), limit=24, flops=None):
        before = mark[0] if mark[0] is not None else operands[0]
        operands = [
            pltpu.with_memory_space_constraint(operand, pltpu.HBM) if spec is far_off else operand
            for operand, spec in zip(operands, in_specs)
        ]
        *outs, mark[0] = pl.pallas_call(
            chained(kernel, len(operands), len(out_shape)),
            grid=grid,
            out_shape=tuple(out_shape) + (shape((8, LANES), F32),),
            in_specs=[loose] + list(in_specs),
            out_specs=tuple(out_specs) + (whole((8, LANES)),),
            scratch_shapes=list(scratch),
            compiler_params=params(limit),
            cost_estimate=cost(pace[0] if flops is None else flops),
            name=name,
        )(before, *operands)
        return outs

    def full(*arrays):
        return [whole(array.shape) for array in arrays]

    def swap_tp(array):
        pairs = [(i, i ^ 1) for i in range(lax.axis_size("tp"))]
        return lax.ppermute(array, "tp", pairs)

    def swap_dp(array, bits):
        return lax.ppermute(array, "dp", [(i, i ^ bits) for i in range(ranks)])

    stages = []
    while 1 << len(stages) < ranks:
        stages.append(1 << len(stages))
    order = [0]
    for bit in reversed(stages):
        order = order + [bit + rest for rest in order]
    order = order[ranks // 2 :] + order[: ranks // 2]
    fused = size % 16 == 0
    pad_row = pad_mask
    half = w_out.shape[0] // 2
    w_near = swap_tp(lax.dynamic_slice_in_dim(w_out, (me % 2) * half, half, 0).astype(F32))
    outs = [shape((rows, 3 * local), LOW), shape((rows, local), LOW), shape((lse_rows, rows), F32)]
    outs += [shape((block, local), F32) for block in blocks]
    qkv, context, lse, *wides = call(
        functools.partial(attend, blocks), "attend", [tokens, w_qkv, b_qv, lengths, pad_row],
        [far_off] * 2 + full(b_qv) + [smem] + full(pad_row), outs, [far_off] * 2 + full(*outs[2:]),
        scratch=[
            pltpu.VMEM((rows, width), LOW),
            pltpu.VMEM((3, width, local), LOW),
            pltpu.VMEM((rows, 3 * local), LOW),
            pltpu.VMEM((rows, local), LOW),
            dma((6,)),
        ],
        limit=56,
    )
    fars = [swap_tp(wide) for wide in wides]
    near = pl.BlockSpec(memory_space=pltpu.VMEM)
    params_of = [b_out, ln1_gain, ln1_bias, b_down, ln2_gain, ln2_bias]
    outs = [shape(w_near.shape, F32), shape((8, width), F32)]
    w_near, vectors = call(
        relay, "relay", [w_near, *params_of], full(w_near, *params_of), outs, full(*outs)
    )
    far_parts = 3 if half % 48 == 0 else 1
    piece = half // far_parts
    w_fars = [swap_dp(w_near[i * piece : (i + 1) * piece], 1) for i in range(far_parts)]
    outs = [shape((2 * local, width), LOW)]
    (w_whole,) = call(
        functools.partial(gather, far_parts), "gather", [place_arr, w_out, w_near, *w_fars],
        [smem, far_off] + full(w_near, *w_fars), outs, full(*outs), scratch=[dma((1,))], flops=10**8,
    )

    tile = min(hidden, 512)
    tiles = hidden // tile

    def columns(height, step):
        return pl.BlockSpec((height, step), lambda f: (0, f))

    saved = []
    for begin, block, far in zip(starts, blocks, fars):
        outs = [
            shape((block, width), F32), shape((block, LANES), F32), shape((block, width), LOW),
            shape((block, hidden), LOW), shape((block, hidden), F32), shape((block, width), F32),
            shape((block, width), F32),
        ]
        outs = call(
            functools.partial(feed, slice(begin, begin + block), tile, begin == 0), "feed",
            [place_arr, far, w_whole, tokens, context, vectors, b_up, w_up, w_down],
            [smem] + full(far, w_whole) + [far_off] * 3 + full(b_up) + [far_off if begin == 0 else near] * 2,
            outs, full(*outs),
            scratch=[
                pltpu.VMEM((block, width), LOW),
                pltpu.VMEM((8, width), F32),
                pltpu.VMEM((block, 2 * local), LOW),
                dma((3 + 2 * tiles,)),
            ]
            + ([pltpu.VMEM((width, hidden), LOW), pltpu.VMEM((hidden, width), LOW)] if begin == 0 else []),
        )
        saved.append(outs + [swap_tp(outs[5])])

    slope_of = [
        call(slopes, "slopes", [s[4]], full(s[4]), [shape(s[4].shape, F32)], full(s[4]))[0] for s in saved
    ]
    back = []
    for begin, block, slope, (_, _, _, _, _, own, base, far) in zip(starts, blocks, slope_of, saved):
        outs = [
            shape((block, width), LOW), shape((block, width), F32), shape((block, width), LOW),
            shape((block, hidden), LOW), shape((block, width), F32), shape((8, width), F32), shape((8, hidden), F32),
        ]
        outs = call(
            functools.partial(feed_back, slice(begin, begin + block), tile), "feed_back",
            [own, far, base, slope, vectors, cotangent, w_up, w_down],
            full(own, far, base, slope) + [far_off] * 2 + [near] * 2,
            outs, full(*outs),
            scratch=[pltpu.VMEM((8, width), F32), pltpu.VMEM((block, width), LOW), dma((2,))],
        )
        back.append(outs + [swap_tp(outs[4])])

    layer_out = jnp.concatenate([outs[0] for outs in back], 0)

    def gradient(lefts, rights, splits, kinds, step, rider=None):
        wide = step * len(kinds)
        sides = max(kinds) + 1
        riders = [] if rider is None else [rider]
        outs = [shape((width // 2 + 8 * len(riders), wide), F32)] * 2
        outs = call(
            functools.partial(
                outer, order if fused else None, size, splits, kinds, len(lefts) - len(splits), len(riders)
            ),
            "outer", [place_arr, *lefts, *rights, *riders],
            [smem] + full(*lefts) + [columns(split, step) for split in splits] + [columns(8, step) for _ in riders],
            outs, [columns(out.shape[0], step) for out in outs],
            grid=(len(kinds),),
            scratch=[pltpu.VMEM((width, rows), LOW), pltpu.VMEM((sides, width, rows), LOW)],
        )
        if not fused:
            every = jnp.concatenate([out[: width // 2] for out in outs], 0).reshape(ranks, size, wide)
            every = jnp.take(every, jnp.array(order, jnp.int32) ^ me, axis=0).reshape(width, wide)
            outs = [every[: width // 2], every[width // 2 :]]
            outs = [jnp.concatenate([out] + riders, 0) for out in outs]
        return outs

    class Chunk:
        def __init__(self, outs, came, wide, column, bits, rides=False):
            keep = outs[1]
            self.wide = wide
            self.parts = {p: [(keep, p, column), (came, p, column)] for p in range(ranks // 2)}
            self.alive = list(self.parts)
            self.bits = list(bits)
            self.extra = [(keep, width // 16), (came, width // 16)] if rides else []

        def add(self, places, flops, rides=False):
            wide = self.wide
            if not fused:
                sums = []
                for p in places:
                    found = [
                        array[row * size : (row + 1) * size, column * wide : (column + 1) * wide]
                        for array, row, column in self.parts[p]
                    ]
                    sums.append(functools.reduce(jnp.add, found))
                if rides:
                    sums.append(functools.reduce(jnp.add, [a[8 * row : 8 * row + 8] for a, row in self.extra]))
                return jnp.concatenate(sums, 0)
            operands, specs, counts = [], [], []
            for p in places:
                counts.append(len(self.parts[p]))
                for array, row, column in self.parts[p]:
                    operands.append(array)
                    specs.append(pl.BlockSpec((size, wide), functools.partial(lambda r, c, n: (r, c), row, column)))
            if rides:
                counts.append(len(self.extra))
                for array, row in self.extra:
                    operands.append(array)
                    specs.append(pl.BlockSpec((8, wide), functools.partial(lambda r, n: (r, 0), row)))
            outs = [shape((len(places) * size + (8 if rides else 0), wide), F32)]
            return call(
                functools.partial(fold_blocks, counts), "fold", operands, specs, outs, full(*outs), flops=flops
            )[0]

        def weight(self, bit):
            return ranks // (2 * bit)

        def send(self, places, flops, rides):
            bit = self.bits[0]
            rides = rides and self.extra and len(self.bits) > 1
            came = swap_dp(self.add(places, flops, rides), bit)
            self.arrived = getattr(self, "arrived", [])
            for i, p in enumerate(places):
                self.arrived.append((p ^ self.weight(bit), (came, i, 0)))
            if rides:
                self.extra = self.extra + [(came, len(places) * size // 8)]

        def close(self):
            for p, part in self.arrived:
                self.parts[p].append(part)
            self.arrived = []
            weight = self.weight(self.bits.pop(0))
            self.alive = [p for p in self.alive if not p & weight]

        def leaving(self):
            weight = self.weight(self.bits[0])
            return [p for p in self.alive if p & weight]

        def step(self, flops=None):
            self.send(self.leaving(), flops, True)
            self.close()

        def high(self, flops=None):
            if len(self.bits) == 1:
                self.step(flops)
            else:
                after = self.weight(self.bits[1])
                self.send([p for p in self.leaving() if p & after], flops, True)

        def low(self, flops=None):
            after = self.weight(self.bits[1])
            self.send([p for p in self.leaving() if not p & after], flops, False)
            self.close()

        def rest(self):
            while self.bits:
                self.step()

        def all_but_last(self):
            last = self.parts[0].pop()
            self.parts[0] = [(self.add([0], None), 0, 0), last]

        def last(self, flops=None):
            self.rest()
            return self.add([0], flops)

    def add_extra(extra):
        if not fused:
            return functools.reduce(jnp.add, [a[8 * row : 8 * row + 8] for a, row in extra])
        wide = extra[0][0].shape[1]
        specs = [pl.BlockSpec((8, wide), functools.partial(lambda index, n: (index, 0), row)) for _, row in extra]
        outs = [shape((8, wide), F32)]
        return call(fold, "fold", [array for array, _ in extra], specs, outs, full(*outs))[0]

    straight, turned = stages[1:], stages[2:] + stages[1:2]
    outs = gradient([o[2] for o in back], [s[3] for s in saved], blocks, [0] * tiles, tile)
    came = swap_dp(outs[0], stages[0])
    down = Chunk(outs, came, hidden // 3 * 2, 0, straight)
    early = Chunk(outs, came, hidden // 3, 2, turned)
    wide = 4 * local

    def first_norm(i):
        outs = [shape((blocks[i], width), F32), shape((blocks[i], width), LOW), shape((8, wide), F32)]
        operands = [back[i][1], back[i][4], back[i][7], saved[i][0], saved[i][1], back[i][5], back[i][6], vectors]
        operands += [norms[-1][2]] if norms else []
        flops = 2 * 10**10 if i == 0 else None
        norms.append(call(norm_one_back, "norm_one_back", operands, full(*operands), outs, full(*outs), flops=flops))

    norms = []
    first_norm(0)
    early.step()
    down.high()
    outs = gradient([s[2] for s in saved], [o[3] for o in back], blocks, [0] * tiles, tile)
    up = Chunk(outs, swap_dp(outs[0], stages[0]), hidden, 0, straight)
    down.low()
    pace[0] = 10**10
    early.step()
    down.step(2 * 10**10)
    up.high()
    first_norm(1)
    pace[0] = 10**8
    dr1s, lows = [n[0] for n in norms], [n[1] for n in norms]
    outs = [shape((rows, 4 * local), LOW), shape((8, wide), F32)]
    operands = lows + [w_out, qkv, context, lse, lengths, pad_row, norms[-1][2]]
    e, bias = call(
        functools.partial(attend_back, len(lows)), "attend_back", operands,
        full(*lows) + [far_off] * 3 + full(lse) + [smem] + full(pad_row, norms[-1][2]), outs, full(*outs),
        scratch=[pltpu.VMEM((local, width), LOW), pltpu.VMEM((rows, 3 * local), LOW), dma((3,))],
    )
    up.low()
    outs = gradient([tokens] + lows, [e], [rows], [0, 0, 0, 1], local, bias)
    mixed = Chunk(outs, swap_dp(outs[0], stages[0]), wide, 0, straight, rides=True)

    while early.bits:
        early.step()
    down.step(5 * 10**9)
    up.step(4 * 10**10)
    mixed.high()
    mixed.low()
    outs = [shape((rows, width), F32)]
    (partial,) = call(
        back_tokens, "back_tokens", [e, w_qkv], full(e) + [far_off], outs, full(*outs),
        scratch=[pltpu.VMEM((3, width, local), LOW), dma((3,))],
    )
    pace[0] = 10**9
    partial_far = swap_tp(partial)
    down = down.last(5 * 10**9)
    up.step()
    mixed.high()
    mixed.low()
    up = up.last()
    mixed.rest()
    bias = add_extra(mixed.extra)
    bias_far = swap_dp(bias, stages[-1])
    mixed.all_but_last()
    early = early.last()
    (d_tokens,) = call(
        join, "join", [partial, partial_far] + dr1s, full(partial, partial_far, *dr1s), outs, full(*outs)
    )
    (bias,) = call(fold, "fold", [bias, bias_far], full(bias, bias_far), [shape(bias.shape, F32)], full(bias))
    if fused:
        outs = [shape((3, size, local), F32), shape((size, local), F32)]
        operands = [array for array, _, _ in mixed.parts[0]]
        d_w_qkv, d_w_out = call(
            functools.partial(spread, local), "spread", operands,
            [pl.BlockSpec((size, wide), lambda n: (0, 0))] * len(operands), outs, full(*outs),
        )
    else:
        last = mixed.add([0], None)
        d_w_qkv = last[:, : 3 * local].reshape(size, 3, local).transpose(1, 0, 2)
        d_w_out = last[:, 3 * local :]
    return (
        layer_out,
        d_tokens,
        d_w_qkv,
        bias[7, : 2 * local].reshape(2, local),
        d_w_out.T,
        bias[5, :width],
        bias[3, :width],
        bias[4, :width],
        up,
        bias[6, :hidden],
        jnp.concatenate([down.T, early.T], 0),
        bias[2, :width],
        bias[0, :width],
        bias[1, :width],
    )


def solution(mesh):
    placed = (
        P("dp", None), P("dp", None), P("dp"), P(None, None, "tp"), P(None, "tp"), P("tp", None),
        P(), P(), P(), P(None, "tp"), P("tp"), P("tp", None), P(), P(), P(), P("dp", None),
    )
    return jax.shard_map(
        on_device,
        mesh=mesh,
        in_specs=placed,
        out_specs=(
            P("dp", None), P("dp", None), P(None, "dp", "tp"), P(None, "tp"), P("tp", "dp"), P(), P(), P(),
            P("dp", "tp"), P("tp"), P("tp", "dp"), P(), P(), P(),
        ),
        check_vma=False,
    )
```

```python
import functools

import jax
import jax.numpy as jnp
from jax import lax
from jax.experimental import pallas as pl
from jax.experimental.pallas import tpu as pltpu
from jax.sharding import PartitionSpec as P

HEAD = 64
NEG_FILL = -1e30
EPS_NORM = 1e-12
LANES = 128
F32 = jnp.float32
LOW = jnp.bfloat16
MIB = 1 << 20


def dot(a, b):
    return lax.dot_general(a, b, (((1,), (0,)), ((), ())), preferred_element_type=F32)


def dot_nt(a, b):
    return lax.dot_general(a, b, (((1,), (1,)), ((), ())), preferred_element_type=F32)


def whole(shape):
    return pl.BlockSpec(shape, lambda *_: (0,) * len(shape))


def params(limit):
    return pltpu.CompilerParams(vmem_limit_bytes=limit * MIB)


def cost(flops):
    return pl.CostEstimate(flops=flops, bytes_accessed=10**6, transcendentals=0)


def key_mask(lengths_ref, pad_ref, rows):
    seqs = lengths_ref.shape[1]
    key_at = lax.broadcasted_iota(jnp.int32, (rows, LANES), 0)
    query_at = lax.broadcasted_iota(jnp.int32, (8, rows), 1)
    key_seg = jnp.zeros((rows, LANES), jnp.int32)
    query_seg = jnp.zeros((8, rows), jnp.int32)
    end = jnp.int32(0)
    for i in range(seqs):
        end = end + lengths_ref[0, i]
        key_seg = key_seg + (key_at >= end).astype(jnp.int32)
        query_seg = query_seg + (query_at >= end).astype(jnp.int32)
    pad = jnp.broadcast_to(pad_ref[...].astype(F32).reshape(1, rows), (LANES, rows)).T
    pieces = []
    for j in range(rows // LANES):
        span = slice(j * LANES, (j + 1) * LANES)
        same = key_seg == query_seg[0:1, span]
        usable = (pad == 1.0) | (key_at == query_at[0:1, span])
        pieces.append(jnp.where(same & usable, 0.0, NEG_FILL))
    return jnp.concatenate(pieces, 1)


def halves():
    lane = lax.broadcasted_iota(jnp.int32, (1, LANES), 1)
    left = (lane < HEAD).astype(F32)
    return left.astype(LOW), (1.0 - left).astype(LOW)


def fetch(sources, targets, sems):
    copies = [pltpu.make_async_copy(source, target, sems.at[i]) for i, (source, target) in enumerate(zip(sources, targets))]
    for copy in copies:
        copy.start()
    return copies


def attend(
    blocks, x_hbm, w_hbm, b_ref, lengths_ref, pad_ref, qkv_hbm, ctx_hbm, lse_ref, *rest
):
    wide_refs, (x_ref, w_ref, qkv_ref, ctx_ref, sems) = rest[:-5], rest[-5:]
    rows = x_ref.shape[0]
    local = w_ref.shape[2]
    scale = float(HEAD) ** (-0.5)
    came = fetch([x_hbm] + [w_hbm.at[i] for i in range(3)], [x_ref] + [w_ref.at[i] for i in range(3)], sems)
    bias = key_mask(lengths_ref, pad_ref, rows)
    sides = halves()
    came[0].wait()
    x = x_ref[...]
    came[1].wait()
    qkv_ref[:, 0:local] = ((dot(x, w_ref[0]) + b_ref[0:1, :].astype(F32)) * scale).astype(LOW)
    came[2].wait()
    qkv_ref[:, local : 2 * local] = dot(x, w_ref[1]).astype(LOW)
    came[3].wait()
    qkv_ref[:, 2 * local :] = (dot(x, w_ref[2]) + b_ref[1:2, :].astype(F32)).astype(LOW)
    saved = pltpu.make_async_copy(qkv_ref, qkv_hbm, sems.at[4])
    saved.start()
    for pair in range(local // LANES):
        at = pair * LANES
        span = slice(at, at + LANES)
        query = qkv_ref[:, span]
        keys = qkv_ref[:, local + at : local + at + LANES]
        flipped = qkv_ref[:, 2 * local + at : 2 * local + at + LANES].T
        parts = []
        for side in range(2):
            scores = dot_nt(keys * sides[side], query) + bias
            top = jnp.max(scores, 0, keepdims=True)
            expo = jnp.exp(scores - top)
            total = jnp.sum(expo, 0, keepdims=True)
            probs = (expo * (1.0 / total)).astype(LOW)
            parts.append(dot(flipped[side * HEAD : (side + 1) * HEAD], probs))
            head = 2 * pair + side
            lse_ref[head : head + 1, :] = top + jnp.log(total)
        context = jnp.concatenate(parts, 0).T.astype(LOW)
        ctx_ref[:, span] = context
        start = 0
        for wide_ref, size in zip(wide_refs, blocks):
            wide_ref[:, span] = context[start : start + size].astype(F32)
            start += size
    kept = pltpu.make_async_copy(ctx_ref, ctx_hbm, sems.at[5])
    kept.start()
    saved.wait()
    kept.wait()


def relay(in_ref, *refs):
    vectors = refs[:6]
    out_ref, vec_ref = refs[-2:]
    out_ref[...] = in_ref[...]
    vec_ref[...] = jnp.zeros(vec_ref.shape, F32)
    for i, ref in enumerate(vectors):
        vec_ref[i : i + 1, :] = ref[...].astype(F32).reshape(1, -1)


def norm_rows(value):
    centered = value - jnp.mean(value, -1, keepdims=True)
    inverse = lax.rsqrt(jnp.mean(centered * centered, -1, keepdims=True) + EPS_NORM)
    return centered * inverse, inverse


def norm_back(grad, normed, inverse, gain):
    scaled = grad * gain
    return inverse * (
        scaled
        - jnp.mean(scaled, -1, keepdims=True)
        - normed * jnp.mean(scaled * normed, -1, keepdims=True)
    )


def row(ref):
    return ref[...].astype(F32)


def gather(far_parts, place_ref, w_own_hbm, w_near_ref, *refs):
    w_fars, (out_ref, sems) = refs[:far_parts], refs[far_parts:]
    local = w_own_hbm.shape[0]
    half = w_near_ref.shape[0]
    core, side = place_ref[0], place_ref[1]
    here = pl.multiple_of(side * local, LANES)
    there = pl.multiple_of((1 - side) * local, LANES)
    (came,) = fetch([w_own_hbm], [out_ref.at[pl.ds(here, local)]], sems)
    out_ref[pl.ds(pl.multiple_of(there + core * half, 16), half), :] = w_near_ref[...].astype(LOW)
    at = there + (1 - core) * half
    for ref in w_fars:
        size = ref.shape[0]
        out_ref[pl.ds(pl.multiple_of(at, 16), size), :] = ref[...].astype(LOW)
        at = at + size
    came.wait()


def feed(taken, tile, streamed, place_ref, far_ref, w_full, x_hbm, own_hbm, *refs):
    vec_hbm, b_up_ref, w_up, w_down = refs[:4]
    normed_ref, inverse_ref, low_ref, act_ref, pre_ref, part_ref, base_ref = refs[4:11]
    x_ref, vec_ref, ctx_full, sems = refs[11:15]
    local = own_hbm.shape[1]
    hidden = w_up.shape[1]
    side = place_ref[1]
    here = pl.multiple_of(side * local, LANES)
    there = pl.multiple_of((1 - side) * local, LANES)
    spans = [slice(at, at + tile) for at in range(0, hidden, tile)]
    sources = [own_hbm.at[taken], x_hbm.at[taken], vec_hbm]
    targets = [ctx_full.at[:, pl.ds(here, local)], x_ref, vec_ref]
    needed = len(sources)
    if streamed:
        w_up_vmem, w_down_vmem = refs[15:]
        for span in spans:
            sources += [w_up.at[:, span], w_down.at[span]]
            targets += [w_up_vmem.at[:, span], w_down_vmem.at[span]]
        w_up, w_down = w_up_vmem, w_down_vmem
    came = fetch(sources, targets, sems)
    ctx_full[:, pl.ds(there, local)] = far_ref[...].astype(LOW)
    for copy in came[:needed]:
        copy.wait()
    attn = dot(ctx_full[...], w_full[...])
    normed, inverse = norm_rows(x_ref[...].astype(F32) + attn + vec_ref[0:1, :])
    normed_ref[...] = normed
    inverse_ref[...] = jnp.broadcast_to(inverse, inverse_ref.shape)
    hidden_rows = normed * vec_ref[1:2, :] + vec_ref[2:3, :]
    base_ref[...] = hidden_rows + vec_ref[3:4, :]
    low = hidden_rows.astype(LOW)
    low_ref[...] = low
    b_up = b_up_ref[...].astype(F32).reshape(1, -1)
    for i, span in enumerate(spans):
        if streamed:
            came[needed + 2 * i].wait()
        pre = dot(low, w_up[:, span]) + b_up[:, span]
        share = 0.5 * (1.0 + lax.erf(pre * 0.7071067811865476))
        act = (pre * share).astype(LOW)
        act_ref[:, span] = act
        pre_ref[:, span] = pre
        if streamed:
            came[needed + 2 * i + 1].wait()
        added = dot(act, w_down[span, :])
        if i == 0:
            part_ref[...] = added
        else:
            part_ref[...] += added


def slopes(pre_ref, out_ref):
    pre = pre_ref[...]
    share = 0.5 * (1.0 + lax.erf(pre * 0.7071067811865476))
    out_ref[...] = share + pre * jnp.exp(-0.5 * pre * pre) * 0.3989422804014327


def feed_back(
    taken, tile, own_ref, far_ref, base_ref, slope_ref, vec_hbm, up_hbm, w_up, w_down,
    out_ref, grad_ref, low_ref, pre_ref, part_ref, sums_ref, b_up_ref,
    vec_ref, up_ref, sems,
):
    hidden = w_up.shape[1]
    spans = [slice(at, at + tile) for at in range(0, hidden, tile)]
    came = fetch([up_hbm.at[taken], vec_hbm], [up_ref, vec_ref], sems)
    normed, inverse = norm_rows(base_ref[...] + (own_ref[...] + far_ref[...]))
    came[1].wait()
    gain = vec_ref[4:5, :]
    out_ref[...] = (normed * gain + vec_ref[5:6, :]).astype(LOW)
    came[0].wait()
    upstream = up_ref[...].astype(F32)
    grad = norm_back(upstream, normed, inverse, gain)
    grad_ref[...] = grad
    low = grad.astype(LOW)
    low_ref[...] = low
    sums_ref[0:1, :] = jnp.sum(upstream * normed, 0, keepdims=True)
    sums_ref[1:2, :] = jnp.sum(upstream, 0, keepdims=True)
    sums_ref[2:3, :] = jnp.sum(grad, 0, keepdims=True)
    sums_ref[3:8, :] = jnp.zeros((5, sums_ref.shape[1]), F32)
    for i, span in enumerate(spans):
        pre = (dot_nt(low, w_down[span, :]) * slope_ref[:, span]).astype(LOW)
        pre_ref[:, span] = pre
        b_up_ref[:, span] = jnp.broadcast_to(jnp.sum(pre.astype(F32), 0, keepdims=True), (8, tile))
        added = dot_nt(pre, w_up[:, span])
        if i == 0:
            part_ref[...] = added
        else:
            part_ref[...] += added


def norm_one_back(own_dr2, own_ref, far_ref, normed_ref, inverse_ref, sums_ref, b_up_ref, vec_ref, *refs):
    before, (dr1_ref, low_ref, bias_ref) = refs[:-3], refs[-3:]
    width = dr1_ref.shape[1]
    grad = own_dr2[...] + (own_ref[...] + far_ref[...])
    norm = normed_ref[...]
    dr1 = norm_back(grad, norm, inverse_ref[:, 0:1], vec_ref[1:2, :])
    dr1_ref[...] = dr1
    low_ref[...] = dr1.astype(LOW)
    bias_ref[...] = before[0][...] if before else jnp.zeros(bias_ref.shape, F32)
    bias_ref[0:3, 0:width] += sums_ref[0:3]
    for i, value in enumerate((grad * norm, grad, dr1)):
        bias_ref[3 + i : 4 + i, 0:width] += jnp.sum(value, 0, keepdims=True)
    bias_ref[6:7, 0 : b_up_ref.shape[1]] += b_up_ref[0:1, :]


def attend_back(
    count, *refs,
):
    attend_back_body(refs[:count], *refs[count:])


def attend_back_body(
    low_refs, w_hbm, qkv_hbm, ctx_hbm, lse_ref, lengths_ref, pad_ref, so_far_ref, e_ref, bias_ref,
    w_ref, qkv_ref, sems,
):
    rows, local = ctx_hbm.shape
    came = fetch([w_hbm, qkv_hbm, ctx_hbm], [w_ref, qkv_ref, e_ref.at[:, 3 * local : 4 * local]], sems)
    scale = float(HEAD) ** (-0.5)
    bias_ref[...] = so_far_ref[...]
    mask = key_mask(lengths_ref, pad_ref, rows)
    sides = halves()
    came[0].wait()
    d_ctx = dot_nt(jnp.concatenate([ref[...] for ref in low_refs], 0), w_ref[...]).astype(LOW)
    came[1].wait()
    for pair in range(local // LANES):
        at = pair * LANES
        span = slice(at, at + LANES)
        query = qkv_ref[:, span]
        keys = qkv_ref[:, local + at : local + at + LANES]
        values = qkv_ref[:, 2 * local + at : 2 * local + at + LANES]
        grads = d_ctx[:, span]
        flipped = keys.T
        d_q = []
        d_k = jnp.zeros((rows, LANES), F32)
        d_v = jnp.zeros((rows, LANES), F32)
        for side in range(2):
            head = 2 * pair + side
            scores = dot_nt(keys * sides[side], query) + mask
            probs = jnp.exp(scores - lse_ref[head : head + 1, :])
            d_p = dot_nt(values * sides[side], grads)
            mixed = jnp.sum(probs * d_p, 0, keepdims=True)
            d_s = (probs * (d_p - mixed)).astype(LOW)
            d_k = d_k + dot(d_s, query * sides[side])
            d_v = d_v + dot(probs.astype(LOW), grads * sides[side])
            d_q.append(dot(flipped[side * HEAD : (side + 1) * HEAD], d_s))
        d_query = jnp.concatenate(d_q, 0).T.astype(LOW).astype(F32) * scale
        d_k = d_k.astype(LOW)
        d_v = d_v.astype(LOW)
        e_ref[:, at : at + LANES] = d_query.astype(LOW)
        e_ref[:, local + at : local + at + LANES] = d_k
        e_ref[:, 2 * local + at : 2 * local + at + LANES] = d_v
        bias_ref[7:8, at : at + LANES] = jnp.sum(d_query, 0, keepdims=True)
        bias_ref[7:8, local + at : local + at + LANES] = jnp.sum(d_v.astype(F32), 0, keepdims=True)
    came[2].wait()


def place_blocks(me, source, target, order, size):
    for i, block in enumerate(order):
        at = pl.multiple_of((me ^ block) * size, size)
        target[i * size : (i + 1) * size, :] = source[pl.ds(at, size), :]


def outer(order, size, splits, kinds, more, rides, place_ref, *refs):
    count = len(splits)
    sides = max(kinds) + 1
    lefts = [refs[:count]] + ([refs[count : count + more]] if more else [])
    rights = refs[count + more : 2 * count + more]
    rider = refs[2 * count + more] if rides else None
    *sent_refs, keep_ref, flipped, placed = refs[2 * count + more + rides :]
    step = pl.program_id(0)

    @pl.when(step == 0)
    def _():
        for index, group in enumerate(lefts):
            source = jnp.concatenate([ref[...] for ref in group], 0).T
            if order is None:
                placed[index] = source
            else:
                flipped[...] = source
                place_blocks(place_ref[2], flipped, placed.at[index], order, size)

    left = placed[0]
    if sides > 1:
        change = kinds.index(1)
        left = placed[jnp.where(step >= change, 1, 0)]
    right = jnp.concatenate([ref[...] for ref in rights], 0)
    half = left.shape[0] // 2
    part = half // len(sent_refs)
    for i, ref in enumerate(sent_refs):
        ref[0:part, :] = dot(left[i * part : (i + 1) * part], right)
    keep_ref[0:half, :] = dot(left[half:], right)
    if rides:
        sent_refs[-1][part:, :] = rider[...]
        keep_ref[half:, :] = rider[...]


def fold(*refs):
    value = refs[0][...]
    for ref in refs[1:-1]:
        value = value + ref[...]
    refs[-1][...] = value


def fold_blocks(counts, *refs):
    out_ref = refs[-1]
    at = start = 0
    for count in counts:
        value = refs[at][...]
        for ref in refs[at + 1 : at + count]:
            value = value + ref[...]
        end = start + value.shape[0]
        out_ref[start:end, :] = value
        at += count
        start = end


def back_tokens(e_ref, w_hbm, out_ref, w_ref, sems):
    local = w_ref.shape[2]
    came = fetch([w_hbm.at[i] for i in range(3)], [w_ref.at[i] for i in range(3)], sems)
    for i in range(3):
        came[i].wait()
        added = dot_nt(e_ref[:, i * local : (i + 1) * local], w_ref[i])
        if i == 0:
            out_ref[...] = added
        else:
            out_ref[...] += added


def join(own_ref, far_ref, *refs):
    out_ref, start = refs[-1], 0
    for ref in refs[:-1]:
        span = slice(start, start + ref.shape[0])
        out_ref[span, :] = ref[...] + (own_ref[span, :] + far_ref[span, :])
        start += ref.shape[0]


def spread(local, *refs):
    qkv_ref, out_ref = refs[-2:]
    value = refs[0][...]
    for ref in refs[1:-2]:
        value = value + ref[...]
    for i in range(3):
        qkv_ref[i] = value[:, i * local : (i + 1) * local]
    out_ref[...] = value[:, 3 * local :]


def pack(width, *refs):
    out_ref = refs[-1]
    value = refs[0][...]
    for ref in refs[1:-1]:
        value = value + ref[...]
    out_ref[:, 0:width] = value[:, 0:width]
    out_ref[:, width:] = jnp.zeros((8, LANES), F32)
    for i in range(width // LANES):
        at = width + i * LANES
        out_ref[i : i + 1, width:] = value[6:7, at : at + LANES]


def chained(kernel, inputs, outputs):
    def body(*refs):
        refs[1 + inputs + outputs][...] = jnp.zeros((8, LANES), F32)
        kernel(*refs[1 : 1 + inputs + outputs], *refs[2 + inputs + outputs :])

    return body


def on_device(
    tokens, lengths, pad_mask, w_qkv, b_qv, w_out, b_out, ln1_gain, ln1_bias,
    w_up, b_up, w_down, b_down, ln2_gain, ln2_bias, cotangent,
):
    rows, width = tokens.shape
    local = w_qkv.shape[2]
    heads = local // HEAD
    hidden = w_up.shape[1]
    ranks = lax.axis_size("dp")
    me = lax.axis_index("dp").astype(jnp.int32)
    place_arr = jnp.stack([me % 2, lax.axis_index("tp").astype(jnp.int32), me])
    size = width // ranks
    blocks = [rows // 2] * 2 if rows % 32 == 0 else [rows]
    starts = [sum(blocks[:i]) for i in range(len(blocks))]
    lse_rows = -(-heads // 8) * 8
    shape = jax.ShapeDtypeStruct
    smem = pl.BlockSpec(memory_space=pltpu.SMEM)
    loose = pl.BlockSpec(memory_space=pl.ANY)
    far_off = pl.BlockSpec(memory_space=pltpu.HBM)
    dma = pltpu.SemaphoreType.DMA
    mark = [None]
    pace = [10**10]

    def call(kernel, name, operands, in_specs, out_shape, out_specs, grid=(1,), scratch=(), limit=24, flops=None):
        before = mark[0] if mark[0] is not None else operands[0]
        operands = [
            pltpu.with_memory_space_constraint(operand, pltpu.HBM) if spec is far_off else operand
            for operand, spec in zip(operands, in_specs)
        ]
        *outs, mark[0] = pl.pallas_call(
            chained(kernel, len(operands), len(out_shape)),
            grid=grid,
            out_shape=tuple(out_shape) + (shape((8, LANES), F32),),
            in_specs=[loose] + list(in_specs),
            out_specs=tuple(out_specs) + (whole((8, LANES)),),
            scratch_shapes=list(scratch),
            compiler_params=params(limit),
            cost_estimate=cost(pace[0] if flops is None else flops),
            name=name,
        )(before, *operands)
        return outs

    def full(*arrays):
        return [whole(array.shape) for array in arrays]

    def swap_tp(array):
        pairs = [(i, i ^ 1) for i in range(lax.axis_size("tp"))]
        return lax.ppermute(array, "tp", pairs)

    def swap_dp(array, bits):
        return lax.ppermute(array, "dp", [(i, i ^ bits) for i in range(ranks)])

    stages = []
    while 1 << len(stages) < ranks:
        stages.append(1 << len(stages))
    order = [0]
    for bit in reversed(stages):
        order = order + [bit + rest for rest in order]
    order = order[ranks // 2 :] + order[: ranks // 2]
    fused = size % 16 == 0
    packed = fused and hidden == 2 * width and width <= 8 * LANES
    pad_row = pad_mask
    half = w_out.shape[0] // 2
    w_near = swap_tp(lax.dynamic_slice_in_dim(w_out, (me % 2) * half, half, 0).astype(F32))
    outs = [shape((rows, 3 * local), LOW), shape((rows, local), LOW), shape((lse_rows, rows), F32)]
    outs += [shape((block, local), F32) for block in blocks]
    qkv, context, lse, *wides = call(
        functools.partial(attend, blocks), "attend", [tokens, w_qkv, b_qv, lengths, pad_row],
        [far_off] * 2 + full(b_qv) + [smem] + full(pad_row), outs, [far_off] * 2 + full(*outs[2:]),
        scratch=[
            pltpu.VMEM((rows, width), LOW),
            pltpu.VMEM((3, width, local), LOW),
            pltpu.VMEM((rows, 3 * local), LOW),
            pltpu.VMEM((rows, local), LOW),
            dma((6,)),
        ],
        limit=56,
    )
    fars = [swap_tp(wide) for wide in wides]
    near = pl.BlockSpec(memory_space=pltpu.VMEM)
    params_of = [b_out, ln1_gain, ln1_bias, b_down, ln2_gain, ln2_bias]
    outs = [shape(w_near.shape, F32), shape((8, width), F32)]
    w_near, vectors = call(
        relay, "relay", [w_near, *params_of], full(w_near, *params_of), outs, full(*outs)
    )
    far_parts = 3 if half % 48 == 0 else 1
    piece = half // far_parts
    w_fars = [swap_dp(w_near[i * piece : (i + 1) * piece], 1) for i in range(far_parts)]
    outs = [shape((2 * local, width), LOW)]
    (w_whole,) = call(
        functools.partial(gather, far_parts), "gather", [place_arr, w_out, w_near, *w_fars],
        [smem, far_off] + full(w_near, *w_fars), outs, full(*outs), scratch=[dma((1,))], flops=10**8,
    )

    tile = min(hidden, 512)
    tiles = hidden // tile

    def columns(height, step):
        return pl.BlockSpec((height, step), lambda f: (0, f))

    saved = []
    for begin, block, far in zip(starts, blocks, fars):
        outs = [
            shape((block, width), F32), shape((block, LANES), F32), shape((block, width), LOW),
            shape((block, hidden), LOW), shape((block, hidden), F32), shape((block, width), F32),
            shape((block, width), F32),
        ]
        outs = call(
            functools.partial(feed, slice(begin, begin + block), tile, begin == 0), "feed",
            [place_arr, far, w_whole, tokens, context, vectors, b_up, w_up, w_down],
            [smem] + full(far, w_whole) + [far_off] * 3 + full(b_up) + [far_off if begin == 0 else near] * 2,
            outs, full(*outs),
            scratch=[
                pltpu.VMEM((block, width), LOW),
                pltpu.VMEM((8, width), F32),
                pltpu.VMEM((block, 2 * local), LOW),
                dma((3 + 2 * tiles,)),
            ]
            + ([pltpu.VMEM((width, hidden), LOW), pltpu.VMEM((hidden, width), LOW)] if begin == 0 else []),
        )
        saved.append(outs + [swap_tp(outs[5])])

    slope_of = [
        call(slopes, "slopes", [s[4]], full(s[4]), [shape(s[4].shape, F32)], full(s[4]))[0] for s in saved
    ]
    back = []
    for begin, block, slope, (_, _, _, _, _, own, base, far) in zip(starts, blocks, slope_of, saved):
        outs = [
            shape((block, width), LOW), shape((block, width), F32), shape((block, width), LOW),
            shape((block, hidden), LOW), shape((block, width), F32), shape((8, width), F32), shape((8, hidden), F32),
        ]
        outs = call(
            functools.partial(feed_back, slice(begin, begin + block), tile), "feed_back",
            [own, far, base, slope, vectors, cotangent, w_up, w_down],
            full(own, far, base, slope) + [far_off] * 2 + [near] * 2,
            outs, full(*outs),
            scratch=[pltpu.VMEM((8, width), F32), pltpu.VMEM((block, width), LOW), dma((2,))],
        )
        back.append(outs + [swap_tp(outs[4])])

    layer_out = jnp.concatenate([outs[0] for outs in back], 0)

    def gradient(lefts, rights, splits, kinds, step, rider=None):
        wide = step * len(kinds)
        sides = max(kinds) + 1
        riders = [] if rider is None else [rider]
        outs = [shape((width // 2 + 8 * len(riders), wide), F32)] * 2
        outs = call(
            functools.partial(
                outer, order if fused else None, size, splits, kinds, len(lefts) - len(splits), len(riders)
            ),
            "outer", [place_arr, *lefts, *rights, *riders],
            [smem] + full(*lefts) + [columns(split, step) for split in splits] + [columns(8, step) for _ in riders],
            outs, [columns(out.shape[0], step) for out in outs],
            grid=(len(kinds),),
            scratch=[pltpu.VMEM((width, rows), LOW), pltpu.VMEM((sides, width, rows), LOW)],
        )
        if not fused:
            every = jnp.concatenate([out[: width // 2] for out in outs], 0).reshape(ranks, size, wide)
            every = jnp.take(every, jnp.array(order, jnp.int32) ^ me, axis=0).reshape(width, wide)
            outs = [every[: width // 2], every[width // 2 :]]
            outs = [jnp.concatenate([out] + riders, 0) for out in outs]
        return outs

    class Chunk:
        def __init__(self, outs, came, wide, column, bits, rides=False):
            keep = outs[1]
            self.wide = wide
            self.parts = {p: [(keep, p, column), (came, p, column)] for p in range(ranks // 2)}
            self.alive = list(self.parts)
            self.bits = list(bits)
            self.extra = [(keep, width // 16), (came, width // 16)] if rides else []

        def add(self, places, flops, rides=False):
            wide = self.wide
            if not fused:
                sums = []
                for p in places:
                    found = [
                        array[row * size : (row + 1) * size, column * wide : (column + 1) * wide]
                        for array, row, column in self.parts[p]
                    ]
                    sums.append(functools.reduce(jnp.add, found))
                if rides:
                    sums.append(functools.reduce(jnp.add, [a[8 * row : 8 * row + 8] for a, row in self.extra]))
                return jnp.concatenate(sums, 0)
            operands, specs, counts = [], [], []
            for p in places:
                counts.append(len(self.parts[p]))
                for array, row, column in self.parts[p]:
                    operands.append(array)
                    specs.append(pl.BlockSpec((size, wide), functools.partial(lambda r, c, n: (r, c), row, column)))
            if rides:
                counts.append(len(self.extra))
                for array, row in self.extra:
                    operands.append(array)
                    specs.append(pl.BlockSpec((8, wide), functools.partial(lambda r, n: (r, 0), row)))
            outs = [shape((len(places) * size + (8 if rides else 0), wide), F32)]
            return call(
                functools.partial(fold_blocks, counts), "fold", operands, specs, outs, full(*outs), flops=flops
            )[0]

        def weight(self, bit):
            return ranks // (2 * bit)

        def send(self, places, flops, rides):
            bit = self.bits[0]
            rides = rides and self.extra and len(self.bits) > 1
            came = swap_dp(self.add(places, flops, rides), bit)
            self.arrived = getattr(self, "arrived", [])
            for i, p in enumerate(places):
                self.arrived.append((p ^ self.weight(bit), (came, i, 0)))
            if rides:
                self.extra = self.extra + [(came, len(places) * size // 8)]

        def close(self):
            for p, part in self.arrived:
                self.parts[p].append(part)
            self.arrived = []
            weight = self.weight(self.bits.pop(0))
            self.alive = [p for p in self.alive if not p & weight]

        def leaving(self):
            weight = self.weight(self.bits[0])
            return [p for p in self.alive if p & weight]

        def step(self, flops=None):
            self.send(self.leaving(), flops, True)
            self.close()

        def high(self, flops=None):
            if len(self.bits) == 1:
                self.step(flops)
            else:
                after = self.weight(self.bits[1])
                self.send([p for p in self.leaving() if p & after], flops, True)

        def low(self, flops=None):
            after = self.weight(self.bits[1])
            self.send([p for p in self.leaving() if not p & after], flops, False)
            self.close()

        def rest(self):
            while self.bits:
                self.step()

        def all_but_last(self):
            last = self.parts[0].pop()
            self.parts[0] = [(self.add([0], None), 0, 0), last]

        def last(self, flops=None):
            self.rest()
            return self.add([0], flops)

    def add_extra(extra):
        if not fused:
            return functools.reduce(jnp.add, [a[8 * row : 8 * row + 8] for a, row in extra])
        wide = extra[0][0].shape[1]
        specs = [pl.BlockSpec((8, wide), functools.partial(lambda index, n: (index, 0), row)) for _, row in extra]
        outs = [shape((8, width + LANES if packed else wide), F32)]
        kernel = functools.partial(pack, width) if packed else fold
        return call(kernel, "fold", [array for array, _ in extra], specs, outs, full(*outs))[0]

    straight, turned = stages[1:], stages[2:] + stages[1:2]
    outs = gradient([o[2] for o in back], [s[3] for s in saved], blocks, [0] * tiles, tile)
    came = swap_dp(outs[0], stages[0])
    down = Chunk(outs, came, hidden // 3 * 2, 0, straight)
    early = Chunk(outs, came, hidden // 3, 2, turned)
    wide = 4 * local

    def first_norm(i):
        outs = [shape((blocks[i], width), F32), shape((blocks[i], width), LOW), shape((8, wide), F32)]
        operands = [back[i][1], back[i][4], back[i][7], saved[i][0], saved[i][1], back[i][5], back[i][6], vectors]
        operands += [norms[-1][2]] if norms else []
        flops = 2 * 10**10 if i == 0 else None
        norms.append(call(norm_one_back, "norm_one_back", operands, full(*operands), outs, full(*outs), flops=flops))

    norms = []
    first_norm(0)
    early.step()
    down.high()
    outs = gradient([s[2] for s in saved], [o[3] for o in back], blocks, [0] * tiles, tile)
    up = Chunk(outs, swap_dp(outs[0], stages[0]), hidden, 0, straight)
    down.low()
    pace[0] = 10**10
    early.step()
    down.step(2 * 10**10)
    up.high()
    first_norm(1)
    pace[0] = 10**8
    dr1s, lows = [n[0] for n in norms], [n[1] for n in norms]
    outs = [shape((rows, 4 * local), LOW), shape((8, wide), F32)]
    operands = lows + [w_out, qkv, context, lse, lengths, pad_row, norms[-1][2]]
    e, bias = call(
        functools.partial(attend_back, len(lows)), "attend_back", operands,
        full(*lows) + [far_off] * 3 + full(lse) + [smem] + full(pad_row, norms[-1][2]), outs, full(*outs),
        scratch=[pltpu.VMEM((local, width), LOW), pltpu.VMEM((rows, 3 * local), LOW), dma((3,))],
    )
    up.low()
    outs = gradient([tokens] + lows, [e], [rows], [0, 0, 0, 1], local, bias)
    mixed = Chunk(outs, swap_dp(outs[0], stages[0]), wide, 0, straight, rides=True)

    while early.bits:
        early.step()
    down.step(5 * 10**9)
    up.step(4 * 10**10)
    mixed.high()
    mixed.low()
    outs = [shape((rows, width), F32)]
    (partial,) = call(
        back_tokens, "back_tokens", [e, w_qkv], full(e) + [far_off], outs, full(*outs),
        scratch=[pltpu.VMEM((3, width, local), LOW), dma((3,))],
    )
    pace[0] = 10**9
    partial_far = swap_tp(partial)
    down = down.last(5 * 10**9)
    up.step()
    mixed.high()
    mixed.low()
    up = up.last()
    mixed.rest()
    bias = add_extra(mixed.extra)
    bias_far = swap_dp(bias, stages[-1])
    mixed.all_but_last()
    early = early.last()
    (d_tokens,) = call(
        join, "join", [partial, partial_far] + dr1s, full(partial, partial_far, *dr1s), outs, full(*outs)
    )
    (bias,) = call(fold, "fold", [bias, bias_far], full(bias, bias_far), [shape(bias.shape, F32)], full(bias))
    if fused:
        outs = [shape((3, size, local), F32), shape((size, local), F32)]
        operands = [array for array, _, _ in mixed.parts[0]]
        d_w_qkv, d_w_out = call(
            functools.partial(spread, local), "spread", operands,
            [pl.BlockSpec((size, wide), lambda n: (0, 0))] * len(operands), outs, full(*outs),
        )
    else:
        last = mixed.add([0], None)
        d_w_qkv = last[:, : 3 * local].reshape(size, 3, local).transpose(1, 0, 2)
        d_w_out = last[:, 3 * local :]
    d_b_up = bias[6, :hidden]
    if packed:
        d_b_up = jnp.concatenate([bias[6, :width], bias[: width // LANES, width:].reshape(hidden - width)])
    return (
        layer_out,
        d_tokens,
        d_w_qkv,
        bias[7, : 2 * local].reshape(2, local),
        d_w_out.T,
        bias[5, :width],
        bias[3, :width],
        bias[4, :width],
        up,
        d_b_up,
        jnp.concatenate([down.T, early.T], 0),
        bias[2, :width],
        bias[0, :width],
        bias[1, :width],
    )


def solution(mesh):
    placed = (
        P("dp", None), P("dp", None), P("dp"), P(None, None, "tp"), P(None, "tp"), P("tp", None),
        P(), P(), P(), P(None, "tp"), P("tp"), P("tp", None), P(), P(), P(), P("dp", None),
    )
    return jax.shard_map(
        on_device,
        mesh=mesh,
        in_specs=placed,
        out_specs=(
            P("dp", None), P("dp", None), P(None, "dp", "tp"), P(None, "tp"), P("tp", "dp"), P(), P(), P(),
            P("dp", "tp"), P("tp"), P("tp", "dp"), P(), P(), P(),
        ),
        check_vma=False,
    )
```
